256 devices in a mesh: tile: 32 (over y, z), head: 8 (over x, core).
Axes of the slice: x: 4, y: 4, z: 8, core: 2. Of those that a mesh axis runs over, the one named last changes fastest.
Arguments:
- query_slab: bfloat16 [32, 8, 32, 5120], P('tile', None, 'head'), may hold values from -30 to 30
- key_slab: bfloat16 [32, 8, 32, 5120], P('tile', None, 'head'), may hold values from -5 to 5
- value_slab: bfloat16 [32, 8, 32, 5120], P('tile', None, 'head'), may hold values from -5 to 5
- upstream: bfloat16 [8192, 5120], P('tile', 'head'), may hold values from -5 to 5
Outputs:
- attended: bfloat16 [8192, 5120], P('tile', 'head')
- query_grad: bfloat16 [8192, 5120], P('tile', 'head')
- key_grad: bfloat16 [8192, 5120], P('tile', 'head')
- value_grad: bfloat16 [8192, 5120], P('tile', 'head')
The draws below stay inside these ranges and needn't reach their ends.
All inputs are finite; a program needn't handle non-finite values.
Results may differ from the reference program's by a relative error of at most 0.012.
Values may be sent and summed in bfloat16 or wider, within the bound.
No kernel may reach another device: no remote copies, remote signals or barrier semaphores. Data moves between devices by JAX's collectives and lax.ppermute only.
A program may use at most 128 MiB of HBM per device.

```python
import jax
import jax.numpy as jnp
from jax import lax

HEADS = 40
HEAD_DIM = 128
FRAMES = 8
FRAME_W = 32
TILE_ROWS = 1
FRAME_H = 32
TOKENS = 8192
N_TILE = 32


def draw_query_slab(key, part):
    shape = (FRAMES * 4, FRAME_H // 4, FRAME_W, HEADS * HEAD_DIM)
    key = jax.random.fold_in(key, 1)
    return jnp.clip(jax.random.normal(key, shape), -5.0, 5.0).astype(jnp.bfloat16)


def draw_key_slab(key, part):
    shape = (FRAMES * 4, FRAME_H // 4, FRAME_W, HEADS * HEAD_DIM)
    key = jax.random.fold_in(key, 2)
    return jnp.clip(jax.random.normal(key, shape), -5.0, 5.0).astype(jnp.bfloat16)


def level_of(key, shape, shards, smallest, top_value):
    gain = 1.0
    for axis_at, parts in shards:
        steps = jax.random.uniform(jax.random.fold_in(jax.random.fold_in(key, 6), axis_at), (parts,), jnp.float32, smallest / len(shards), top_value / len(shards))
        gain = gain * jnp.repeat(jnp.exp(steps), shape[axis_at] // parts).reshape((-1,) + (1,) * (len(shape) - 1 - axis_at))
    return gain


def gaussian(key, shape, deviation, bound, split=(), held_as=jnp.bfloat16):
    factor_of = level_of(key, shape, split, -0.22, 0.18) if split else 1.0
    entries = jax.random.normal(key, shape, jnp.float32) * deviation * factor_of
    return jnp.minimum(jnp.maximum(entries, -bound), bound).astype(held_as)


def setup_inputs(seed: int = 0) -> dict:
    seeds = jax.random.split(jax.random.key(seed), 5)
    query_slab = draw_query_slab(jax.random.fold_in(seeds[4], 71), 0)
    key_slab = draw_key_slab(jax.random.fold_in(seeds[4], 71), 0)
    value_slab = gaussian(seeds[2], (4 * FRAMES, FRAME_H // 4, FRAME_W, HEADS * HEAD_DIM), 1.0, 5.0, ((0, 32), (2, 8)))
    upstream = gaussian(seeds[3], (TOKENS, HEADS * HEAD_DIM), 1.0, 5.0, ((0, 32), (1, 8)))
    return {"query_slab": query_slab, "key_slab": key_slab, "value_slab": value_slab, "upstream": upstream}


masked_score = -1.0e30


def to_tiles(grid, tile_rows, tile_cols):
    features = grid.shape[-1]
    shaped = grid.reshape(FRAMES, tile_rows, 4, tile_cols, 4, features)
    return shaped.transpose(1, 3, 0, 2, 4, 5).reshape(tile_rows, tile_cols, FRAMES * 16, features)


def from_tiles(tiles):
    tile_rows = tiles.shape[0]
    tile_cols = tiles.shape[1]
    features = tiles.shape[-1]
    shaped = tiles.reshape(tile_rows, tile_cols, FRAMES, 4, 4, features)
    return shaped.transpose(2, 0, 3, 1, 4, 5).reshape(FRAMES * tile_rows * tile_cols * 16, features)


def window_keys(nearby, tile_rows, tile_cols):
    features = nearby.shape[-1]
    shaped = nearby.reshape(2, FRAMES, tile_rows + 2, 4, tile_cols + 2, 4, features)
    pieces = [shaped[:, :, row_step:row_step + tile_rows, :, col_step:col_step + tile_cols] for row_step in range(3) for col_step in range(3)]
    stacked = jnp.stack(pieces, axis=1)
    ordered = stacked.transpose(0, 3, 5, 1, 2, 4, 6, 7)
    return ordered.reshape(2, tile_rows, tile_cols, 144 * FRAMES, features)


def fold_keys(window, tile_rows, tile_cols):
    features = window.shape[-1]
    portions = window.reshape(tile_rows, tile_cols, 3, 3, FRAMES, 4, 4, features)
    accumulated = jnp.zeros((FRAMES, tile_rows + 2, 4, tile_cols + 2, 4, features), jnp.float32)
    for row_step in range(3):
        for col_step in range(3):
            portion = portions[:, :, row_step, col_step].transpose(2, 0, 3, 1, 4, 5)
            accumulated = accumulated.at[:, row_step:row_step + tile_rows, :, col_step:col_step + tile_cols].add(portion)
    return accumulated.reshape(FRAMES, 4 * (tile_rows + 2), 4 * (tile_cols + 2), features)


def key_mask(tile_rows, tile_cols, row_first, col_first, rows_all, cols_all):
    row_index = jnp.arange(tile_rows, dtype=jnp.int32)[:, None, None, None]
    col_index = jnp.arange(tile_cols, dtype=jnp.int32)[None, :, None, None]
    row_steps = jnp.arange(3, dtype=jnp.int32)[None, None, :, None]
    col_steps = jnp.arange(3, dtype=jnp.int32)[None, None, None, :]
    row_place = row_first + row_index + row_steps - 1
    col_place = col_first + col_index + col_steps - 1
    usable = (row_place >= 0) & (row_place < rows_all) & (col_place >= 0) & (col_place < cols_all)
    spread = jnp.broadcast_to(usable[..., None], (tile_rows, tile_cols, 3, 3, FRAMES * 16))
    return spread.reshape(tile_rows, tile_cols, 144 * FRAMES)


def attend(query_blocks, key_window, value_window, grad_blocks, usable):
    tile_rows, pair_count, query_count, features = query_blocks.shape
    head_count = features // HEAD_DIM
    key_count = key_window.shape[2]
    best = lax.Precision.HIGHEST
    query_heads = query_blocks.astype(jnp.float32).reshape(tile_rows, pair_count, query_count, head_count, HEAD_DIM)
    grad_heads = grad_blocks.astype(jnp.float32).reshape(tile_rows, pair_count, query_count, head_count, HEAD_DIM)
    key_heads = key_window.astype(jnp.float32).reshape(tile_rows, pair_count, key_count, head_count, HEAD_DIM)
    value_heads = value_window.astype(jnp.float32).reshape(tile_rows, pair_count, key_count, head_count, HEAD_DIM)
    scaling = HEAD_DIM ** -0.5
    scores = jnp.einsum("rcqhd,rckhd->rchqk", query_heads, key_heads, precision=best) * scaling
    scores = jnp.where(usable[:, :, None, None, :], scores, masked_score)
    highest = jnp.max(scores, axis=-1, keepdims=True)
    raised = jnp.exp(scores - highest)
    weights = raised / jnp.sum(raised, axis=-1, keepdims=True)
    weights_low = lax.optimization_barrier(weights.astype(jnp.bfloat16)).astype(jnp.float32)
    mixed = jnp.einsum("rchqk,rckhd->rcqhd", weights_low, value_heads, precision=best)
    offsets = jnp.sum(grad_heads * mixed, axis=-1).transpose(0, 1, 3, 2)
    weight_grad = jnp.einsum("rcqhd,rckhd->rchqk", grad_heads, value_heads, precision=best)
    score_grad = weights * (weight_grad - offsets[..., None])
    score_low = lax.optimization_barrier(score_grad.astype(jnp.bfloat16)).astype(jnp.float32)
    query_grad = jnp.einsum("rchqk,rckhd->rcqhd", score_low, key_heads, precision=best) * scaling
    key_terms = jnp.einsum("rchqk,rcqhd->rckhd", score_low, query_heads, precision=best) * scaling
    value_terms = jnp.einsum("rchqk,rcqhd->rckhd", weights_low, grad_heads, precision=best)
    return (mixed.reshape(tile_rows, pair_count, query_count, features),
            query_grad.reshape(tile_rows, pair_count, query_count, features),
            key_terms.reshape(tile_rows, pair_count, key_count, features),
            value_terms.reshape(tile_rows, pair_count, key_count, features))


def reference(query_slab, key_slab, value_slab, upstream):
    features = HEADS * HEAD_DIM
    tile_cols = FRAME_W // 16
    band_width = 4 * tile_cols
    line_count = 4 * TILE_ROWS
    rows_all = FRAME_H // 4

    def to_grid(slab):
        shaped = slab.reshape(FRAMES, 4, rows_all, FRAME_W, features).transpose(0, 2, 1, 3, 4)
        return shaped.reshape(FRAMES, FRAME_H, FRAME_W, features)

    query_grid = to_grid(query_slab)
    pair_grid = jnp.stack((to_grid(key_slab), to_grid(value_slab)))
    padded = jnp.pad(pair_grid, ((0, 0), (0, 0), (4, 4), (4, 4), (0, 0)))
    grad_owned = upstream.reshape(N_TILE, FRAMES, line_count, band_width, features)

    def one_owner(owner_index):
        row_group = owner_index // 4
        col_group = owner_index % 4
        zero = jnp.zeros((), jnp.int32)
        row_first = row_group * line_count
        col_first = col_group * band_width
        owned_query = lax.dynamic_slice(query_grid, (zero, row_first, col_first, zero), (FRAMES, line_count, band_width, features))
        nearby = lax.dynamic_slice(padded, (zero, zero, row_first, col_first, zero), (2, FRAMES, line_count + 8, band_width + 8, features))
        windows = window_keys(nearby, TILE_ROWS, tile_cols)
        usable = key_mask(TILE_ROWS, tile_cols, row_group * TILE_ROWS, col_group * tile_cols, rows_all, 4 * tile_cols)
        grad_rows = lax.dynamic_index_in_dim(grad_owned, owner_index, 0, keepdims=False)
        mixed, query_grad, key_terms, value_terms = attend(to_tiles(owned_query, TILE_ROWS, tile_cols), windows[0], windows[1], to_tiles(grad_rows, TILE_ROWS, tile_cols), usable)
        extended = jnp.stack((fold_keys(key_terms, TILE_ROWS, tile_cols), fold_keys(value_terms, TILE_ROWS, tile_cols)))
        middle = extended[:, :, 4:4 + line_count]
        return (from_tiles(mixed).astype(jnp.bfloat16), from_tiles(query_grad).astype(jnp.bfloat16), middle,
                extended[:, :, 0:4].astype(jnp.bfloat16), extended[:, :, line_count + 4:].astype(jnp.bfloat16))

    attended, query_grad, middle, top_bands, bottom_bands = lax.map(one_owner, jnp.arange(N_TILE, dtype=jnp.int32))
    empty_rows = jnp.zeros_like(top_bands[:4])
    from_above = jnp.concatenate((empty_rows, bottom_bands[:-4]), axis=0).astype(jnp.float32)
    from_below = jnp.concatenate((top_bands[4:], empty_rows), axis=0).astype(jnp.float32)
    incoming = jnp.pad(from_above, ((0, 0), (0, 0), (0, 0), (0, line_count - 4), (0, 0), (0, 0)))
    incoming = incoming + jnp.pad(from_below, ((0, 0), (0, 0), (0, 0), (line_count - 4, 0), (0, 0), (0, 0)))
    rowed = middle + incoming
    left_bands = rowed[:, :, :, :, 0:4].astype(jnp.bfloat16)
    right_bands = rowed[:, :, :, :, band_width + 4:].astype(jnp.bfloat16)
    col_groups = (jnp.arange(N_TILE, dtype=jnp.int32) % 4)[:, None, None, None, None, None]
    empty_one = jnp.zeros_like(left_bands[:1])
    from_left = jnp.where(col_groups > 0, jnp.concatenate((empty_one, right_bands[:-1]), axis=0), jnp.zeros_like(right_bands)).astype(jnp.float32)
    from_right = jnp.where(col_groups < 3, jnp.concatenate((left_bands[1:], empty_one), axis=0), jnp.zeros_like(left_bands)).astype(jnp.float32)
    summed = rowed[:, :, :, :, 4:band_width + 4]
    summed = summed + jnp.pad(from_left, ((0, 0), (0, 0), (0, 0), (0, 0), (0, band_width - 4), (0, 0)))
    summed = summed + jnp.pad(from_right, ((0, 0), (0, 0), (0, 0), (0, 0), (band_width - 4, 0), (0, 0)))
    summed = summed.astype(jnp.bfloat16)
    key_grad = summed[:, 0].reshape(TOKENS, features)
    value_grad = summed[:, 1].reshape(TOKENS, features)
    return (attended.reshape(TOKENS, features), query_grad.reshape(TOKENS, features), key_grad, value_grad)
```

```python
import functools
import math

import jax
import jax.numpy as jnp
import numpy as np
from jax import lax
from jax.experimental import pallas as pl
from jax.experimental.pallas import tpu as pltpu
from jax.sharding import PartitionSpec as P

HEAD_DIM = 128
HEADS_HERE = 5
STRIPS = 4
SLOTS = 8
TILE = 128
LOW = jnp.bfloat16
WIDE = jnp.float32
NEVER = -1e30


def route(step):
    pairs = []
    for strip in range(STRIPS):
        for slot in range(SLOTS):
            goal = step(strip, slot)
            if goal is not None:
                pairs.append((strip * SLOTS + slot, goal[0] * SLOTS + goal[1]))
    return pairs


def shifted(rows, columns):
    def step(strip, slot):
        there = (strip + rows, slot + columns)
        return there if 0 <= there[0] < STRIPS and 0 <= there[1] < SLOTS else None

    return route(step)


def owner_of(which, turn):
    def step(strip, slot):
        odd = slot % 2
        if which == 2:
            unit = 5 * slot + (0 if odd else 4)
        else:
            unit = 5 * slot + odd + 2 * which
        return (strip, ((turn + odd) % 2) * 4 + (unit % 8) // 2)

    return route(step)


def flipped(pairs):
    return [(target, source) for source, target in pairs]


HALO_STEPS = ((1, 0), (-1, 0), (0, 1), (0, -1), (1, 1), (1, -1), (-1, 1), (-1, -1))
OWNER_STEPS = tuple((which, turn) for which in range(3) for turn in range(2))


def whole(count):
    return [pl.BlockSpec(memory_space=pltpu.VMEM)] * count


def owner_table():
    slot = lax.axis_index("tile") % SLOTS
    row, pair = slot // 4, slot % 4
    heads = []
    for which, turn in OWNER_STEPS:
        odd = (row + turn) % 2
        if which == 2:
            unit = 10 * ((pair + 2) % 4) + 4
        else:
            even_unit = 10 * ((pair - which + 4) % 4) + 2 * which
            odd_unit = 10 * ((pair - 3 - which + 8) % 4) + 6 + 2 * which
            unit = jnp.where(odd == 1, odd_unit, even_unit)
        heads.append(unit // 8)
    return jnp.stack(heads + [row]).astype(jnp.int32)


def spread_kernel(table, upstream, *outs):
    line = lax.broadcasted_iota(jnp.int32, (2 * TILE, 2 * TILE), 0)
    col = lax.broadcasted_iota(jnp.int32, (2 * TILE, 2 * TILE), 1)
    source = ((line & 127) >> 2) * 8 + (line >> 7) * 4 + (line & 3)
    order = (col == source).astype(LOW)
    for at, (which, turn) in enumerate(OWNER_STEPS):
        head = pl.multiple_of(table[at] * HEAD_DIM, HEAD_DIM)
        tiles = jnp.dot(order, upstream[:, pl.ds(head, HEAD_DIM)], preferred_element_type=WIDE)
        tiles = tiles.astype(LOW)
        if which == 2:
            second = ((table[6] + turn) % 2) == 1
            outs[at][...] = jnp.where(second, tiles[TILE:], tiles[:TILE])
        else:
            outs[at][...] = tiles.reshape(2, TILE, HEAD_DIM)


def spread(table, upstream):
    shapes = [
        jax.ShapeDtypeStruct((TILE, HEAD_DIM) if which == 2 else (2, TILE, HEAD_DIM), LOW)
        for which, _ in OWNER_STEPS
    ]
    return pl.pallas_call(
        spread_kernel,
        out_shape=shapes,
        in_specs=[pl.BlockSpec(memory_space=pltpu.SMEM)] + whole(1),
        out_specs=whole(6),
        compiler_params=pltpu.CompilerParams(vmem_limit_bytes=16 << 20),
        name="spread",
    )(table, upstream)


def gather_kernel(table, *refs):
    first, second, outs = refs[:6], refs[6:12], refs[12:16]
    single = refs[16]
    line = lax.broadcasted_iota(jnp.int32, (2 * TILE, 2 * TILE), 0)
    col = lax.broadcasted_iota(jnp.int32, (2 * TILE, 2 * TILE), 1)
    source = ((line >> 2) & 1) * TILE + (line >> 3) * 4 + (line & 3)
    order = (col == source).astype(LOW)
    for group, received in enumerate((first, second)):
        for kind in range(2):
            out = outs[2 * group + kind]
            for at in range(4):
                head = pl.multiple_of(table[at] * HEAD_DIM, HEAD_DIM)
                tiles = received[at][kind].reshape(2 * TILE, HEAD_DIM)
                out[:, pl.ds(head, HEAD_DIM)] = jnp.dot(
                    order, tiles, preferred_element_type=WIDE
                ).astype(LOW)
            flip = table[6] == 1
            one, two = received[4][kind], received[5][kind]
            single[:TILE] = jnp.where(flip, two, one)
            single[TILE:] = jnp.where(flip, one, two)
            head = pl.multiple_of(table[4] * HEAD_DIM, HEAD_DIM)
            out[:, pl.ds(head, HEAD_DIM)] = jnp.dot(
                order, single[...], preferred_element_type=WIDE
            ).astype(LOW)


def gather(table, first, second):
    return pl.pallas_call(
        gather_kernel,
        out_shape=[jax.ShapeDtypeStruct((2 * TILE, HEADS_HERE * HEAD_DIM), LOW)] * 4,
        in_specs=[pl.BlockSpec(memory_space=pltpu.SMEM)] + whole(12),
        out_specs=whole(4),
        scratch_shapes=[pltpu.VMEM((2 * TILE, HEAD_DIM), LOW)],
        compiler_params=pltpu.CompilerParams(vmem_limit_bytes=16 << 20),
        name="gather",
    )(table, *first, *second)


def unit_table():
    place = lax.axis_index("tile")
    strip, slot = place // SLOTS, place % SLOTS
    cols = [(5 * slot + at) % 8 for at in range(5)]
    return jnp.stack([strip, slot % 2] + cols).astype(jnp.int32)


def nt(one, two):
    return lax.dot_general(one, two, (((1,), (1,)), ((), ())), preferred_element_type=WIDE)


def nn(one, two):
    return jnp.dot(one, two, preferred_element_type=WIDE)


def fill_outs(odd, held, outs):
    for at, (which, turn) in enumerate(OWNER_STEPS):
        row = (turn + odd) % 2
        for kind in range(2):
            if which == 2:
                outs[at][kind] = held[kind, row, 4 - 4 * odd]
            else:
                for part in range(2):
                    outs[at][kind, part] = held[kind, row, odd + 2 * which + part]


def owner_shapes():
    return [
        jax.ShapeDtypeStruct((2, TILE, HEAD_DIM) if which == 2 else (2, 2, TILE, HEAD_DIM), LOW)
        for which, _ in OWNER_STEPS
    ]


def attend_kernel(table, own, *refs):
    halos, grads = refs[:8], refs[8:14]
    outs, terms, edges = refs[14:20], refs[20], refs[21:29]
    pair, turned, grad, total, held = refs[29:]
    strip, odd = table[0], table[1]
    scaling = HEAD_DIM**-0.5
    rate = scaling * math.log2(math.e)

    for kind in range(2):
        for at in range(5):
            for row in range(2):
                pair[kind, at + 1, row] = own[kind + 1, row, at]
            pair[kind, at + 1, 2] = halos[0][kind, at]
            pair[kind, at + 1, 3] = halos[1][kind, at]
        for row in range(2):
            pair[kind, 0, row] = halos[2][kind, row]
            pair[kind, 6, row] = halos[3][kind, row]
        pair[kind, 0, 2] = halos[4][kind]
        pair[kind, 6, 2] = halos[5][kind]
        pair[kind, 0, 3] = halos[6][kind]
        pair[kind, 6, 3] = halos[7][kind]
    for kind in range(2):
        for at in range(7):
            for row in range(4):
                turned[kind, at, row] = pair[kind, at, row].T
    for at, (which, turn) in enumerate(OWNER_STEPS):
        row = (turn + odd) % 2
        if which == 2:
            grad[row, 4 - 4 * odd] = grads[at][...]
        else:
            for part in range(2):
                grad[row, odd + 2 * which + part] = grads[at][part]
    total[...] = jnp.zeros_like(total)

    def one_unit(unit, carry):
        column = table[2 + unit]
        queries = [own[0, row, unit] for row in range(2)]
        both = jnp.concatenate(queries, axis=0)
        ups = [grad[row, unit] for row in range(2)]
        up_both = jnp.concatenate(ups, axis=0)
        column_ok = (column > 0, None, column < 7)
        row_ok = (strip > 0, strip < STRIPS - 1)

        def products(kind, left, left_both):
            inner, outer = [], []
            for step in range(3):
                slot = unit + step
                near = pair[kind, slot, 0:2].reshape(2 * TILE, HEAD_DIM)
                inner.append(nt(near, left_both))
                outer.append(
                    jnp.concatenate(
                        [nt(pair[kind, slot, 2 + row], left[row]) for row in range(2)], axis=1
                    )
                )
            return inner, outer

        inner, outer = products(0, queries, both)
        lane = lax.broadcasted_iota(jnp.int32, (1, 2 * TILE), 1)
        row_bias = jnp.where(
            lane < TILE,
            jnp.where(row_ok[0], 0.0, NEVER),
            jnp.where(row_ok[1], 0.0, NEVER),
        )
        for step in range(3):
            if column_ok[step] is None:
                outer[step] = outer[step] + row_bias
            else:
                bias = jnp.where(column_ok[step], 0.0, NEVER)
                inner[step] = inner[step] + bias
                outer[step] = outer[step] + (row_bias + bias)
        highest = functools.reduce(
            jnp.maximum, [jnp.max(block, axis=0, keepdims=True) for block in inner + outer]
        )
        raised = [jnp.exp2((block - highest) * rate) for block in inner + outer]
        amount = sum(jnp.sum(block, axis=0, keepdims=True) for block in raised)
        inverse = 1.0 / amount
        weights = [block * inverse for block in raised]
        low = [block.astype(LOW) for block in weights]

        def mix(kind, parts):
            near = sum(
                nn(turned[kind, unit + step, row], parts[step][row * TILE : (row + 1) * TILE])
                for step in range(3)
                for row in range(2)
            )
            far = [
                sum(
                    nn(
                        turned[kind, unit + step, 2 + row],
                        parts[3 + step][:, row * TILE : (row + 1) * TILE],
                    )
                    for step in range(3)
                )
                for row in range(2)
            ]
            return near + jnp.concatenate(far, axis=1)

        def fold(kind, parts, right, right_both):
            for step in range(3):
                slot = unit + step
                near = nn(parts[step], right_both)
                for row in range(2):
                    total[kind, slot, row] += near[row * TILE : (row + 1) * TILE]
                    total[kind, slot, 2 + row] += nn(
                        parts[3 + step][:, row * TILE : (row + 1) * TILE], right[row]
                    )

        mixed = mix(1, low).T
        offsets = jnp.sum((up_both.astype(WIDE) * mixed).T, axis=0, keepdims=True)
        for row in range(2):
            held[0, row, unit] = mixed[row * TILE : (row + 1) * TILE].astype(LOW)
        fold(1, low, ups, up_both)
        inner, outer = products(1, ups, up_both)
        slopes = [
            (weight * (block - offsets)).astype(LOW)
            for weight, block in zip(weights, inner + outer)
        ]
        query_grad = mix(0, slopes).T * scaling
        for row in range(2):
            held[1, row, unit] = query_grad[row * TILE : (row + 1) * TILE].astype(LOW)
        fold(0, slopes, queries, both)
        return carry

    lax.fori_loop(0, 5, one_unit, 0)
    fill_outs(odd, held, outs)
    for kind, factor in ((0, scaling), (1, 1.0)):
        for at in range(5):
            for row in range(2):
                terms[kind, row, at] = total[kind, at + 1, row] * factor
            edges[0][kind, at] = (total[kind, at + 1, 3] * factor).astype(LOW)
            edges[1][kind, at] = (total[kind, at + 1, 2] * factor).astype(LOW)
        for row in range(2):
            edges[2][kind, row] = (total[kind, 6, row] * factor).astype(LOW)
            edges[3][kind, row] = (total[kind, 0, row] * factor).astype(LOW)
        edges[4][kind] = (total[kind, 6, 3] * factor).astype(LOW)
        edges[5][kind] = (total[kind, 0, 3] * factor).astype(LOW)
        edges[6][kind] = (total[kind, 6, 2] * factor).astype(LOW)
        edges[7][kind] = (total[kind, 0, 2] * factor).astype(LOW)


def halo_shapes():
    middle = [(5,), (5,), (2,), (2,), (), (), (), ()]
    return [jax.ShapeDtypeStruct((2,) + size + (TILE, HEAD_DIM), LOW) for size in middle]


def attend(table, own, halos, grads):
    return pl.pallas_call(
        attend_kernel,
        out_shape=owner_shapes()
        + [jax.ShapeDtypeStruct((2, 2, 5, TILE, HEAD_DIM), WIDE)]
        + halo_shapes(),
        in_specs=[pl.BlockSpec(memory_space=pltpu.SMEM)] + whole(15),
        out_specs=whole(15),
        scratch_shapes=[
            pltpu.VMEM((2, 7, 4, TILE, HEAD_DIM), LOW),
            pltpu.VMEM((2, 7, 4, HEAD_DIM, TILE), LOW),
            pltpu.VMEM((2, 5, TILE, HEAD_DIM), LOW),
            pltpu.VMEM((2, 7, 4, TILE, HEAD_DIM), WIDE),
            pltpu.VMEM((2, 2, 5, TILE, HEAD_DIM), LOW),
        ],
        compiler_params=pltpu.CompilerParams(vmem_limit_bytes=40 << 20),
        cost_estimate=pl.CostEstimate(
            flops=3_000_000_000, bytes_accessed=8_000_000, transcendentals=1_500_000
        ),
        name="attend",
    )(table, own, *halos, *grads)


def combine_kernel(table, terms, *refs):
    edges, outs, held = refs[:8], refs[8:14], refs[14]
    for kind in range(2):
        for row in range(2):
            for at in range(5):
                value = terms[kind, row, at] + edges[row][kind, at].astype(WIDE)
                if at == 0:
                    value = value + edges[2][kind, row].astype(WIDE)
                    value = value + edges[4 + 2 * row][kind].astype(WIDE)
                if at == 4:
                    value = value + edges[3][kind, row].astype(WIDE)
                    value = value + edges[5 + 2 * row][kind].astype(WIDE)
                held[kind, row, at] = value.astype(LOW)
    fill_outs(table[1], held, outs)


def combine(table, terms, edges):
    return pl.pallas_call(
        combine_kernel,
        out_shape=owner_shapes(),
        in_specs=[pl.BlockSpec(memory_space=pltpu.SMEM)] + whole(9),
        out_specs=whole(6),
        scratch_shapes=[pltpu.VMEM((2, 2, 5, TILE, HEAD_DIM), LOW)],
        compiler_params=pltpu.CompilerParams(vmem_limit_bytes=16 << 20),
        name="combine",
    )(table, terms, *edges)


def send_all(parts, routes):
    return [lax.ppermute(part, "tile", path) for part, path in zip(parts, routes)]


def local(query_slab, key_slab, value_slab, upstream):
    owners = owner_table()
    units = unit_table()
    to_owner = [owner_of(which, turn) for which, turn in OWNER_STEPS]
    halo_routes = [shifted(*step) for step in HALO_STEPS]

    with jax.named_scope("upstream_to_units"):
        grads = send_all(spread(owners, upstream), [flipped(path) for path in to_owner])

    with jax.named_scope("heads"):
        lines = [
            slab.reshape(8, 4, 40, 128).transpose(2, 0, 1, 3).reshape(8, 5, 32, 128)
            for slab in (query_slab, key_slab, value_slab)
        ]
        by_head = lax.all_to_all(jnp.stack(lines, axis=1), "head", 0, 0, tiled=True)
    with jax.named_scope("tiles"):
        shaped = by_head.reshape(8, 3, 5, 4, 8, 128).transpose(3, 2, 0, 1, 4, 5)
        got = lax.all_to_all(shaped.reshape(32, 5, 3, 8, 128), "tile", 0, 0, tiled=True)
        own = got.reshape(32, 5, 3, 2, 4, 128).transpose(2, 3, 1, 0, 4, 5)
        own = own.reshape(3, 2, 5, TILE, HEAD_DIM)
    with jax.named_scope("halos"):
        pair = own[1:]
        leaving = [
            pair[:, 1],
            pair[:, 0],
            pair[:, :, 4],
            pair[:, :, 0],
            pair[:, 1, 4],
            pair[:, 1, 0],
            pair[:, 0, 4],
            pair[:, 0, 0],
        ]
        halos = send_all(leaving, halo_routes)
    with jax.named_scope("attention"):
        results = attend(units, own, halos, grads)
    first, terms, edges = results[:6], results[6], results[7:]
    with jax.named_scope("terms"):
        edges = send_all(edges, halo_routes)
    with jax.named_scope("outputs_home"):
        first = send_all(first, to_owner)
    with jax.named_scope("key_terms_home"):
        second = send_all(combine(units, terms, edges), to_owner)
    with jax.named_scope("settle"):
        return tuple(gather(owners, first, second))


def solution(mesh):
    slab = P("tile", None, "head", None)
    block = P("tile", "head")
    return jax.shard_map(
        local,
        mesh=mesh,
        in_specs=(slab, slab, slab, block),
        out_specs=(block, block, block, block),
        check_vma=False,
    )
```

```python
import functools
import math

import jax
import jax.numpy as jnp
import numpy as np
from jax import lax
from jax.experimental import pallas as pl
from jax.experimental.pallas import tpu as pltpu
from jax.sharding import PartitionSpec as P

HEAD_DIM = 128
HEADS_HERE = 5
STRIPS = 4
SLOTS = 8
TILE = 128
LOW = jnp.bfloat16
WIDE = jnp.float32
NEVER = -1e30


def route(step):
    pairs = []
    for strip in range(STRIPS):
        for slot in range(SLOTS):
            goal = step(strip, slot)
            if goal is not None:
                pairs.append((strip * SLOTS + slot, goal[0] * SLOTS + goal[1]))
    return pairs


def shifted(rows, columns):
    def step(strip, slot):
        there = (strip + rows, slot + columns)
        return there if 0 <= there[0] < STRIPS and 0 <= there[1] < SLOTS else None

    return route(step)


def owner_of(which, turn):
    def step(strip, slot):
        odd = slot % 2
        if which == 2:
            unit = 5 * slot + (0 if odd else 4)
        else:
            unit = 5 * slot + odd + 2 * which
        return (strip, ((turn + odd) % 2) * 4 + (unit % 8) // 2)

    return route(step)


def flipped(pairs):
    return [(target, source) for source, target in pairs]


ROW_STEPS = ((1, 0), (-1, 0))
COLUMN_STEPS = ((0, 1), (0, -1))
OWNER_STEPS = tuple((which, turn) for which in range(3) for turn in range(2))


def whole(count):
    return [pl.BlockSpec(memory_space=pltpu.VMEM)] * count


def owner_table():
    slot = lax.axis_index("tile") % SLOTS
    row, pair = slot // 4, slot % 4
    heads = []
    for which, turn in OWNER_STEPS:
        odd = (row + turn) % 2
        if which == 2:
            unit = 10 * ((pair + 2) % 4) + 4
        else:
            even_unit = 10 * ((pair - which + 4) % 4) + 2 * which
            odd_unit = 10 * ((pair - 3 - which + 8) % 4) + 6 + 2 * which
            unit = jnp.where(odd == 1, odd_unit, even_unit)
        heads.append(unit // 8)
    return jnp.stack(heads + [row]).astype(jnp.int32)


def spread_kernel(table, upstream, *outs):
    line = lax.broadcasted_iota(jnp.int32, (2 * TILE, 2 * TILE), 0)
    col = lax.broadcasted_iota(jnp.int32, (2 * TILE, 2 * TILE), 1)
    source = ((line & 127) >> 2) * 8 + (line >> 7) * 4 + (line & 3)
    order = (col == source).astype(LOW)
    for at, (which, turn) in enumerate(OWNER_STEPS):
        head = pl.multiple_of(table[at] * HEAD_DIM, HEAD_DIM)
        tiles = jnp.dot(order, upstream[:, pl.ds(head, HEAD_DIM)], preferred_element_type=WIDE)
        tiles = tiles.astype(LOW)
        if which == 2:
            second = ((table[6] + turn) % 2) == 1
            outs[at][...] = jnp.where(second, tiles[TILE:], tiles[:TILE])
        else:
            outs[at][...] = tiles.reshape(2, TILE, HEAD_DIM)


def spread(table, upstream):
    shapes = [
        jax.ShapeDtypeStruct((TILE, HEAD_DIM) if which == 2 else (2, TILE, HEAD_DIM), LOW)
        for which, _ in OWNER_STEPS
    ]
    return pl.pallas_call(
        spread_kernel,
        out_shape=shapes,
        in_specs=[pl.BlockSpec(memory_space=pltpu.SMEM)] + whole(1),
        out_specs=whole(6),
        compiler_params=pltpu.CompilerParams(vmem_limit_bytes=16 << 20),
        name="spread",
    )(table, upstream)


def gather_kernel(table, *refs):
    first, second, outs = refs[:6], refs[6:12], refs[12:16]
    single = refs[16]
    line = lax.broadcasted_iota(jnp.int32, (2 * TILE, 2 * TILE), 0)
    col = lax.broadcasted_iota(jnp.int32, (2 * TILE, 2 * TILE), 1)
    source = ((line >> 2) & 1) * TILE + (line >> 3) * 4 + (line & 3)
    order = (col == source).astype(LOW)
    for group, received in enumerate((first, second)):
        for kind in range(2):
            out = outs[2 * group + kind]
            for at in range(4):
                head = pl.multiple_of(table[at] * HEAD_DIM, HEAD_DIM)
                tiles = received[at][kind].reshape(2 * TILE, HEAD_DIM)
                out[:, pl.ds(head, HEAD_DIM)] = jnp.dot(
                    order, tiles, preferred_element_type=WIDE
                ).astype(LOW)
            flip = table[6] == 1
            one, two = received[4][kind], received[5][kind]
            single[:TILE] = jnp.where(flip, two, one)
            single[TILE:] = jnp.where(flip, one, two)
            head = pl.multiple_of(table[4] * HEAD_DIM, HEAD_DIM)
            out[:, pl.ds(head, HEAD_DIM)] = jnp.dot(
                order, single[...], preferred_element_type=WIDE
            ).astype(LOW)


def gather(table, first, second):
    return pl.pallas_call(
        gather_kernel,
        out_shape=[jax.ShapeDtypeStruct((2 * TILE, HEADS_HERE * HEAD_DIM), LOW)] * 4,
        in_specs=[pl.BlockSpec(memory_space=pltpu.SMEM)] + whole(12),
        out_specs=whole(4),
        scratch_shapes=[pltpu.VMEM((2 * TILE, HEAD_DIM), LOW)],
        compiler_params=pltpu.CompilerParams(vmem_limit_bytes=16 << 20),
        name="gather",
    )(table, *first, *second)


def unit_table():
    place = lax.axis_index("tile")
    strip, slot = place // SLOTS, place % SLOTS
    cols = [(5 * slot + at) % 8 for at in range(5)]
    return jnp.stack([strip, slot % 2] + cols).astype(jnp.int32)


def nt(one, two):
    return lax.dot_general(one, two, (((1,), (1,)), ((), ())), preferred_element_type=WIDE)


def nn(one, two):
    return jnp.dot(one, two, preferred_element_type=WIDE)


def fill_outs(odd, held, outs):
    for at, (which, turn) in enumerate(OWNER_STEPS):
        row = (turn + odd) % 2
        for kind in range(2):
            if which == 2:
                outs[at][kind] = held[kind, row, 4 - 4 * odd]
            else:
                for part in range(2):
                    outs[at][kind, part] = held[kind, row, odd + 2 * which + part]


def owner_shapes():
    return [
        jax.ShapeDtypeStruct((2, TILE, HEAD_DIM) if which == 2 else (2, 2, TILE, HEAD_DIM), LOW)
        for which, _ in OWNER_STEPS
    ]


def attend_kernel(table, own, near, *refs):
    halos, grads = refs[:4], refs[4:10]
    outs, terms, edges = refs[10:16], refs[16], refs[17:19]
    pair, turned, grad, total, held = refs[19:]
    strip, odd = table[0], table[1]
    scaling = HEAD_DIM**-0.5
    rate = scaling * math.log2(math.e)

    for kind in range(2):
        for at in range(5):
            for row in range(2):
                pair[kind, at + 1, row] = near[kind, row, at]
        for row in range(2):
            pair[kind, 0, row] = halos[0][kind, row]
            pair[kind, 6, row] = halos[1][kind, row]
        for at in range(7):
            pair[kind, at, 2] = halos[2][kind, at]
            pair[kind, at, 3] = halos[3][kind, at]
    for kind in range(2):
        for at in range(7):
            for row in range(4):
                turned[kind, at, row] = pair[kind, at, row].T
    for at, (which, turn) in enumerate(OWNER_STEPS):
        row = (turn + odd) % 2
        if which == 2:
            grad[row, 4 - 4 * odd] = grads[at][...]
        else:
            for part in range(2):
                grad[row, odd + 2 * which + part] = grads[at][part]
    total[...] = jnp.zeros_like(total)

    def one_unit(unit, carry):
        column = table[2 + unit]
        queries = [own[row, unit] for row in range(2)]
        both = jnp.concatenate(queries, axis=0)
        ups = [grad[row, unit] for row in range(2)]
        up_both = jnp.concatenate(ups, axis=0)
        column_ok = (column > 0, None, column < 7)
        row_ok = (strip > 0, strip < STRIPS - 1)

        def products(kind, left, left_both):
            inner, outer = [], []
            for step in range(3):
                slot = unit + step
                near = pair[kind, slot, 0:2].reshape(2 * TILE, HEAD_DIM)
                inner.append(nt(near, left_both))
                outer.append(
                    jnp.concatenate(
                        [nt(pair[kind, slot, 2 + row], left[row]) for row in range(2)], axis=1
                    )
                )
            return inner, outer

        inner, outer = products(0, queries, both)
        lane = lax.broadcasted_iota(jnp.int32, (1, 2 * TILE), 1)
        row_bias = jnp.where(
            lane < TILE,
            jnp.where(row_ok[0], 0.0, NEVER),
            jnp.where(row_ok[1], 0.0, NEVER),
        )
        for step in range(3):
            if column_ok[step] is None:
                outer[step] = outer[step] + row_bias
            else:
                bias = jnp.where(column_ok[step], 0.0, NEVER)
                inner[step] = inner[step] + bias
                outer[step] = outer[step] + (row_bias + bias)
        highest = functools.reduce(
            jnp.maximum, [jnp.max(block, axis=0, keepdims=True) for block in inner + outer]
        )
        raised = [jnp.exp2((block - highest) * rate) for block in inner + outer]
        amount = sum(jnp.sum(block, axis=0, keepdims=True) for block in raised)
        inverse = 1.0 / amount
        weights = [block * inverse for block in raised]
        low = [block.astype(LOW) for block in weights]

        def mix(kind, parts):
            near = sum(
                nn(turned[kind, unit + step, row], parts[step][row * TILE : (row + 1) * TILE])
                for step in range(3)
                for row in range(2)
            )
            far = [
                sum(
                    nn(
                        turned[kind, unit + step, 2 + row],
                        parts[3 + step][:, row * TILE : (row + 1) * TILE],
                    )
                    for step in range(3)
                )
                for row in range(2)
            ]
            return near + jnp.concatenate(far, axis=1)

        def fold(kind, parts, right, right_both):
            for step in range(3):
                slot = unit + step
                near = nn(parts[step], right_both)
                for row in range(2):
                    total[kind, slot, row] += near[row * TILE : (row + 1) * TILE]
                    total[kind, slot, 2 + row] += nn(
                        parts[3 + step][:, row * TILE : (row + 1) * TILE], right[row]
                    )

        mixed = mix(1, low).T
        offsets = jnp.sum((up_both.astype(WIDE) * mixed).T, axis=0, keepdims=True)
        for row in range(2):
            held[0, row, unit] = mixed[row * TILE : (row + 1) * TILE].astype(LOW)
        fold(1, low, ups, up_both)
        inner, outer = products(1, ups, up_both)
        slopes = [
            (weight * (block - offsets)).astype(LOW)
            for weight, block in zip(weights, inner + outer)
        ]
        query_grad = mix(0, slopes).T * scaling
        for row in range(2):
            held[1, row, unit] = query_grad[row * TILE : (row + 1) * TILE].astype(LOW)
        fold(0, slopes, queries, both)
        return carry

    lax.fori_loop(0, 5, one_unit, 0)
    fill_outs(odd, held, outs)
    for kind, factor in ((0, scaling), (1, 1.0)):
        for at in range(7):
            for row in range(2):
                terms[kind, row, at] = total[kind, at, row] * factor
                edges[row][kind, at] = (total[kind, at, 3 - row] * factor).astype(LOW)


def column_shapes():
    return [jax.ShapeDtypeStruct((2, 2, TILE, HEAD_DIM), LOW)] * 2


def attend(table, own, pair, halos, grads):
    return pl.pallas_call(
        attend_kernel,
        out_shape=owner_shapes()
        + [jax.ShapeDtypeStruct((2, 2, 7, TILE, HEAD_DIM), WIDE)]
        + [jax.ShapeDtypeStruct((2, 7, TILE, HEAD_DIM), LOW)] * 2,
        in_specs=[pl.BlockSpec(memory_space=pltpu.SMEM)] + whole(12),
        out_specs=whole(9),
        scratch_shapes=[
            pltpu.VMEM((2, 7, 4, TILE, HEAD_DIM), LOW),
            pltpu.VMEM((2, 7, 4, HEAD_DIM, TILE), LOW),
            pltpu.VMEM((2, 5, TILE, HEAD_DIM), LOW),
            pltpu.VMEM((2, 7, 4, TILE, HEAD_DIM), WIDE),
            pltpu.VMEM((2, 2, 5, TILE, HEAD_DIM), LOW),
        ],
        compiler_params=pltpu.CompilerParams(vmem_limit_bytes=40 << 20),
        cost_estimate=pl.CostEstimate(
            flops=3_000_000_000, bytes_accessed=8_000_000, transcendentals=1_500_000
        ),
        name="attend",
    )(table, own, pair, *halos, *grads)


def rims_kernel(terms, above, below, right, left):
    for kind in range(2):
        for row, edge in enumerate((above, below)):
            for out, at in ((right, 6), (left, 0)):
                out[kind, row] = (terms[kind, row, at] + edge[kind, at].astype(WIDE)).astype(LOW)


def rims(terms, edges):
    return pl.pallas_call(
        rims_kernel,
        out_shape=column_shapes(),
        in_specs=whole(3),
        out_specs=whole(2),
        compiler_params=pltpu.CompilerParams(vmem_limit_bytes=16 << 20),
        name="rims",
    )(terms, *edges)


def combine_kernel(table, terms, *refs):
    edges, columns, outs, held = refs[:2], refs[2:4], refs[4:10], refs[10]
    for kind in range(2):
        for row in range(2):
            for at in range(5):
                value = terms[kind, row, at + 1] + edges[row][kind, at + 1].astype(WIDE)
                if at == 0:
                    value = value + columns[0][kind, row].astype(WIDE)
                if at == 4:
                    value = value + columns[1][kind, row].astype(WIDE)
                held[kind, row, at] = value.astype(LOW)
    fill_outs(table[1], held, outs)


def combine(table, terms, edges, columns):
    return pl.pallas_call(
        combine_kernel,
        out_shape=owner_shapes(),
        in_specs=[pl.BlockSpec(memory_space=pltpu.SMEM)] + whole(5),
        out_specs=whole(6),
        scratch_shapes=[pltpu.VMEM((2, 2, 5, TILE, HEAD_DIM), LOW)],
        compiler_params=pltpu.CompilerParams(vmem_limit_bytes=16 << 20),
        name="combine",
    )(table, terms, *edges, *columns)


def send_all(parts, routes):
    return [lax.ppermute(part, "tile", path) for part, path in zip(parts, routes)]


def local(query_slab, key_slab, value_slab, upstream):
    owners = owner_table()
    units = unit_table()
    to_owner = [owner_of(which, turn) for which, turn in OWNER_STEPS]
    row_routes = [shifted(*step) for step in ROW_STEPS]
    column_routes = [shifted(*step) for step in COLUMN_STEPS]

    with jax.named_scope("upstream_to_units"):
        grads = send_all(spread(owners, upstream), [flipped(path) for path in to_owner])

    def by_head(*slabs):
        lines = [
            slab.reshape(8, 4, 40, 128).transpose(2, 0, 1, 3).reshape(8, 5, 32, 128)
            for slab in slabs
        ]
        return jnp.stack(lines, axis=1)

    def by_unit(swapped):
        shaped = swapped.reshape(8, -1, 5, 4, 8, 128).transpose(3, 2, 0, 1, 4, 5)
        return shaped.reshape(32, 5, -1, 8, 128)

    def by_tile(got):
        own = got.reshape(32, 5, -1, 2, 4, 128).transpose(2, 3, 1, 0, 4, 5)
        return own.reshape(-1, 2, 5, TILE, HEAD_DIM)

    with jax.named_scope("heads"):
        lines = by_head(key_slab, value_slab, query_slab)
        swapped = lax.all_to_all(lines, "head", 0, 0, tiled=True)
    with jax.named_scope("key_value_tiles"):
        shaped, grads = lax.optimization_barrier((by_unit(swapped[:, :2]), grads))
        pair = by_tile(lax.all_to_all(shaped, "tile", 0, 0, tiled=True))
    with jax.named_scope("query_tiles"):
        own = by_tile(lax.all_to_all(by_unit(swapped[:, 2:]), "tile", 0, 0, tiled=True))[0]
    with jax.named_scope("halos"):
        sides = send_all([pair[:, :, 4], pair[:, :, 0]], column_routes)
        leaving = [
            jnp.concatenate([sides[0][:, row, None], pair[:, row], sides[1][:, row, None]], axis=1)
            for row in (1, 0)
        ]
        halos = sides + send_all(leaving, row_routes)
    with jax.named_scope("attention"):
        results = attend(units, own, pair, halos, grads)
    first, terms, edges = results[:6], results[6], results[7:]
    with jax.named_scope("terms"):
        edges = send_all(edges, row_routes)
        early = send_all(first[:3], to_owner[:3])
        edges, early = lax.optimization_barrier((edges, early))
        columns = send_all(rims(terms, edges), column_routes)
        late = send_all(first[3:], to_owner[3:])
    with jax.named_scope("key_terms_home"):
        columns, late = lax.optimization_barrier((columns, late))
        second = send_all(combine(units, terms, edges, columns), to_owner)
    first = early + late
    with jax.named_scope("settle"):
        return tuple(gather(owners, first, second))


def solution(mesh):
    slab = P("tile", None, "head", None)
    block = P("tile", "head")
    return jax.shard_map(
        local,
        mesh=mesh,
        in_specs=(slab, slab, slab, block),
        out_specs=(block, block, block, block),
        check_vma=False,
    )
```

```python
import functools
import math

import jax
import jax.numpy as jnp
import numpy as np
from jax import lax
from jax.experimental import pallas as pl
from jax.experimental.pallas import tpu as pltpu
from jax.sharding import PartitionSpec as P

HEAD_DIM = 128
HEADS_HERE = 5
STRIPS = 4
SLOTS = 8
TILE = 128
LOW = jnp.bfloat16
WIDE = jnp.float32
NEVER = -1e30


def route(step):
    pairs = []
    for strip in range(STRIPS):
        for slot in range(SLOTS):
            goal = step(strip, slot)
            if goal is not None:
                pairs.append((strip * SLOTS + slot, goal[0] * SLOTS + goal[1]))
    return pairs


def shifted(rows, columns):
    def step(strip, slot):
        there = (strip + rows, slot + columns)
        return there if 0 <= there[0] < STRIPS and 0 <= there[1] < SLOTS else None

    return route(step)


def owner_of(which, turn):
    def step(strip, slot):
        odd = slot % 2
        if which == 2:
            unit = 5 * slot + (0 if odd else 4)
        else:
            unit = 5 * slot + odd + 2 * which
        return (strip, ((turn + odd) % 2) * 4 + (unit % 8) // 2)

    return route(step)


def flipped(pairs):
    return [(target, source) for source, target in pairs]


ROW_STEPS = ((1, 0), (-1, 0))
COLUMN_STEPS = ((0, 1), (0, -1))
EARLY = 3
OWNER_STEPS = tuple((which, turn) for which in range(3) for turn in range(2))


def nt(one, two):
    return lax.dot_general(one, two, (((1,), (1,)), ((), ())), preferred_element_type=WIDE)


def nn(one, two):
    return jnp.dot(one, two, preferred_element_type=WIDE)


def whole(count):
    return [pl.BlockSpec(memory_space=pltpu.VMEM)] * count


def owner_rows():
    rows = []
    for slot in range(SLOTS):
        row, pair = slot // 4, slot % 4
        heads = []
        for which, turn in OWNER_STEPS:
            if which == 2:
                unit = 10 * ((pair + 2) % 4) + 4
            elif (row + turn) % 2:
                unit = 10 * ((pair - 3 - which) % 4) + 6 + 2 * which
            else:
                unit = 10 * ((pair - which) % 4) + 2 * which
            heads.append(unit // 8)
        rows.append(heads + [row])
    return rows


def place_table():
    owners = owner_rows()
    rows = [
        owners[slot] + [strip, slot % 2] + [(5 * slot + at) % 8 for at in range(5)]
        for strip in range(STRIPS)
        for slot in range(SLOTS)
    ]
    every = jnp.asarray(np.array(rows, np.int32))
    return lax.dynamic_index_in_dim(every, lax.axis_index("tile"), 0, keepdims=False)


def spread_kernel(table, upstream, *outs):
    line = lax.broadcasted_iota(jnp.int32, (2 * TILE, 2 * TILE), 0)
    col = lax.broadcasted_iota(jnp.int32, (2 * TILE, 2 * TILE), 1)
    source = ((line & 127) >> 2) * 8 + (line >> 7) * 4 + (line & 3)
    order = (col == source).astype(LOW)
    for at, (which, turn) in enumerate(OWNER_STEPS):
        head = pl.multiple_of(table[at] * HEAD_DIM, HEAD_DIM)
        tiles = jnp.dot(order, upstream[:, pl.ds(head, HEAD_DIM)], preferred_element_type=WIDE)
        tiles = tiles.astype(LOW)
        if which == 2:
            second = ((table[6] + turn) % 2) == 1
            outs[at][...] = jnp.where(second, tiles[TILE:], tiles[:TILE])
        else:
            outs[at][...] = tiles.reshape(2, TILE, HEAD_DIM)


def spread(table, upstream):
    shapes = [
        jax.ShapeDtypeStruct((TILE, HEAD_DIM) if which == 2 else (2, TILE, HEAD_DIM), LOW)
        for which, _ in OWNER_STEPS
    ]
    return pl.pallas_call(
        spread_kernel,
        out_shape=shapes,
        in_specs=[pl.BlockSpec(memory_space=pltpu.SMEM)] + whole(1),
        out_specs=whole(6),
        compiler_params=pltpu.CompilerParams(vmem_limit_bytes=16 << 20),
        name="spread",
    )(table, upstream)


def gather_kernel(table, *refs):
    received, outs, single = refs[:6], refs[6:10], refs[10]
    line = lax.broadcasted_iota(jnp.int32, (2 * TILE, 2 * TILE), 0)
    col = lax.broadcasted_iota(jnp.int32, (2 * TILE, 2 * TILE), 1)
    source = ((line >> 2) & 1) * TILE + (line >> 3) * 4 + (line & 3)
    order = (col == source).astype(LOW)
    for kind, out in enumerate(outs):
        for at in range(4):
            head = pl.multiple_of(table[at] * HEAD_DIM, HEAD_DIM)
            tiles = received[at][kind].reshape(2 * TILE, HEAD_DIM)
            out[:, pl.ds(head, HEAD_DIM)] = nn(order, tiles).astype(LOW)
        flip = table[6] == 1
        one, two = received[4][kind], received[5][kind]
        single[:TILE] = jnp.where(flip, two, one)
        single[TILE:] = jnp.where(flip, one, two)
        head = pl.multiple_of(table[4] * HEAD_DIM, HEAD_DIM)
        out[:, pl.ds(head, HEAD_DIM)] = nn(order, single[...]).astype(LOW)


def gather(table, received):
    return pl.pallas_call(
        gather_kernel,
        out_shape=[jax.ShapeDtypeStruct((2 * TILE, HEADS_HERE * HEAD_DIM), LOW)] * 4,
        in_specs=[pl.BlockSpec(memory_space=pltpu.SMEM)] + whole(6),
        out_specs=whole(4),
        scratch_shapes=[pltpu.VMEM((2 * TILE, HEAD_DIM), LOW)],
        compiler_params=pltpu.CompilerParams(vmem_limit_bytes=16 << 20),
        name="gather",
    )(table, *received)


def deal_kernel(swapped, out):
    for slot in range(SLOTS):
        for at in range(7):
            unit = min(max(5 * slot + at - 1, 0), 39)
            head, column = unit // 8, unit % 8
            for kind in range(3):
                if kind == 0 and not 1 <= at <= 5:
                    continue
                place = at - 1 if kind == 0 else 7 * kind - 2 + at
                lines = swapped[column, kind, head].reshape(STRIPS, 8, HEAD_DIM)
                for strip in range(STRIPS):
                    out[strip * SLOTS + slot, place] = lines[strip]


def deal(swapped):
    return pl.pallas_call(
        deal_kernel,
        out_shape=jax.ShapeDtypeStruct((STRIPS * SLOTS, 19, 8, HEAD_DIM), LOW),
        in_specs=whole(1),
        out_specs=whole(1)[0],
        compiler_params=pltpu.CompilerParams(vmem_limit_bytes=16 << 20),
        name="deal",
    )(swapped)


def attend_kernel(table, own, above, below, *refs):
    grads, held, terms, edges = refs[:6], refs[6], refs[7], refs[8:10]
    pair, turned, grad, total = refs[10:]
    strip, odd = table[7], table[8]
    scaling = HEAD_DIM**-0.5
    rate = scaling * math.log2(math.e)

    for kind in range(2):
        for at in range(7):
            for row in range(2):
                pair[kind, at, row] = own[row, 5 + 7 * kind + at]
            pair[kind, at, 2] = above[7 * kind + at]
            pair[kind, at, 3] = below[7 * kind + at]
    for kind in range(2):
        for at in range(7):
            for row in range(4):
                turned[kind, at, row] = pair[kind, at, row].T
    for at, (which, turn) in enumerate(OWNER_STEPS):
        row = (turn + odd) % 2
        if which == 2:
            grad[row, 4 - 4 * odd] = grads[at][...]
        else:
            for part in range(2):
                grad[row, odd + 2 * which + part] = grads[at][part]
    total[...] = jnp.zeros_like(total)

    def one_unit(unit, carry):
        column = table[9 + unit]
        queries = [own[row, unit] for row in range(2)]
        both = jnp.concatenate(queries, axis=0)
        ups = [grad[row, unit] for row in range(2)]
        up_both = jnp.concatenate(ups, axis=0)
        column_ok = (column > 0, None, column < 7)
        row_ok = (strip > 0, strip < STRIPS - 1)

        def products(kind, left, left_both):
            inner, outer = [], []
            for step in range(3):
                slot = unit + step
                near = pair[kind, slot, 0:2].reshape(2 * TILE, HEAD_DIM)
                inner.append(nt(near, left_both))
                outer.append(
                    jnp.concatenate(
                        [nt(pair[kind, slot, 2 + row], left[row]) for row in range(2)], axis=1
                    )
                )
            return inner, outer

        inner, outer = products(0, queries, both)
        lane = lax.broadcasted_iota(jnp.int32, (1, 2 * TILE), 1)
        row_bias = jnp.where(
            lane < TILE,
            jnp.where(row_ok[0], 0.0, NEVER),
            jnp.where(row_ok[1], 0.0, NEVER),
        )
        for step in range(3):
            if column_ok[step] is None:
                outer[step] = outer[step] + row_bias
            else:
                bias = jnp.where(column_ok[step], 0.0, NEVER)
                inner[step] = inner[step] + bias
                outer[step] = outer[step] + (row_bias + bias)
        highest = functools.reduce(
            jnp.maximum, [jnp.max(block, axis=0, keepdims=True) for block in inner + outer]
        )
        raised = [jnp.exp2((block - highest) * rate) for block in inner + outer]
        amount = sum(jnp.sum(block, axis=0, keepdims=True) for block in raised)
        inverse = 1.0 / amount
        weights = [block * inverse for block in raised]
        low = [block.astype(LOW) for block in weights]

        def mix(kind, parts):
            near = sum(
                nn(turned[kind, unit + step, row], parts[step][row * TILE : (row + 1) * TILE])
                for step in range(3)
                for row in range(2)
            )
            far = [
                sum(
                    nn(
                        turned[kind, unit + step, 2 + row],
                        parts[3 + step][:, row * TILE : (row + 1) * TILE],
                    )
                    for step in range(3)
                )
                for row in range(2)
            ]
            return near + jnp.concatenate(far, axis=1)

        def fold(kind, parts, right, right_both):
            for step in range(3):
                slot = unit + step
                near = nn(parts[step], right_both)
                for row in range(2):
                    total[kind, slot, row] += near[row * TILE : (row + 1) * TILE]
                    total[kind, slot, 2 + row] += nn(
                        parts[3 + step][:, row * TILE : (row + 1) * TILE], right[row]
                    )

        mixed = mix(1, low).T
        offsets = jnp.sum((up_both.astype(WIDE) * mixed).T, axis=0, keepdims=True)
        for row in range(2):
            held[0, row, unit] = mixed[row * TILE : (row + 1) * TILE].astype(LOW)
        fold(1, low, ups, up_both)
        inner, outer = products(1, ups, up_both)
        slopes = [
            (weight * (block - offsets)).astype(LOW)
            for weight, block in zip(weights, inner + outer)
        ]
        query_grad = mix(0, slopes).T * scaling
        for row in range(2):
            held[1, row, unit] = query_grad[row * TILE : (row + 1) * TILE].astype(LOW)
        fold(0, slopes, queries, both)
        return carry

    lax.fori_loop(0, 5, one_unit, 0)
    for kind, factor in ((0, scaling), (1, 1.0)):
        for at in range(7):
            for row in range(2):
                terms[kind, row, at] = total[kind, at, row] * factor
                edges[row][kind, at] = (total[kind, at, 3 - row] * factor).astype(LOW)


def column_shapes():
    return [jax.ShapeDtypeStruct((2, 2, TILE, HEAD_DIM), LOW)] * 2


def attend(table, own, halos, grads):
    return pl.pallas_call(
        attend_kernel,
        out_shape=[
            jax.ShapeDtypeStruct((2, 2, 5, TILE, HEAD_DIM), LOW),
            jax.ShapeDtypeStruct((2, 2, 7, TILE, HEAD_DIM), WIDE),
            jax.ShapeDtypeStruct((2, 7, TILE, HEAD_DIM), LOW),
            jax.ShapeDtypeStruct((2, 7, TILE, HEAD_DIM), LOW),
        ],
        in_specs=[pl.BlockSpec(memory_space=pltpu.SMEM)] + whole(9),
        out_specs=whole(4),
        scratch_shapes=[
            pltpu.VMEM((2, 7, 4, TILE, HEAD_DIM), LOW),
            pltpu.VMEM((2, 7, 4, HEAD_DIM, TILE), LOW),
            pltpu.VMEM((2, 5, TILE, HEAD_DIM), LOW),
            pltpu.VMEM((2, 7, 4, TILE, HEAD_DIM), WIDE),
        ],
        compiler_params=pltpu.CompilerParams(vmem_limit_bytes=40 << 20),
        cost_estimate=pl.CostEstimate(
            flops=3_000_000_000, bytes_accessed=8_000_000, transcendentals=1_500_000
        ),
        name="attend",
    )(table, own, *halos, *grads)


def rims_kernel(terms, above, below, right, left):
    for kind in range(2):
        for row, edge in enumerate((above, below)):
            for out, at in ((right, 6), (left, 0)):
                out[kind, row] = (terms[kind, row, at] + edge[kind, at].astype(WIDE)).astype(LOW)


def rims(terms, edges):
    return pl.pallas_call(
        rims_kernel,
        out_shape=column_shapes(),
        in_specs=whole(3),
        out_specs=whole(2),
        compiler_params=pltpu.CompilerParams(vmem_limit_bytes=16 << 20),
        name="rims",
    )(terms, *edges)


def combine_kernel(table, first, terms, *refs):
    edges, columns, outs, held = refs[:2], refs[2:4], refs[4:10], refs[10]
    odd = table[8]
    for kind in range(2):
        for row in range(2):
            for at in range(5):
                value = terms[kind, row, at + 1] + edges[row][kind, at + 1].astype(WIDE)
                if at == 0:
                    value = value + columns[0][kind, row].astype(WIDE)
                if at == 4:
                    value = value + columns[1][kind, row].astype(WIDE)
                held[kind, row, at] = value.astype(LOW)
    for at, (which, turn) in enumerate(OWNER_STEPS):
        row = (turn + odd) % 2
        for kind in range(4):
            source = (first, held)[kind // 2]
            if which == 2:
                outs[at][kind] = source[kind % 2, row, 4 - 4 * odd]
            else:
                for part in range(2):
                    outs[at][kind, part] = source[kind % 2, row, odd + 2 * which + part]


def combine(table, first, terms, edges, columns):
    shapes = [
        jax.ShapeDtypeStruct((4, TILE, HEAD_DIM) if which == 2 else (4, 2, TILE, HEAD_DIM), LOW)
        for which, _ in OWNER_STEPS
    ]
    return pl.pallas_call(
        combine_kernel,
        out_shape=shapes,
        in_specs=[pl.BlockSpec(memory_space=pltpu.SMEM)] + whole(6),
        out_specs=whole(6),
        scratch_shapes=[pltpu.VMEM((2, 2, 5, TILE, HEAD_DIM), LOW)],
        compiler_params=pltpu.CompilerParams(vmem_limit_bytes=16 << 20),
        name="combine",
    )(table, first, terms, *edges, *columns)


def send_all(parts, routes):
    return [lax.ppermute(part, "tile", path) for part, path in zip(parts, routes)]


def local(query_slab, key_slab, value_slab, upstream):
    place = place_table()
    to_owner = [owner_of(which, turn) for which, turn in OWNER_STEPS]
    row_routes = [shifted(*step) for step in ROW_STEPS]
    column_routes = [shifted(*step) for step in COLUMN_STEPS]

    with jax.named_scope("upstream_to_units"):
        grads = send_all(spread(place, upstream), [flipped(path) for path in to_owner])

    with jax.named_scope("heads"):
        lines = [
            slab.reshape(8, 4, 40, 128).transpose(2, 0, 1, 3).reshape(8, 5, 32, 128)
            for slab in (query_slab, key_slab, value_slab)
        ]
        swapped = lax.all_to_all(jnp.stack(lines, axis=1), "head", 0, 0, tiled=True)
    with jax.named_scope("tiles"):
        dealt, early = lax.optimization_barrier((deal(swapped), grads[:EARLY]))
        got = lax.all_to_all(dealt, "tile", 0, 0, tiled=True)
        own = got.reshape(32, 19, 2, 4, 128).transpose(2, 1, 0, 3, 4)
        own = own.reshape(2, 19, TILE, HEAD_DIM)
        own, late = lax.optimization_barrier((own, grads[EARLY:]))
    with jax.named_scope("halos"):
        halos = send_all([own[1, 5:], own[0, 5:]], row_routes)
    with jax.named_scope("attention"):
        first, terms, *edges = attend(place, own, halos, early + late)
    with jax.named_scope("terms"):
        edges = send_all(edges, row_routes)
        columns = send_all(rims(terms, edges), column_routes)
    with jax.named_scope("outputs_home"):
        received = send_all(combine(place, first, terms, edges, columns), to_owner)
    with jax.named_scope("settle"):
        return tuple(gather(place, received))


def solution(mesh):
    slab = P("tile", None, "head", None)
    block = P("tile", "head")
    return jax.shard_map(
        local,
        mesh=mesh,
        in_specs=(slab, slab, slab, block),
        out_specs=(block, block, block, block),
        check_vma=False,
    )
```

```python
import functools
import math

import jax
import jax.numpy as jnp
import numpy as np
from jax import lax
from jax.experimental import pallas as pl
from jax.experimental.pallas import tpu as pltpu
from jax.sharding import PartitionSpec as P

HEAD_DIM = 128
HEADS_HERE = 5
STRIPS = 4
SLOTS = 8
TILE = 128
LOW = jnp.bfloat16
WIDE = jnp.float32
NEVER = -1e30


def route(step):
    pairs = []
    for strip in range(STRIPS):
        for slot in range(SLOTS):
            goal = step(strip, slot)
            if goal is not None:
                pairs.append((strip * SLOTS + slot, goal[0] * SLOTS + goal[1]))
    return pairs


def shifted(rows, columns):
    def step(strip, slot):
        there = (strip + rows, slot + columns)
        return there if 0 <= there[0] < STRIPS and 0 <= there[1] < SLOTS else None

    return route(step)


def owner_of(which, turn):
    def step(strip, slot):
        odd = slot % 2
        if which == 2:
            unit = 5 * slot + (0 if odd else 4)
        else:
            unit = 5 * slot + odd + 2 * which
        return (strip, ((turn + odd) % 2) * 4 + (unit % 8) // 2)

    return route(step)


def flipped(pairs):
    return [(target, source) for source, target in pairs]


ROW_STEPS = ((1, 0), (-1, 0))
COLUMN_STEPS = ((0, 1), (0, -1))
EARLY = 3
OWNER_STEPS = tuple((which, turn) for which in range(3) for turn in range(2))


def nt(one, two):
    return lax.dot_general(one, two, (((1,), (1,)), ((), ())), preferred_element_type=WIDE)


def nn(one, two):
    return jnp.dot(one, two, preferred_element_type=WIDE)


def whole(count):
    return [pl.BlockSpec(memory_space=pltpu.VMEM)] * count


def owner_rows():
    rows = []
    for slot in range(SLOTS):
        row, pair = slot // 4, slot % 4
        heads = []
        for which, turn in OWNER_STEPS:
            if which == 2:
                unit = 10 * ((pair + 2) % 4) + 4
            elif (row + turn) % 2:
                unit = 10 * ((pair - 3 - which) % 4) + 6 + 2 * which
            else:
                unit = 10 * ((pair - which) % 4) + 2 * which
            heads.append(unit // 8)
        rows.append(heads + [row])
    return rows


def place_table():
    owners = owner_rows()
    rows = [
        owners[slot] + [strip, slot % 2] + [(5 * slot + at) % 8 for at in range(5)]
        for strip in range(STRIPS)
        for slot in range(SLOTS)
    ]
    every = jnp.asarray(np.array(rows, np.int32))
    return lax.dynamic_index_in_dim(every, lax.axis_index("tile"), 0, keepdims=False)


def spread_kernel(table, upstream, *outs):
    line = lax.broadcasted_iota(jnp.int32, (2 * TILE, 2 * TILE), 0)
    col = lax.broadcasted_iota(jnp.int32, (2 * TILE, 2 * TILE), 1)
    source = ((line & 127) >> 2) * 8 + (line >> 7) * 4 + (line & 3)
    order = (col == source).astype(LOW)
    for at, (which, turn) in enumerate(OWNER_STEPS):
        head = pl.multiple_of(table[at] * HEAD_DIM, HEAD_DIM)
        tiles = jnp.dot(order, upstream[:, pl.ds(head, HEAD_DIM)], preferred_element_type=WIDE)
        tiles = tiles.astype(LOW)
        if which == 2:
            second = ((table[6] + turn) % 2) == 1
            outs[at][...] = jnp.where(second, tiles[TILE:], tiles[:TILE])
        else:
            outs[at][...] = tiles.reshape(2, TILE, HEAD_DIM)


def spread(table, upstream):
    shapes = [
        jax.ShapeDtypeStruct((TILE, HEAD_DIM) if which == 2 else (2, TILE, HEAD_DIM), LOW)
        for which, _ in OWNER_STEPS
    ]
    return pl.pallas_call(
        spread_kernel,
        out_shape=shapes,
        in_specs=[pl.BlockSpec(memory_space=pltpu.SMEM)] + whole(1),
        out_specs=whole(6),
        compiler_params=pltpu.CompilerParams(vmem_limit_bytes=16 << 20),
        name="spread",
    )(table, upstream)


def gather_kernel(table, *refs):
    firsts, seconds, singles, outs, single = refs[:4], refs[4:8], refs[8:10], refs[10:14], refs[14]
    line = lax.broadcasted_iota(jnp.int32, (2 * TILE, 2 * TILE), 0)
    col = lax.broadcasted_iota(jnp.int32, (2 * TILE, 2 * TILE), 1)
    source = ((line >> 2) & 1) * TILE + (line >> 3) * 4 + (line & 3)
    order = (col == source).astype(LOW)
    for kind, out in enumerate(outs):
        for at in range(4):
            head = pl.multiple_of(table[at] * HEAD_DIM, HEAD_DIM)
            tiles = (firsts, seconds)[kind // 2][at][kind % 2].reshape(2 * TILE, HEAD_DIM)
            out[:, pl.ds(head, HEAD_DIM)] = nn(order, tiles).astype(LOW)
        flip = table[6] == 1
        one, two = singles[0][kind], singles[1][kind]
        single[:TILE] = jnp.where(flip, two, one)
        single[TILE:] = jnp.where(flip, one, two)
        head = pl.multiple_of(table[4] * HEAD_DIM, HEAD_DIM)
        out[:, pl.ds(head, HEAD_DIM)] = nn(order, single[...]).astype(LOW)


def gather(table, first, second):
    return pl.pallas_call(
        gather_kernel,
        out_shape=[jax.ShapeDtypeStruct((2 * TILE, HEADS_HERE * HEAD_DIM), LOW)] * 4,
        in_specs=[pl.BlockSpec(memory_space=pltpu.SMEM)] + whole(10),
        out_specs=whole(4),
        scratch_shapes=[pltpu.VMEM((2 * TILE, HEAD_DIM), LOW)],
        compiler_params=pltpu.CompilerParams(vmem_limit_bytes=16 << 20),
        name="gather",
    )(table, *first, *second)


def deal_kernel(swapped, out):
    for slot in range(SLOTS):
        for at in range(7):
            unit = min(max(5 * slot + at - 1, 0), 39)
            head, column = unit // 8, unit % 8
            for kind in range(3):
                if kind == 0 and not 1 <= at <= 5:
                    continue
                place = at - 1 if kind == 0 else 7 * kind - 2 + at
                lines = swapped[column, kind, head].reshape(STRIPS, 8, HEAD_DIM)
                for strip in range(STRIPS):
                    out[strip * SLOTS + slot, place] = lines[strip]


def deal(swapped):
    return pl.pallas_call(
        deal_kernel,
        out_shape=jax.ShapeDtypeStruct((STRIPS * SLOTS, 19, 8, HEAD_DIM), LOW),
        in_specs=whole(1),
        out_specs=whole(1)[0],
        compiler_params=pltpu.CompilerParams(vmem_limit_bytes=16 << 20),
        name="deal",
    )(swapped)


def send_pairs(odd, held, outs):
    for out, (which, turn) in zip(outs, OWNER_STEPS):
        row = (turn + odd) % 2
        for kind in range(2):
            for part in range(2):
                out[kind, part] = held[kind, row, odd + 2 * which + part]


def pair_shapes():
    return [jax.ShapeDtypeStruct((2, 2, TILE, HEAD_DIM), LOW)] * 4


def attend_kernel(table, own, above, below, *refs):
    grads, firsts, rest, terms, edges = refs[:6], refs[6:10], refs[10], refs[11], refs[12:14]
    pair, turned, grad, total, held = refs[14:]
    strip, odd = table[7], table[8]
    scaling = HEAD_DIM**-0.5
    rate = scaling * math.log2(math.e)

    for kind in range(2):
        for at in range(7):
            for row in range(2):
                pair[kind, at, row] = own[row, 5 + 7 * kind + at]
            pair[kind, at, 2] = above[7 * kind + at]
            pair[kind, at, 3] = below[7 * kind + at]
    for kind in range(2):
        for at in range(7):
            for row in range(4):
                turned[kind, at, row] = pair[kind, at, row].T
    for at, (which, turn) in enumerate(OWNER_STEPS):
        row = (turn + odd) % 2
        if which == 2:
            grad[row, 4 - 4 * odd] = grads[at][...]
        else:
            for part in range(2):
                grad[row, odd + 2 * which + part] = grads[at][part]
    total[...] = jnp.zeros_like(total)

    def one_unit(unit, carry):
        column = table[9 + unit]
        queries = [own[row, unit] for row in range(2)]
        both = jnp.concatenate(queries, axis=0)
        ups = [grad[row, unit] for row in range(2)]
        up_both = jnp.concatenate(ups, axis=0)
        column_ok = (column > 0, None, column < 7)
        row_ok = (strip > 0, strip < STRIPS - 1)

        def products(kind, left, left_both):
            inner, outer = [], []
            for step in range(3):
                slot = unit + step
                near = pair[kind, slot, 0:2].reshape(2 * TILE, HEAD_DIM)
                inner.append(nt(near, left_both))
                outer.append(
                    jnp.concatenate(
                        [nt(pair[kind, slot, 2 + row], left[row]) for row in range(2)], axis=1
                    )
                )
            return inner, outer

        inner, outer = products(0, queries, both)
        lane = lax.broadcasted_iota(jnp.int32, (1, 2 * TILE), 1)
        row_bias = jnp.where(
            lane < TILE,
            jnp.where(row_ok[0], 0.0, NEVER),
            jnp.where(row_ok[1], 0.0, NEVER),
        )
        for step in range(3):
            if column_ok[step] is None:
                outer[step] = outer[step] + row_bias
            else:
                bias = jnp.where(column_ok[step], 0.0, NEVER)
                inner[step] = inner[step] + bias
                outer[step] = outer[step] + (row_bias + bias)
        highest = functools.reduce(
            jnp.maximum, [jnp.max(block, axis=0, keepdims=True) for block in inner + outer]
        )
        raised = [jnp.exp2((block - highest) * rate) for block in inner + outer]
        amount = sum(jnp.sum(block, axis=0, keepdims=True) for block in raised)
        inverse = 1.0 / amount
        weights = [block * inverse for block in raised]
        low = [block.astype(LOW) for block in weights]

        def mix(kind, parts):
            near = sum(
                nn(turned[kind, unit + step, row], parts[step][row * TILE : (row + 1) * TILE])
                for step in range(3)
                for row in range(2)
            )
            far = [
                sum(
                    nn(
                        turned[kind, unit + step, 2 + row],
                        parts[3 + step][:, row * TILE : (row + 1) * TILE],
                    )
                    for step in range(3)
                )
                for row in range(2)
            ]
            return near + jnp.concatenate(far, axis=1)

        def fold(kind, parts, right, right_both):
            for step in range(3):
                slot = unit + step
                near = nn(parts[step], right_both)
                for row in range(2):
                    total[kind, slot, row] += near[row * TILE : (row + 1) * TILE]
                    total[kind, slot, 2 + row] += nn(
                        parts[3 + step][:, row * TILE : (row + 1) * TILE], right[row]
                    )

        mixed = mix(1, low).T
        offsets = jnp.sum((up_both.astype(WIDE) * mixed).T, axis=0, keepdims=True)
        for row in range(2):
            held[0, row, unit] = mixed[row * TILE : (row + 1) * TILE].astype(LOW)
        fold(1, low, ups, up_both)
        inner, outer = products(1, ups, up_both)
        slopes = [
            (weight * (block - offsets)).astype(LOW)
            for weight, block in zip(weights, inner + outer)
        ]
        query_grad = mix(0, slopes).T * scaling
        for row in range(2):
            held[1, row, unit] = query_grad[row * TILE : (row + 1) * TILE].astype(LOW)
        fold(0, slopes, queries, both)
        return carry

    lax.fori_loop(0, 5, one_unit, 0)
    send_pairs(odd, held, firsts)
    for kind in range(2):
        for row in range(2):
            rest[kind, row] = held[kind, row, 4 - 4 * odd]
    for kind, factor in ((0, scaling), (1, 1.0)):
        for at in range(7):
            for row in range(2):
                terms[kind, row, at] = total[kind, at, row] * factor
                edges[row][kind, at] = (total[kind, at, 3 - row] * factor).astype(LOW)


def column_shapes():
    return [jax.ShapeDtypeStruct((2, 2, TILE, HEAD_DIM), LOW)] * 2


def attend(table, own, halos, grads):
    return pl.pallas_call(
        attend_kernel,
        out_shape=pair_shapes()
        + [
            jax.ShapeDtypeStruct((2, 2, TILE, HEAD_DIM), LOW),
            jax.ShapeDtypeStruct((2, 2, 7, TILE, HEAD_DIM), WIDE),
            jax.ShapeDtypeStruct((2, 7, TILE, HEAD_DIM), LOW),
            jax.ShapeDtypeStruct((2, 7, TILE, HEAD_DIM), LOW),
        ],
        in_specs=[pl.BlockSpec(memory_space=pltpu.SMEM)] + whole(9),
        out_specs=whole(8),
        scratch_shapes=[
            pltpu.VMEM((2, 7, 4, TILE, HEAD_DIM), LOW),
            pltpu.VMEM((2, 7, 4, HEAD_DIM, TILE), LOW),
            pltpu.VMEM((2, 5, TILE, HEAD_DIM), LOW),
            pltpu.VMEM((2, 7, 4, TILE, HEAD_DIM), WIDE),
            pltpu.VMEM((2, 2, 5, TILE, HEAD_DIM), LOW),
        ],
        compiler_params=pltpu.CompilerParams(vmem_limit_bytes=40 << 20),
        cost_estimate=pl.CostEstimate(
            flops=3_000_000_000, bytes_accessed=8_000_000, transcendentals=1_500_000
        ),
        name="attend",
    )(table, own, *halos, *grads)


def rims_kernel(terms, above, below, right, left):
    for kind in range(2):
        for row, edge in enumerate((above, below)):
            for out, at in ((right, 6), (left, 0)):
                out[kind, row] = (terms[kind, row, at] + edge[kind, at].astype(WIDE)).astype(LOW)


def rims(terms, edges):
    return pl.pallas_call(
        rims_kernel,
        out_shape=column_shapes(),
        in_specs=whole(3),
        out_specs=whole(2),
        compiler_params=pltpu.CompilerParams(vmem_limit_bytes=16 << 20),
        name="rims",
    )(terms, *edges)


def combine_kernel(table, rest, terms, *refs):
    edges, columns, outs, held = refs[:2], refs[2:4], refs[4:10], refs[10]
    odd = table[8]
    for kind in range(2):
        for row in range(2):
            for at in range(5):
                value = terms[kind, row, at + 1] + edges[row][kind, at + 1].astype(WIDE)
                if at == 0:
                    value = value + columns[0][kind, row].astype(WIDE)
                if at == 4:
                    value = value + columns[1][kind, row].astype(WIDE)
                held[kind, row, at] = value.astype(LOW)
    send_pairs(odd, held, outs[:4])
    for turn in range(2):
        row = (turn + odd) % 2
        for kind in range(2):
            outs[4 + turn][kind] = rest[kind, row]
            outs[4 + turn][2 + kind] = held[kind, row, 4 - 4 * odd]


def combine(table, rest, terms, edges, columns):
    return pl.pallas_call(
        combine_kernel,
        out_shape=pair_shapes() + [jax.ShapeDtypeStruct((4, TILE, HEAD_DIM), LOW)] * 2,
        in_specs=[pl.BlockSpec(memory_space=pltpu.SMEM)] + whole(6),
        out_specs=whole(6),
        scratch_shapes=[pltpu.VMEM((2, 2, 5, TILE, HEAD_DIM), LOW)],
        compiler_params=pltpu.CompilerParams(vmem_limit_bytes=16 << 20),
        name="combine",
    )(table, rest, terms, *edges, *columns)


def send_all(parts, routes):
    return [lax.ppermute(part, "tile", path) for part, path in zip(parts, routes)]


def local(query_slab, key_slab, value_slab, upstream):
    place = place_table()
    to_owner = [owner_of(which, turn) for which, turn in OWNER_STEPS]
    row_routes = [shifted(*step) for step in ROW_STEPS]
    column_routes = [shifted(*step) for step in COLUMN_STEPS]

    with jax.named_scope("upstream_to_units"):
        grads = send_all(spread(place, upstream), [flipped(path) for path in to_owner])

    with jax.named_scope("heads"):
        lines = [
            slab.reshape(8, 4, 40, 128).transpose(2, 0, 1, 3).reshape(8, 5, 32, 128)
            for slab in (query_slab, key_slab, value_slab)
        ]
        swapped = lax.all_to_all(jnp.stack(lines, axis=1), "head", 0, 0, tiled=True)
    with jax.named_scope("tiles"):
        dealt, early = lax.optimization_barrier((deal(swapped), grads[:EARLY]))
        got = lax.all_to_all(dealt, "tile", 0, 0, tiled=True)
        own = got.reshape(32, 19, 2, 4, 128).transpose(2, 1, 0, 3, 4)
        own = own.reshape(2, 19, TILE, HEAD_DIM)
        own, late = lax.optimization_barrier((own, grads[EARLY:]))
    with jax.named_scope("halos"):
        halos = send_all([own[1, 5:], own[0, 5:]], row_routes)
    with jax.named_scope("attention"):
        *first, rest, terms, above, below = attend(place, own, halos, early + late)
    with jax.named_scope("terms"):
        edges = send_all([above, below], row_routes)
        early = send_all(first[:2], to_owner[:2])
        edges, early = lax.optimization_barrier((edges, early))
        columns = send_all(rims(terms, edges), column_routes)
        late = send_all(first[2:], to_owner[2:])
        columns, late = lax.optimization_barrier((columns, late))
    with jax.named_scope("outputs_home"):
        second = send_all(combine(place, rest, terms, edges, columns), to_owner)
    with jax.named_scope("settle"):
        return tuple(gather(place, early + late, second))


def solution(mesh):
    slab = P("tile", None, "head", None)
    block = P("tile", "head")
    return jax.shard_map(
        local,
        mesh=mesh,
        in_specs=(slab, slab, slab, block),
        out_specs=(block, block, block, block),
        check_vma=False,
    )
```

```python
import functools
import math

import jax
import jax.numpy as jnp
import numpy as np
from jax import lax
from jax.experimental import pallas as pl
from jax.experimental.pallas import tpu as pltpu
from jax.sharding import PartitionSpec as P

HEAD_DIM = 128
HEADS_HERE = 5
STRIPS = 4
SLOTS = 8
TILE = 128
LOW = jnp.bfloat16
WIDE = jnp.float32
NEVER = -1e30


def route(step):
    pairs = []
    for strip in range(STRIPS):
        for slot in range(SLOTS):
            goal = step(strip, slot)
            if goal is not None:
                pairs.append((strip * SLOTS + slot, goal[0] * SLOTS + goal[1]))
    return pairs


def shifted(rows, columns):
    def step(strip, slot):
        there = (strip + rows, slot + columns)
        return there if 0 <= there[0] < STRIPS and 0 <= there[1] < SLOTS else None

    return route(step)


def first_of(which, odd):
    return (3 * odd, 2 - odd, 4 - 4 * odd)[which]


def owner_of(which, turn):
    def step(strip, slot):
        odd = slot % 2
        unit = 5 * slot + first_of(which, odd)
        return (strip, ((turn + odd) % 2) * 4 + (unit % 8) // 2)

    return route(step)


def flipped(pairs):
    return [(target, source) for source, target in pairs]


ROW_STEPS = ((1, 0), (-1, 0))
COLUMN_STEPS = ((0, 1), (0, -1))
EARLY = 3
OWNER_STEPS = tuple((which, turn) for which in range(3) for turn in range(2))


def nt(one, two):
    return lax.dot_general(one, two, (((1,), (1,)), ((), ())), preferred_element_type=WIDE)


def nn(one, two):
    return jnp.dot(one, two, preferred_element_type=WIDE)


def whole(count):
    return [pl.BlockSpec(memory_space=pltpu.VMEM)] * count


def owner_rows():
    rows = []
    for slot in range(SLOTS):
        row, pair = slot // 4, slot % 4
        heads = []
        for which, turn in OWNER_STEPS:
            if which == 2:
                unit = 10 * ((pair + 2) % 4) + 4
            elif (row + turn) % 2:
                unit = 10 * ((pair - 3 * which) % 4) + 8 - 2 * which
            else:
                unit = 10 * ((pair - which) % 4) + 2 * which
            heads.append(unit // 8)
        rows.append(heads + [row])
    return rows


def place_table():
    owners = owner_rows()
    rows = [
        owners[slot] + [strip, slot % 2] + [(5 * slot + at) % 8 for at in range(5)]
        for strip in range(STRIPS)
        for slot in range(SLOTS)
    ]
    every = jnp.asarray(np.array(rows, np.int32))
    return lax.dynamic_index_in_dim(every, lax.axis_index("tile"), 0, keepdims=False)


def spread_kernel(table, upstream, *outs):
    line = lax.broadcasted_iota(jnp.int32, (2 * TILE, 2 * TILE), 0)
    col = lax.broadcasted_iota(jnp.int32, (2 * TILE, 2 * TILE), 1)
    source = ((line & 127) >> 2) * 8 + (line >> 7) * 4 + (line & 3)
    order = (col == source).astype(LOW)
    for at, (which, turn) in enumerate(OWNER_STEPS):
        head = pl.multiple_of(table[at] * HEAD_DIM, HEAD_DIM)
        tiles = jnp.dot(order, upstream[:, pl.ds(head, HEAD_DIM)], preferred_element_type=WIDE)
        tiles = tiles.astype(LOW)
        if which == 2:
            second = ((table[6] + turn) % 2) == 1
            outs[at][...] = jnp.where(second, tiles[TILE:], tiles[:TILE])
        else:
            outs[at][...] = tiles.reshape(2, TILE, HEAD_DIM)


def spread(table, upstream):
    shapes = [
        jax.ShapeDtypeStruct((TILE, HEAD_DIM) if which == 2 else (2, TILE, HEAD_DIM), LOW)
        for which, _ in OWNER_STEPS
    ]
    return pl.pallas_call(
        spread_kernel,
        out_shape=shapes,
        in_specs=[pl.BlockSpec(memory_space=pltpu.SMEM)] + whole(1),
        out_specs=whole(6),
        compiler_params=pltpu.CompilerParams(vmem_limit_bytes=16 << 20),
        name="spread",
    )(table, upstream)


def gather_kernel(table, *refs):
    early, free, late, singles = refs[:2], refs[2:4], refs[4:6], refs[6:8]
    outs, single = refs[8:12], refs[12]
    line = lax.broadcasted_iota(jnp.int32, (2 * TILE, 2 * TILE), 0)
    col = lax.broadcasted_iota(jnp.int32, (2 * TILE, 2 * TILE), 1)
    source = ((line >> 2) & 1) * TILE + (line >> 3) * 4 + (line & 3)
    order = (col == source).astype(LOW)
    for kind, out in enumerate(outs):
        for at in range(4):
            head = pl.multiple_of(table[at] * HEAD_DIM, HEAD_DIM)
            edge = (early, late)[kind // 2][at % 2].at[kind % 2]
            tiles = (edge[...] if at < 2 else free[at % 2][kind]).reshape(2 * TILE, HEAD_DIM)
            out[:, pl.ds(head, HEAD_DIM)] = nn(order, tiles).astype(LOW)
        flip = table[6] == 1
        one, two = singles[0][kind], singles[1][kind]
        single[:TILE] = jnp.where(flip, two, one)
        single[TILE:] = jnp.where(flip, one, two)
        head = pl.multiple_of(table[4] * HEAD_DIM, HEAD_DIM)
        out[:, pl.ds(head, HEAD_DIM)] = nn(order, single[...]).astype(LOW)


def gather(table, received):
    return pl.pallas_call(
        gather_kernel,
        out_shape=[jax.ShapeDtypeStruct((2 * TILE, HEADS_HERE * HEAD_DIM), LOW)] * 4,
        in_specs=[pl.BlockSpec(memory_space=pltpu.SMEM)] + whole(8),
        out_specs=whole(4),
        scratch_shapes=[pltpu.VMEM((2 * TILE, HEAD_DIM), LOW)],
        compiler_params=pltpu.CompilerParams(vmem_limit_bytes=16 << 20),
        name="gather",
    )(table, *received)


def deal_kernel(swapped, out):
    for slot in range(SLOTS):
        for at in range(7):
            unit = min(max(5 * slot + at - 1, 0), 39)
            head, column = unit // 8, unit % 8
            for kind in range(3):
                if kind == 0 and not 1 <= at <= 5:
                    continue
                place = at - 1 if kind == 0 else 7 * kind - 2 + at
                lines = swapped[column, kind, head].reshape(STRIPS, 8, HEAD_DIM)
                for strip in range(STRIPS):
                    out[strip * SLOTS + slot, place] = lines[strip]


def deal(swapped):
    return pl.pallas_call(
        deal_kernel,
        out_shape=jax.ShapeDtypeStruct((STRIPS * SLOTS, 19, 8, HEAD_DIM), LOW),
        in_specs=whole(1),
        out_specs=whole(1)[0],
        compiler_params=pltpu.CompilerParams(vmem_limit_bytes=16 << 20),
        name="deal",
    )(swapped)


def pair_shapes(kinds, count):
    return [jax.ShapeDtypeStruct((kinds, 2, TILE, HEAD_DIM), LOW)] * count


def attend_kernel(table, own, above, below, *refs):
    grads, firsts, rest, terms, edges = refs[:6], refs[6:8], refs[8], refs[9], refs[10:12]
    pair, turned, grad, total, held = refs[12:]
    strip, odd = table[7], table[8]
    scaling = HEAD_DIM**-0.5
    rate = scaling * math.log2(math.e)

    for kind in range(2):
        for at in range(7):
            for row in range(2):
                pair[kind, at, row] = own[row, 5 + 7 * kind + at]
            pair[kind, at, 2] = above[7 * kind + at]
            pair[kind, at, 3] = below[7 * kind + at]
    for kind in range(2):
        for at in range(7):
            for row in range(4):
                turned[kind, at, row] = pair[kind, at, row].T
    for at, (which, turn) in enumerate(OWNER_STEPS):
        row = (turn + odd) % 2
        first = first_of(which, odd)
        if which == 2:
            grad[row, first] = grads[at][...]
        else:
            for part in range(2):
                grad[row, first + part] = grads[at][part]
    total[...] = jnp.zeros_like(total)

    def one_unit(unit, carry):
        column = table[9 + unit]
        queries = [own[row, unit] for row in range(2)]
        both = jnp.concatenate(queries, axis=0)
        ups = [grad[row, unit] for row in range(2)]
        up_both = jnp.concatenate(ups, axis=0)
        column_ok = (column > 0, None, column < 7)
        row_ok = (strip > 0, strip < STRIPS - 1)

        def products(kind, left, left_both):
            inner, outer = [], []
            for step in range(3):
                slot = unit + step
                near = pair[kind, slot, 0:2].reshape(2 * TILE, HEAD_DIM)
                inner.append(nt(near, left_both))
                outer.append(
                    jnp.concatenate(
                        [nt(pair[kind, slot, 2 + row], left[row]) for row in range(2)], axis=1
                    )
                )
            return inner, outer

        inner, outer = products(0, queries, both)
        lane = lax.broadcasted_iota(jnp.int32, (1, 2 * TILE), 1)
        row_bias = jnp.where(
            lane < TILE,
            jnp.where(row_ok[0], 0.0, NEVER),
            jnp.where(row_ok[1], 0.0, NEVER),
        )
        for step in range(3):
            if column_ok[step] is None:
                outer[step] = outer[step] + row_bias
            else:
                bias = jnp.where(column_ok[step], 0.0, NEVER)
                inner[step] = inner[step] + bias
                outer[step] = outer[step] + (row_bias + bias)
        highest = functools.reduce(
            jnp.maximum, [jnp.max(block, axis=0, keepdims=True) for block in inner + outer]
        )
        raised = [jnp.exp2((block - highest) * rate) for block in inner + outer]
        amount = sum(jnp.sum(block, axis=0, keepdims=True) for block in raised)
        inverse = 1.0 / amount
        weights = [block * inverse for block in raised]
        low = [block.astype(LOW) for block in weights]

        def mix(kind, parts):
            near = sum(
                nn(turned[kind, unit + step, row], parts[step][row * TILE : (row + 1) * TILE])
                for step in range(3)
                for row in range(2)
            )
            far = [
                sum(
                    nn(
                        turned[kind, unit + step, 2 + row],
                        parts[3 + step][:, row * TILE : (row + 1) * TILE],
                    )
                    for step in range(3)
                )
                for row in range(2)
            ]
            return near + jnp.concatenate(far, axis=1)

        def fold(kind, parts, right, right_both):
            for step in range(3):
                slot = unit + step
                near = nn(parts[step], right_both)
                for row in range(2):
                    total[kind, slot, row] += near[row * TILE : (row + 1) * TILE]
                    total[kind, slot, 2 + row] += nn(
                        parts[3 + step][:, row * TILE : (row + 1) * TILE], right[row]
                    )

        mixed = mix(1, low).T
        offsets = jnp.sum((up_both.astype(WIDE) * mixed).T, axis=0, keepdims=True)
        for row in range(2):
            held[0, row, unit] = mixed[row * TILE : (row + 1) * TILE].astype(LOW)
        fold(1, low, ups, up_both)
        inner, outer = products(1, ups, up_both)
        slopes = [
            (weight * (block - offsets)).astype(LOW)
            for weight, block in zip(weights, inner + outer)
        ]
        query_grad = mix(0, slopes).T * scaling
        for row in range(2):
            held[1, row, unit] = query_grad[row * TILE : (row + 1) * TILE].astype(LOW)
        fold(0, slopes, queries, both)
        return carry

    lax.fori_loop(0, 5, one_unit, 0)
    for kind in range(2):
        for turn in range(2):
            row = (turn + odd) % 2
            for part in range(2):
                firsts[turn][kind, part] = held[kind, row, first_of(0, odd) + part]
                rest[kind, turn, part] = held[kind, row, first_of(1, odd) + part]
            rest[kind, turn, 2] = held[kind, row, first_of(2, odd)]
    for kind, factor in ((0, scaling), (1, 1.0)):
        for at in range(7):
            for row in range(2):
                terms[kind, row, at] = total[kind, at, row] * factor
                edges[row][kind, at] = (total[kind, at, 3 - row] * factor).astype(LOW)


def column_shapes():
    return [jax.ShapeDtypeStruct((2, 2, TILE, HEAD_DIM), LOW)] * 2


def attend(table, own, halos, grads):
    return pl.pallas_call(
        attend_kernel,
        out_shape=pair_shapes(2, 2)
        + [
            jax.ShapeDtypeStruct((2, 2, 3, TILE, HEAD_DIM), LOW),
            jax.ShapeDtypeStruct((2, 2, 7, TILE, HEAD_DIM), WIDE),
            jax.ShapeDtypeStruct((2, 7, TILE, HEAD_DIM), LOW),
            jax.ShapeDtypeStruct((2, 7, TILE, HEAD_DIM), LOW),
        ],
        in_specs=[pl.BlockSpec(memory_space=pltpu.SMEM)] + whole(9),
        out_specs=whole(6),
        scratch_shapes=[
            pltpu.VMEM((2, 7, 4, TILE, HEAD_DIM), LOW),
            pltpu.VMEM((2, 7, 4, HEAD_DIM, TILE), LOW),
            pltpu.VMEM((2, 5, TILE, HEAD_DIM), LOW),
            pltpu.VMEM((2, 7, 4, TILE, HEAD_DIM), WIDE),
            pltpu.VMEM((2, 2, 5, TILE, HEAD_DIM), LOW),
        ],
        compiler_params=pltpu.CompilerParams(vmem_limit_bytes=40 << 20),
        cost_estimate=pl.CostEstimate(
            flops=3_000_000_000, bytes_accessed=8_000_000, transcendentals=1_500_000
        ),
        name="attend",
    )(table, own, *halos, *grads)


def rims_kernel(table, rest, terms, above, below, right, left, *outs):
    odd = table[8]
    edges = (above, below)
    for kind in range(2):
        for row, edge in enumerate(edges):
            for out, at in ((right, 6), (left, 0)):
                out[kind, row] = (terms[kind, row, at] + edge[kind, at].astype(WIDE)).astype(LOW)
    for turn in range(2):
        for part in range(2):
            at = first_of(1, odd) + part + 1
            for kind in range(2):
                outs[turn][kind, part] = rest[kind, turn, part]
                flip = (turn + odd) % 2 == 1
                edge = jnp.where(flip, below[kind, at], above[kind, at])
                value = terms[kind, (turn + odd) % 2, at] + edge.astype(WIDE)
                outs[turn][2 + kind, part] = value.astype(LOW)


def rims(table, rest, terms, edges):
    return pl.pallas_call(
        rims_kernel,
        out_shape=column_shapes() + pair_shapes(4, 2),
        in_specs=[pl.BlockSpec(memory_space=pltpu.SMEM)] + whole(4),
        out_specs=whole(4),
        compiler_params=pltpu.CompilerParams(vmem_limit_bytes=16 << 20),
        name="rims",
    )(table, rest, terms, *edges)


def combine_kernel(table, rest, terms, above, below, before, after, *outs):
    odd = table[8]
    flipped = odd == 1
    for turn in range(2):
        row = (turn + odd) % 2
        for kind in range(2):

            def summed(at):
                edge = jnp.where(row == 1, below[kind, at + 1], above[kind, at + 1])
                return terms[kind, row, at + 1] + edge.astype(WIDE)

            first = first_of(0, odd)
            left = before[kind, row].astype(WIDE)
            right = after[kind, row].astype(WIDE)
            one, two = summed(first), summed(first + 1)
            outs[turn][kind, 0] = jnp.where(flipped, one, one + left).astype(LOW)
            outs[turn][kind, 1] = jnp.where(flipped, two + right, two).astype(LOW)
            alone = summed(first_of(2, odd)) + jnp.where(flipped, left, right)
            outs[2 + turn][kind] = rest[kind, turn, 2]
            outs[2 + turn][2 + kind] = alone.astype(LOW)


def combine(table, rest, terms, edges, columns):
    return pl.pallas_call(
        combine_kernel,
        out_shape=pair_shapes(2, 2) + [jax.ShapeDtypeStruct((4, TILE, HEAD_DIM), LOW)] * 2,
        in_specs=[pl.BlockSpec(memory_space=pltpu.SMEM)] + whole(6),
        out_specs=whole(4),
        compiler_params=pltpu.CompilerParams(vmem_limit_bytes=16 << 20),
        name="combine",
    )(table, rest, terms, *edges, *columns)


def send_all(parts, routes):
    return [lax.ppermute(part, "tile", path) for part, path in zip(parts, routes)]


def local(query_slab, key_slab, value_slab, upstream):
    place = place_table()
    to_owner = [owner_of(which, turn) for which, turn in OWNER_STEPS]
    row_routes = [shifted(*step) for step in ROW_STEPS]
    column_routes = [shifted(*step) for step in COLUMN_STEPS]

    with jax.named_scope("upstream_to_units"):
        grads = send_all(spread(place, upstream), [flipped(path) for path in to_owner])

    with jax.named_scope("heads"):
        lines = [
            slab.reshape(8, 4, 40, 128).transpose(2, 0, 1, 3).reshape(8, 5, 32, 128)
            for slab in (query_slab, key_slab, value_slab)
        ]
        swapped = lax.all_to_all(jnp.stack(lines, axis=1), "head", 0, 0, tiled=True)
    with jax.named_scope("tiles"):
        dealt, early = lax.optimization_barrier((deal(swapped), grads[:EARLY]))
        got = lax.all_to_all(dealt, "tile", 0, 0, tiled=True)
        own = got.reshape(32, 19, 2, 4, 128).transpose(2, 1, 0, 3, 4)
        own = own.reshape(2, 19, TILE, HEAD_DIM)
        own, late = lax.optimization_barrier((own, grads[EARLY:]))
    with jax.named_scope("halos"):
        halos = send_all([own[1, 5:], own[0, 5:]], row_routes)
    with jax.named_scope("attention"):
        *edge_pairs, rest, terms, above, below = attend(place, own, halos, early + late)
    with jax.named_scope("row_terms"):
        edges = send_all([above, below], row_routes)
        early = send_all(edge_pairs, to_owner[:2])
        edges, early = lax.optimization_barrier((edges, early))
    with jax.named_scope("column_terms"):
        right, left, *free = rims(place, rest, terms, edges)
        columns = send_all([right, left], column_routes)
        free = send_all(free, to_owner[2:4])
    with jax.named_scope("outputs_home"):
        leaving = combine(place, rest, terms, edges, columns)
        leaving, free = lax.optimization_barrier((leaving, free))
        late = send_all(leaving, to_owner[:2] + to_owner[4:])
    with jax.named_scope("settle"):
        return tuple(gather(place, early + free + late))


def solution(mesh):
    slab = P("tile", None, "head", None)
    block = P("tile", "head")
    return jax.shard_map(
        local,
        mesh=mesh,
        in_specs=(slab, slab, slab, block),
        out_specs=(block, block, block, block),
        check_vma=False,
    )
```

```python
import functools
import math

import jax
import jax.numpy as jnp
import numpy as np
from jax import lax
from jax.experimental import pallas as pl
from jax.experimental.pallas import tpu as pltpu
from jax.sharding import PartitionSpec as P

HEAD_DIM = 128
HEADS_HERE = 5
STRIPS = 4
SLOTS = 8
TILE = 128
LOW = jnp.bfloat16
WIDE = jnp.float32
NEVER = -1e30


def route(step):
    pairs = []
    for strip in range(STRIPS):
        for slot in range(SLOTS):
            goal = step(strip, slot)
            if goal is not None:
                pairs.append((strip * SLOTS + slot, goal[0] * SLOTS + goal[1]))
    return pairs


def shifted(rows, columns):
    def step(strip, slot):
        there = (strip + rows, slot + columns)
        return there if 0 <= there[0] < STRIPS and 0 <= there[1] < SLOTS else None

    return route(step)


def first_of(which, odd):
    return (3 * odd, 2 - odd, 4 - 4 * odd)[which]


def owner_of(which, turn):
    def step(strip, slot):
        odd = slot % 2
        unit = 5 * slot + first_of(which, odd)
        return (strip, ((turn + odd) % 2) * 4 + (unit % 8) // 2)

    return route(step)


def flipped(pairs):
    return [(target, source) for source, target in pairs]


ROW_STEPS = ((1, 0), (-1, 0))
COLUMN_STEPS = ((0, 1), (0, -1))
EARLY = 3
OWNER_STEPS = tuple((which, turn) for which in range(3) for turn in range(2))


def nt(one, two):
    return lax.dot_general(one, two, (((1,), (1,)), ((), ())), preferred_element_type=WIDE)


def nn(one, two):
    return jnp.dot(one, two, preferred_element_type=WIDE)


def whole(count):
    return [pl.BlockSpec(memory_space=pltpu.VMEM)] * count


def owner_rows():
    rows = []
    for slot in range(SLOTS):
        row, pair = slot // 4, slot % 4
        heads = []
        for which, turn in OWNER_STEPS:
            if which == 2:
                unit = 10 * ((pair + 2) % 4) + 4
            elif (row + turn) % 2:
                unit = 10 * ((pair - 3 * which) % 4) + 8 - 2 * which
            else:
                unit = 10 * ((pair - which) % 4) + 2 * which
            heads.append(unit // 8)
        rows.append(heads + [row])
    return rows


def place_table():
    owners = owner_rows()
    rows = [
        owners[slot] + [strip, slot % 2] + [(5 * slot + at) % 8 for at in range(5)]
        for strip in range(STRIPS)
        for slot in range(SLOTS)
    ]
    every = jnp.asarray(np.array(rows, np.int32))
    return lax.dynamic_index_in_dim(every, lax.axis_index("tile"), 0, keepdims=False)


def spread_kernel(table, upstream, *outs):
    line = lax.broadcasted_iota(jnp.int32, (2 * TILE, 2 * TILE), 0)
    col = lax.broadcasted_iota(jnp.int32, (2 * TILE, 2 * TILE), 1)
    source = ((line & 127) >> 2) * 8 + (line >> 7) * 4 + (line & 3)
    order = (col == source).astype(LOW)
    for at, (which, turn) in enumerate(OWNER_STEPS):
        head = pl.multiple_of(table[at] * HEAD_DIM, HEAD_DIM)
        tiles = jnp.dot(order, upstream[:, pl.ds(head, HEAD_DIM)], preferred_element_type=WIDE)
        tiles = tiles.astype(LOW)
        if which == 2:
            second = ((table[6] + turn) % 2) == 1
            outs[at][...] = jnp.where(second, tiles[TILE:], tiles[:TILE])
        else:
            outs[at][...] = tiles.reshape(2, TILE, HEAD_DIM)


def spread(table, upstream):
    shapes = [
        jax.ShapeDtypeStruct((TILE, HEAD_DIM) if which == 2 else (2, TILE, HEAD_DIM), LOW)
        for which, _ in OWNER_STEPS
    ]
    return pl.pallas_call(
        spread_kernel,
        out_shape=shapes,
        in_specs=[pl.BlockSpec(memory_space=pltpu.SMEM)] + whole(1),
        out_specs=whole(6),
        compiler_params=pltpu.CompilerParams(vmem_limit_bytes=16 << 20),
        name="spread",
    )(table, upstream)


def gather_kernel(table, *refs):
    free, late, singles = refs[:2], refs[2:4], refs[4:6]
    outs, single = refs[6:10], refs[10]
    line = lax.broadcasted_iota(jnp.int32, (2 * TILE, 2 * TILE), 0)
    col = lax.broadcasted_iota(jnp.int32, (2 * TILE, 2 * TILE), 1)
    source = ((line >> 2) & 1) * TILE + (line >> 3) * 4 + (line & 3)
    order = (col == source).astype(LOW)
    for kind, out in enumerate(outs):
        for at in range(4):
            head = pl.multiple_of(table[at] * HEAD_DIM, HEAD_DIM)
            tiles = (late, free)[at // 2][at % 2][kind].reshape(2 * TILE, HEAD_DIM)
            out[:, pl.ds(head, HEAD_DIM)] = nn(order, tiles).astype(LOW)
        flip = table[6] == 1
        one, two = singles[0][kind], singles[1][kind]
        single[:TILE] = jnp.where(flip, two, one)
        single[TILE:] = jnp.where(flip, one, two)
        head = pl.multiple_of(table[4] * HEAD_DIM, HEAD_DIM)
        out[:, pl.ds(head, HEAD_DIM)] = nn(order, single[...]).astype(LOW)


def gather(table, received):
    return pl.pallas_call(
        gather_kernel,
        out_shape=[jax.ShapeDtypeStruct((2 * TILE, HEADS_HERE * HEAD_DIM), LOW)] * 4,
        in_specs=[pl.BlockSpec(memory_space=pltpu.SMEM)] + whole(6),
        out_specs=whole(4),
        scratch_shapes=[pltpu.VMEM((2 * TILE, HEAD_DIM), LOW)],
        compiler_params=pltpu.CompilerParams(vmem_limit_bytes=16 << 20),
        name="gather",
    )(table, *received)


def deal_kernel(swapped, out):
    for slot in range(SLOTS):
        for at in range(7):
            unit = min(max(5 * slot + at - 1, 0), 39)
            head, column = unit // 8, unit % 8
            for kind in range(3):
                if kind == 0 and not 1 <= at <= 5:
                    continue
                place = at - 1 if kind == 0 else 7 * kind - 2 + at
                lines = swapped[column, kind, head].reshape(STRIPS, 8, HEAD_DIM)
                for strip in range(STRIPS):
                    out[strip * SLOTS + slot, place] = lines[strip]


def deal(swapped):
    return pl.pallas_call(
        deal_kernel,
        out_shape=jax.ShapeDtypeStruct((STRIPS * SLOTS, 19, 8, HEAD_DIM), LOW),
        in_specs=whole(1),
        out_specs=whole(1)[0],
        compiler_params=pltpu.CompilerParams(vmem_limit_bytes=16 << 20),
        name="deal",
    )(swapped)


def pair_shapes(kinds, count):
    return [jax.ShapeDtypeStruct((kinds, 2, TILE, HEAD_DIM), LOW)] * count


def attend_kernel(table, own, above, below, *refs):
    grads, rest, terms, edges = refs[:6], refs[6], refs[7], refs[8:10]
    pair, turned, outer_turned, grad, total, held = refs[10:]
    strip, odd = table[7], table[8]
    scaling = HEAD_DIM**-0.5
    rate = scaling * math.log2(math.e)

    for kind in range(2):
        for at in range(7):
            for row in range(2):
                pair[kind, at, row] = own[row, 5 + 7 * kind + at]
            pair[kind, at, 2] = above[7 * kind + at]
            pair[kind, at, 3] = below[7 * kind + at]
    for kind in range(2):
        for at in range(7):
            for row in range(2):
                lanes = pl.ds((2 * at + row) * TILE, TILE)
                turned[kind, :, lanes] = pair[kind, at, row].T
                outer_turned[kind, row, :, pl.ds(at * TILE, TILE)] = pair[kind, at, 2 + row].T
    for at, (which, turn) in enumerate(OWNER_STEPS):
        row = (turn + odd) % 2
        first = first_of(which, odd)
        if which == 2:
            grad[row, first] = grads[at][...]
        else:
            for part in range(2):
                grad[row, first + part] = grads[at][part]
    total[...] = jnp.zeros_like(total)

    def one_unit(unit, carry):
        column = table[9 + unit]
        queries = [own[row, unit] for row in range(2)]
        both = jnp.concatenate(queries, axis=0)
        ups = [grad[row, unit] for row in range(2)]
        up_both = jnp.concatenate(ups, axis=0)
        column_ok = (column > 0, None, column < 7)
        row_ok = (strip > 0, strip < STRIPS - 1)

        def products(kind, left, left_both):
            inner, outer = [], []
            for step in range(3):
                slot = unit + step
                near = pair[kind, slot, 0:2].reshape(2 * TILE, HEAD_DIM)
                inner.append(nt(near, left_both))
                outer.append(
                    jnp.concatenate(
                        [nt(pair[kind, slot, 2 + row], left[row]) for row in range(2)], axis=1
                    )
                )
            return inner, outer

        inner, outer = products(0, queries, both)
        lane = lax.broadcasted_iota(jnp.int32, (1, 2 * TILE), 1)
        row_bias = jnp.where(
            lane < TILE,
            jnp.where(row_ok[0], 0.0, NEVER),
            jnp.where(row_ok[1], 0.0, NEVER),
        )
        for step in range(3):
            if column_ok[step] is None:
                outer[step] = outer[step] + row_bias
            else:
                bias = jnp.where(column_ok[step], 0.0, NEVER)
                inner[step] = inner[step] + bias
                outer[step] = outer[step] + (row_bias + bias)
        highest = functools.reduce(
            jnp.maximum, [jnp.max(block, axis=0, keepdims=True) for block in inner + outer]
        )
        raised = [jnp.exp2((block - highest) * rate) for block in inner + outer]
        amount = sum(jnp.sum(block, axis=0, keepdims=True) for block in raised)
        inverse = 1.0 / amount
        weights = [block * inverse for block in raised]
        low = [block.astype(LOW) for block in weights]

        def mix(kind, parts):
            near = sum(
                nn(
                    turned[kind, :, pl.ds(pl.multiple_of((unit + step) * 256, 256), 256)],
                    parts[step],
                )
                for step in range(3)
            )
            far = [
                sum(
                    nn(
                        outer_turned[
                            kind, row, :, pl.ds(pl.multiple_of((unit + step) * TILE, TILE), TILE)
                        ],
                        parts[3 + step][:, row * TILE : (row + 1) * TILE],
                    )
                    for step in range(3)
                )
                for row in range(2)
            ]
            return near + jnp.concatenate(far, axis=1)

        def fold(kind, parts, right, right_both):
            for step in range(3):
                slot = unit + step
                near = nn(parts[step], right_both)
                for row in range(2):
                    total[kind, slot, row] += near[row * TILE : (row + 1) * TILE]
                    total[kind, slot, 2 + row] += nn(
                        parts[3 + step][:, row * TILE : (row + 1) * TILE], right[row]
                    )

        mixed = mix(1, low).T
        offsets = jnp.sum((up_both.astype(WIDE) * mixed).T, axis=0, keepdims=True)
        for row in range(2):
            held[0, row, unit] = mixed[row * TILE : (row + 1) * TILE].astype(LOW)
        fold(1, low, ups, up_both)
        inner, outer = products(1, ups, up_both)
        slopes = [
            (weight * (block - offsets)).astype(LOW)
            for weight, block in zip(weights, inner + outer)
        ]
        query_grad = mix(0, slopes).T * scaling
        for row in range(2):
            held[1, row, unit] = query_grad[row * TILE : (row + 1) * TILE].astype(LOW)
        fold(0, slopes, queries, both)
        return carry

    lax.fori_loop(0, 5, one_unit, 0, unroll=True)
    for kind in range(2):
        for turn in range(2):
            row = (turn + odd) % 2
            for part in range(2):
                rest[kind, turn, part] = held[kind, row, first_of(0, odd) + part]
                rest[kind, turn, 2 + part] = held[kind, row, first_of(1, odd) + part]
            rest[kind, turn, 4] = held[kind, row, first_of(2, odd)]
    for kind, factor in ((0, scaling), (1, 1.0)):
        for at in range(7):
            for row in range(2):
                terms[kind, row, at] = total[kind, at, row] * factor
                edges[row][kind, at] = (total[kind, at, 3 - row] * factor).astype(LOW)


def column_shapes():
    return [jax.ShapeDtypeStruct((2, 2, TILE, HEAD_DIM), LOW)] * 2


def attend(table, own, halos, grads):
    return pl.pallas_call(
        attend_kernel,
        out_shape=[
            jax.ShapeDtypeStruct((2, 2, 5, TILE, HEAD_DIM), LOW),
            jax.ShapeDtypeStruct((2, 2, 7, TILE, HEAD_DIM), WIDE),
            jax.ShapeDtypeStruct((2, 7, TILE, HEAD_DIM), LOW),
            jax.ShapeDtypeStruct((2, 7, TILE, HEAD_DIM), LOW),
        ],
        in_specs=[pl.BlockSpec(memory_space=pltpu.SMEM)] + whole(9),
        out_specs=whole(4),
        scratch_shapes=[
            pltpu.VMEM((2, 7, 4, TILE, HEAD_DIM), LOW),
            pltpu.VMEM((2, HEAD_DIM, 14 * TILE), LOW),
            pltpu.VMEM((2, 2, HEAD_DIM, 7 * TILE), LOW),
            pltpu.VMEM((2, 5, TILE, HEAD_DIM), LOW),
            pltpu.VMEM((2, 7, 4, TILE, HEAD_DIM), WIDE),
            pltpu.VMEM((2, 2, 5, TILE, HEAD_DIM), LOW),
        ],
        compiler_params=pltpu.CompilerParams(vmem_limit_bytes=40 << 20),
        cost_estimate=pl.CostEstimate(
            flops=3_000_000_000, bytes_accessed=8_000_000, transcendentals=1_500_000
        ),
        name="attend",
    )(table, own, *halos, *grads)


def rims_kernel(table, rest, terms, above, below, right, left, *outs):
    odd = table[8]
    edges = (above, below)
    for kind in range(2):
        for row, edge in enumerate(edges):
            for out, at in ((right, 6), (left, 0)):
                out[kind, row] = (terms[kind, row, at] + edge[kind, at].astype(WIDE)).astype(LOW)
    for turn in range(2):
        for part in range(2):
            at = first_of(1, odd) + part + 1
            for kind in range(2):
                outs[turn][kind, part] = rest[kind, turn, 2 + part]
                flip = (turn + odd) % 2 == 1
                edge = jnp.where(flip, below[kind, at], above[kind, at])
                value = terms[kind, (turn + odd) % 2, at] + edge.astype(WIDE)
                outs[turn][2 + kind, part] = value.astype(LOW)


def rims(table, rest, terms, edges):
    return pl.pallas_call(
        rims_kernel,
        out_shape=column_shapes() + pair_shapes(4, 2),
        in_specs=[pl.BlockSpec(memory_space=pltpu.SMEM)] + whole(4),
        out_specs=whole(4),
        compiler_params=pltpu.CompilerParams(vmem_limit_bytes=16 << 20),
        name="rims",
    )(table, rest, terms, *edges)


def combine_kernel(table, rest, terms, above, below, before, after, *outs):
    odd = table[8]
    flipped = odd == 1
    for turn in range(2):
        row = (turn + odd) % 2
        for kind in range(2):

            def summed(at):
                edge = jnp.where(row == 1, below[kind, at + 1], above[kind, at + 1])
                return terms[kind, row, at + 1] + edge.astype(WIDE)

            first = first_of(0, odd)
            left = before[kind, row].astype(WIDE)
            right = after[kind, row].astype(WIDE)
            one, two = summed(first), summed(first + 1)
            for part in range(2):
                outs[turn][kind, part] = rest[kind, turn, part]
            outs[turn][2 + kind, 0] = jnp.where(flipped, one, one + left).astype(LOW)
            outs[turn][2 + kind, 1] = jnp.where(flipped, two + right, two).astype(LOW)
            alone = summed(first_of(2, odd)) + jnp.where(flipped, left, right)
            outs[2 + turn][kind] = rest[kind, turn, 4]
            outs[2 + turn][2 + kind] = alone.astype(LOW)


def combine(table, rest, terms, edges, columns):
    return pl.pallas_call(
        combine_kernel,
        out_shape=pair_shapes(4, 2) + [jax.ShapeDtypeStruct((4, TILE, HEAD_DIM), LOW)] * 2,
        in_specs=[pl.BlockSpec(memory_space=pltpu.SMEM)] + whole(6),
        out_specs=whole(4),
        compiler_params=pltpu.CompilerParams(vmem_limit_bytes=16 << 20),
        name="combine",
    )(table, rest, terms, *edges, *columns)


def send_all(parts, routes):
    return [lax.ppermute(part, "tile", path) for part, path in zip(parts, routes)]


def local(query_slab, key_slab, value_slab, upstream):
    place = place_table()
    to_owner = [owner_of(which, turn) for which, turn in OWNER_STEPS]
    row_routes = [shifted(*step) for step in ROW_STEPS]
    column_routes = [shifted(*step) for step in COLUMN_STEPS]

    with jax.named_scope("upstream_to_units"):
        grads = send_all(spread(place, upstream), [flipped(path) for path in to_owner])

    with jax.named_scope("heads"):
        lines = [
            slab.reshape(8, 4, 40, 128).transpose(2, 0, 1, 3).reshape(8, 5, 32, 128)
            for slab in (query_slab, key_slab, value_slab)
        ]
        swapped = lax.all_to_all(jnp.stack(lines, axis=1), "head", 0, 0, tiled=True)
    with jax.named_scope("tiles"):
        dealt, early = lax.optimization_barrier((deal(swapped), grads[:EARLY]))
        got = lax.all_to_all(dealt, "tile", 0, 0, tiled=True)
        own = got.reshape(32, 19, 2, 4, 128).transpose(2, 1, 0, 3, 4)
        own = own.reshape(2, 19, TILE, HEAD_DIM)
        own, late = lax.optimization_barrier((own, grads[EARLY:]))
    with jax.named_scope("halos"):
        halos = send_all([own[1, 5:], own[0, 5:]], row_routes)
    with jax.named_scope("attention"):
        rest, terms, above, below = attend(place, own, halos, early + late)
    with jax.named_scope("row_terms"):
        edges = send_all([above, below], row_routes)
    with jax.named_scope("column_terms"):
        right, left, *free = rims(place, rest, terms, edges)
        columns = send_all([right, left], column_routes)
        free = send_all(free, to_owner[2:4])
    with jax.named_scope("outputs_home"):
        leaving = combine(place, rest, terms, edges, columns)
        leaving, free = lax.optimization_barrier((leaving, free))
        late = send_all(leaving, to_owner[:2] + to_owner[4:])
    with jax.named_scope("settle"):
        return tuple(gather(place, free + late))


def solution(mesh):
    slab = P("tile", None, "head", None)
    block = P("tile", "head")
    return jax.shard_map(
        local,
        mesh=mesh,
        in_specs=(slab, slab, slab, block),
        out_specs=(block, block, block, block),
        check_vma=False,
    )
```

```python
import functools
import math

import jax
import jax.numpy as jnp
import numpy as np
from jax import lax
from jax.experimental import pallas as pl
from jax.experimental.pallas import tpu as pltpu
from jax.sharding import PartitionSpec as P

HEAD_DIM = 128
HEADS_HERE = 5
STRIPS = 4
SLOTS = 8
TILE = 128
LOW = jnp.bfloat16
WIDE = jnp.float32
NEVER = -1e30


def route(step):
    pairs = []
    for strip in range(STRIPS):
        for slot in range(SLOTS):
            goal = step(strip, slot)
            if goal is not None:
                pairs.append((strip * SLOTS + slot, goal[0] * SLOTS + goal[1]))
    return pairs


def run_at(slot):
    return (5 - slot) % SLOTS


def shifted(rows, columns):
    def step(strip, slot):
        there = (strip + rows, run_at(slot) + columns)
        if 0 <= there[0] < STRIPS and 0 <= there[1] < SLOTS:
            return there[0], run_at(there[1])
        return None

    return route(step)


def first_of(which, odd):
    return (3 * odd, 2 - odd, 4 - 4 * odd)[which]


def owner_of(which, turn):
    def step(strip, slot):
        run = run_at(slot)
        odd = run % 2
        unit = 5 * run + first_of(which, odd)
        return (strip, ((turn + odd) % 2) * 4 + (unit % 8) // 2)

    return route(step)


def flipped(pairs):
    return [(target, source) for source, target in pairs]


ROW_STEPS = ((1, 0), (-1, 0))
COLUMN_STEPS = ((0, 1), (0, -1))
EARLY = 3
OWNER_STEPS = tuple((which, turn) for which in range(3) for turn in range(2))


def nt(one, two):
    return lax.dot_general(one, two, (((1,), (1,)), ((), ())), preferred_element_type=WIDE)


def nn(one, two):
    return jnp.dot(one, two, preferred_element_type=WIDE)


def whole(count):
    return [pl.BlockSpec(memory_space=pltpu.VMEM)] * count


def owner_rows():
    rows = []
    for slot in range(SLOTS):
        row, pair = slot // 4, slot % 4
        heads = []
        for which, turn in OWNER_STEPS:
            if which == 2:
                unit = 10 * ((pair + 2) % 4) + 4
            elif (row + turn) % 2:
                unit = 10 * ((pair - 3 * which) % 4) + 8 - 2 * which
            else:
                unit = 10 * ((pair - which) % 4) + 2 * which
            heads.append(unit // 8)
        rows.append(heads + [row])
    return rows


def place_table():
    owners = owner_rows()
    rows = [
        owners[slot]
        + [strip, run_at(slot) % 2]
        + [(5 * run_at(slot) + at) % 8 for at in range(5)]
        for strip in range(STRIPS)
        for slot in range(SLOTS)
    ]
    every = jnp.asarray(np.array(rows, np.int32))
    return lax.dynamic_index_in_dim(every, lax.axis_index("tile"), 0, keepdims=False)


def spread_kernel(table, upstream, *outs):
    line = lax.broadcasted_iota(jnp.int32, (2 * TILE, 2 * TILE), 0)
    col = lax.broadcasted_iota(jnp.int32, (2 * TILE, 2 * TILE), 1)
    source = ((line & 127) >> 2) * 8 + (line >> 7) * 4 + (line & 3)
    order = (col == source).astype(LOW)
    for at, (which, turn) in enumerate(OWNER_STEPS):
        head = pl.multiple_of(table[at] * HEAD_DIM, HEAD_DIM)
        tiles = jnp.dot(order, upstream[:, pl.ds(head, HEAD_DIM)], preferred_element_type=WIDE)
        tiles = tiles.astype(LOW)
        if which == 2:
            second = ((table[6] + turn) % 2) == 1
            outs[at][...] = jnp.where(second, tiles[TILE:], tiles[:TILE])
        else:
            outs[at][...] = tiles.reshape(2, TILE, HEAD_DIM)


def spread(table, upstream):
    shapes = [
        jax.ShapeDtypeStruct((TILE, HEAD_DIM) if which == 2 else (2, TILE, HEAD_DIM), LOW)
        for which, _ in OWNER_STEPS
    ]
    return pl.pallas_call(
        spread_kernel,
        out_shape=shapes,
        in_specs=[pl.BlockSpec(memory_space=pltpu.SMEM)] + whole(1),
        out_specs=whole(6),
        compiler_params=pltpu.CompilerParams(vmem_limit_bytes=16 << 20),
        name="spread",
    )(table, upstream)


def gather_kernel(table, *refs):
    free, late, singles = refs[:2], refs[2:4], refs[4:6]
    outs = refs[6:10]
    line = lax.broadcasted_iota(jnp.int32, (2 * TILE, 2 * TILE), 0)
    col = lax.broadcasted_iota(jnp.int32, (2 * TILE, 2 * TILE), 1)
    source = ((line >> 2) & 1) * TILE + (line >> 3) * 4 + (line & 3)
    order = (col == source).astype(LOW)
    flip = table[6] == 1

    def place(at, tiles):
        head = pl.multiple_of(table[at] * HEAD_DIM, HEAD_DIM)
        ordered = nn(order, jnp.concatenate(tiles, axis=1)).astype(LOW)
        for kind, out in enumerate(outs):
            out[:, pl.ds(head, HEAD_DIM)] = ordered[:, kind * HEAD_DIM : (kind + 1) * HEAD_DIM]

    for at in range(4):
        received = (late, free)[at // 2][at % 2]
        place(at, [received[kind].reshape(2 * TILE, HEAD_DIM) for kind in range(4)])
    one, two = singles[0][...], singles[1][...]
    tops, lows = jnp.where(flip, two, one), jnp.where(flip, one, two)
    place(4, [jnp.concatenate([tops[kind], lows[kind]], axis=0) for kind in range(4)])


def gather(table, received):
    return pl.pallas_call(
        gather_kernel,
        out_shape=[jax.ShapeDtypeStruct((2 * TILE, HEADS_HERE * HEAD_DIM), LOW)] * 4,
        in_specs=[pl.BlockSpec(memory_space=pltpu.SMEM)] + whole(6),
        out_specs=whole(4),
        compiler_params=pltpu.CompilerParams(vmem_limit_bytes=16 << 20),
        name="gather",
    )(table, *received)


def pack_kernel(query, key, value, out):
    for kind, slab in enumerate((query, key, value)):
        for group in range(8):
            for head in range(HEADS_HERE):
                at = (group * HEADS_HERE + head) * HEAD_DIM
                lines = slab[0, :, :, at : at + HEAD_DIM]
                out[group, kind, head] = lines.reshape(32, HEAD_DIM)


def pack(query, key, value):
    return pl.pallas_call(
        pack_kernel,
        out_shape=jax.ShapeDtypeStruct((8, 3, HEADS_HERE, 32, HEAD_DIM), LOW),
        in_specs=whole(3),
        out_specs=whole(1)[0],
        compiler_params=pltpu.CompilerParams(vmem_limit_bytes=16 << 20),
        name="pack",
    )(query, key, value)


def deal_kernel(swapped, out):
    for slot in range(SLOTS):
        for at in range(7):
            unit = min(max(5 * run_at(slot) + at - 1, 0), 39)
            head, column = unit // 8, unit % 8
            for kind in range(3):
                if kind == 0 and not 1 <= at <= 5:
                    continue
                place = at - 1 if kind == 0 else 7 * kind - 2 + at
                lines = swapped[column, kind, head].reshape(STRIPS, 8, HEAD_DIM)
                for strip in range(STRIPS):
                    out[strip * SLOTS + slot, place] = lines[strip]


def deal(swapped):
    return pl.pallas_call(
        deal_kernel,
        out_shape=jax.ShapeDtypeStruct((STRIPS * SLOTS, 19, 8, HEAD_DIM), LOW),
        in_specs=whole(1),
        out_specs=whole(1)[0],
        compiler_params=pltpu.CompilerParams(vmem_limit_bytes=16 << 20),
        name="deal",
    )(swapped)


def pair_shapes(kinds, count):
    return [jax.ShapeDtypeStruct((kinds, 2, TILE, HEAD_DIM), LOW)] * count


def attend_kernel(table, own, above, below, *refs):
    grads, rest, terms, edges = refs[:6], refs[6], refs[7], refs[8:10]
    pair, turned, outer_turned, grad, total, held = refs[10:]
    strip, odd = table[7], table[8]
    scaling = HEAD_DIM**-0.5
    rate = scaling * math.log2(math.e)

    for kind in range(2):
        for at in range(7):
            for row in range(2):
                pair[kind, at, row] = own[row, 5 + 7 * kind + at]
            pair[kind, at, 2] = above[7 * kind + at]
            pair[kind, at, 3] = below[7 * kind + at]
    for kind in range(2):
        for at in range(7):
            for row in range(2):
                lanes = pl.ds((2 * at + row) * TILE, TILE)
                turned[kind, :, lanes] = pair[kind, at, row].T
                outer_turned[kind, row, :, pl.ds(at * TILE, TILE)] = pair[kind, at, 2 + row].T
    for at, (which, turn) in enumerate(OWNER_STEPS):
        row = (turn + odd) % 2
        first = first_of(which, odd)
        if which == 2:
            grad[row, first] = grads[at][...]
        else:
            for part in range(2):
                grad[row, first + part] = grads[at][part]
    total[...] = jnp.zeros_like(total)

    def one_unit(unit, carry):
        column = table[9 + unit]
        queries = [own[row, unit] for row in range(2)]
        both = jnp.concatenate(queries, axis=0)
        ups = [grad[row, unit] for row in range(2)]
        up_both = jnp.concatenate(ups, axis=0)
        column_ok = (column > 0, None, column < 7)
        row_ok = (strip > 0, strip < STRIPS - 1)

        def products(kind, left, left_both):
            inner, outer = [], []
            for step in range(3):
                slot = unit + step
                near = pair[kind, slot, 0:2].reshape(2 * TILE, HEAD_DIM)
                inner.append(nt(near, left_both))
                outer.append(
                    jnp.concatenate(
                        [nt(pair[kind, slot, 2 + row], left[row]) for row in range(2)], axis=1
                    )
                )
            return inner, outer

        inner, outer = products(0, queries, both)
        lane = lax.broadcasted_iota(jnp.int32, (1, 2 * TILE), 1)
        row_bias = jnp.where(
            lane < TILE,
            jnp.where(row_ok[0], 0.0, NEVER),
            jnp.where(row_ok[1], 0.0, NEVER),
        )
        for step in range(3):
            if column_ok[step] is None:
                outer[step] = outer[step] + row_bias
            else:
                bias = jnp.where(column_ok[step], 0.0, NEVER)
                inner[step] = inner[step] + bias
                outer[step] = outer[step] + (row_bias + bias)
        highest = functools.reduce(
            jnp.maximum, [jnp.max(block, axis=0, keepdims=True) for block in inner + outer]
        )
        raised = [jnp.exp2((block - highest) * rate) for block in inner + outer]
        amount = sum(jnp.sum(block, axis=0, keepdims=True) for block in raised)
        inverse = 1.0 / amount
        weights = [block * inverse for block in raised]
        low = [block.astype(LOW) for block in weights]

        def mix(kind, parts):
            near = sum(
                nn(
                    turned[kind, :, pl.ds(pl.multiple_of((unit + step) * 256, 256), 256)],
                    parts[step],
                )
                for step in range(3)
            )
            far = [
                sum(
                    nn(
                        outer_turned[
                            kind, row, :, pl.ds(pl.multiple_of((unit + step) * TILE, TILE), TILE)
                        ],
                        parts[3 + step][:, row * TILE : (row + 1) * TILE],
                    )
                    for step in range(3)
                )
                for row in range(2)
            ]
            return near + jnp.concatenate(far, axis=1)

        def fold(kind, parts, right, right_both):
            for step in range(3):
                slot = unit + step
                near = nn(parts[step], right_both)
                for row in range(2):
                    total[kind, slot, row] += near[row * TILE : (row + 1) * TILE]
                    total[kind, slot, 2 + row] += nn(
                        parts[3 + step][:, row * TILE : (row + 1) * TILE], right[row]
                    )

        mixed = mix(1, low).T
        offsets = jnp.sum((up_both.astype(WIDE) * mixed).T, axis=0, keepdims=True)
        for row in range(2):
            held[0, row, unit] = mixed[row * TILE : (row + 1) * TILE].astype(LOW)
        fold(1, low, ups, up_both)
        inner, outer = products(1, ups, up_both)
        slopes = [
            (weight * (block - offsets)).astype(LOW)
            for weight, block in zip(weights, inner + outer)
        ]
        query_grad = mix(0, slopes).T * scaling
        for row in range(2):
            held[1, row, unit] = query_grad[row * TILE : (row + 1) * TILE].astype(LOW)
        fold(0, slopes, queries, both)
        return carry

    lax.fori_loop(0, 5, one_unit, 0, unroll=True)
    for kind in range(2):
        for turn in range(2):
            row = (turn + odd) % 2
            for part in range(2):
                rest[kind, turn, part] = held[kind, row, first_of(0, odd) + part]
                rest[kind, turn, 2 + part] = held[kind, row, first_of(1, odd) + part]
            rest[kind, turn, 4] = held[kind, row, first_of(2, odd)]
    for kind, factor in ((0, scaling), (1, 1.0)):
        for at in range(7):
            for row in range(2):
                terms[kind, row, at] = total[kind, at, row] * factor
                edges[row][kind, at] = (total[kind, at, 3 - row] * factor).astype(LOW)


def column_shapes():
    return [jax.ShapeDtypeStruct((2, 2, TILE, HEAD_DIM), LOW)] * 2


def attend(table, own, halos, grads):
    return pl.pallas_call(
        attend_kernel,
        out_shape=[
            jax.ShapeDtypeStruct((2, 2, 5, TILE, HEAD_DIM), LOW),
            jax.ShapeDtypeStruct((2, 2, 7, TILE, HEAD_DIM), WIDE),
            jax.ShapeDtypeStruct((2, 7, TILE, HEAD_DIM), LOW),
            jax.ShapeDtypeStruct((2, 7, TILE, HEAD_DIM), LOW),
        ],
        in_specs=[pl.BlockSpec(memory_space=pltpu.SMEM)] + whole(9),
        out_specs=whole(4),
        scratch_shapes=[
            pltpu.VMEM((2, 7, 4, TILE, HEAD_DIM), LOW),
            pltpu.VMEM((2, HEAD_DIM, 14 * TILE), LOW),
            pltpu.VMEM((2, 2, HEAD_DIM, 7 * TILE), LOW),
            pltpu.VMEM((2, 5, TILE, HEAD_DIM), LOW),
            pltpu.VMEM((2, 7, 4, TILE, HEAD_DIM), WIDE),
            pltpu.VMEM((2, 2, 5, TILE, HEAD_DIM), LOW),
        ],
        compiler_params=pltpu.CompilerParams(vmem_limit_bytes=40 << 20),
        cost_estimate=pl.CostEstimate(
            flops=3_000_000_000, bytes_accessed=8_000_000, transcendentals=1_500_000
        ),
        name="attend",
    )(table, own, *halos, *grads)


def rims_kernel(table, rest, terms, above, below, right, left, *outs):
    odd = table[8]
    edges = (above, below)
    for kind in range(2):
        for row, edge in enumerate(edges):
            for out, at in ((right, 6), (left, 0)):
                out[kind, row] = (terms[kind, row, at] + edge[kind, at].astype(WIDE)).astype(LOW)
    for turn in range(2):
        for part in range(2):
            at = first_of(1, odd) + part + 1
            for kind in range(2):
                outs[turn][kind, part] = rest[kind, turn, 2 + part]
                flip = (turn + odd) % 2 == 1
                edge = jnp.where(flip, below[kind, at], above[kind, at])
                value = terms[kind, (turn + odd) % 2, at] + edge.astype(WIDE)
                outs[turn][2 + kind, part] = value.astype(LOW)


def rims(table, rest, terms, edges):
    return pl.pallas_call(
        rims_kernel,
        out_shape=column_shapes() + pair_shapes(4, 2),
        in_specs=[pl.BlockSpec(memory_space=pltpu.SMEM)] + whole(4),
        out_specs=whole(4),
        compiler_params=pltpu.CompilerParams(vmem_limit_bytes=16 << 20),
        name="rims",
    )(table, rest, terms, *edges)


def combine_kernel(table, rest, terms, above, below, before, after, *outs):
    odd = table[8]
    flipped = odd == 1
    for turn in range(2):
        row = (turn + odd) % 2
        for kind in range(2):

            def summed(at):
                edge = jnp.where(row == 1, below[kind, at + 1], above[kind, at + 1])
                return terms[kind, row, at + 1] + edge.astype(WIDE)

            first = first_of(0, odd)
            left = before[kind, row].astype(WIDE)
            right = after[kind, row].astype(WIDE)
            one, two = summed(first), summed(first + 1)
            for part in range(2):
                outs[turn][kind, part] = rest[kind, turn, part]
            outs[turn][2 + kind, 0] = jnp.where(flipped, one, one + left).astype(LOW)
            outs[turn][2 + kind, 1] = jnp.where(flipped, two + right, two).astype(LOW)
            alone = summed(first_of(2, odd)) + jnp.where(flipped, left, right)
            outs[2 + turn][kind] = rest[kind, turn, 4]
            outs[2 + turn][2 + kind] = alone.astype(LOW)


def combine(table, rest, terms, edges, columns):
    return pl.pallas_call(
        combine_kernel,
        out_shape=pair_shapes(4, 2) + [jax.ShapeDtypeStruct((4, TILE, HEAD_DIM), LOW)] * 2,
        in_specs=[pl.BlockSpec(memory_space=pltpu.SMEM)] + whole(6),
        out_specs=whole(4),
        compiler_params=pltpu.CompilerParams(vmem_limit_bytes=16 << 20),
        name="combine",
    )(table, rest, terms, *edges, *columns)


def send_all(parts, routes):
    return [lax.ppermute(part, "tile", path) for part, path in zip(parts, routes)]


def local(query_slab, key_slab, value_slab, upstream):
    place = place_table()
    to_owner = [owner_of(which, turn) for which, turn in OWNER_STEPS]
    row_routes = [shifted(*step) for step in ROW_STEPS]
    column_routes = [shifted(*step) for step in COLUMN_STEPS]

    with jax.named_scope("upstream_to_units"):
        grads = send_all(spread(place, upstream), [flipped(path) for path in to_owner])

    with jax.named_scope("heads"):
        lines = pack(query_slab, key_slab, value_slab)
        swapped = lax.all_to_all(lines, "head", 0, 0, tiled=True)
    with jax.named_scope("tiles"):
        dealt, early = lax.optimization_barrier((deal(swapped), grads[:EARLY]))
        got = lax.all_to_all(dealt, "tile", 0, 0, tiled=True)
        own = got.reshape(32, 19, 2, 4, 128).transpose(2, 1, 0, 3, 4)
        own = own.reshape(2, 19, TILE, HEAD_DIM)
        own, late = lax.optimization_barrier((own, grads[EARLY:]))
    with jax.named_scope("halos"):
        halos = send_all([own[1, 5:], own[0, 5:]], row_routes)
    with jax.named_scope("attention"):
        rest, terms, above, below = attend(place, own, halos, early + late)
    with jax.named_scope("row_terms"):
        edges = send_all([above, below], row_routes)
    with jax.named_scope("column_terms"):
        right, left, *free = rims(place, rest, terms, edges)
        columns = send_all([right, left], column_routes)
        free = send_all(free, to_owner[2:4])
    with jax.named_scope("outputs_home"):
        leaving = combine(place, rest, terms, edges, columns)
        leaving, free = lax.optimization_barrier((leaving, free))
        late = send_all(leaving, to_owner[:2] + to_owner[4:])
    with jax.named_scope("settle"):
        return tuple(gather(place, free + late))


def solution(mesh):
    slab = P("tile", None, "head", None)
    block = P("tile", "head")
    return jax.shard_map(
        local,
        mesh=mesh,
        in_specs=(slab, slab, slab, block),
        out_specs=(block, block, block, block),
        check_vma=False,
    )
```

```python
import functools
import math

import jax
import jax.numpy as jnp
import numpy as np
from jax import lax
from jax.experimental import pallas as pl
from jax.experimental.pallas import tpu as pltpu
from jax.sharding import PartitionSpec as P

HEAD_DIM = 128
HEADS_HERE = 5
STRIPS = 4
SLOTS = 8
TILE = 128
LOW = jnp.bfloat16
WIDE = jnp.float32
NEVER = -1e30


def route(step):
    pairs = []
    for strip in range(STRIPS):
        for slot in range(SLOTS):
            goal = step(strip, slot)
            if goal is not None:
                pairs.append((strip * SLOTS + slot, goal[0] * SLOTS + goal[1]))
    return pairs


def run_at(slot):
    return (5 - slot) % SLOTS


def shifted(rows, columns):
    def step(strip, slot):
        there = (strip + rows, run_at(slot) + columns)
        if 0 <= there[0] < STRIPS and 0 <= there[1] < SLOTS:
            return there[0], run_at(there[1])
        return None

    return route(step)


def first_of(which, odd):
    return (3 * odd, 2 - odd, 4 - 4 * odd)[which]


def owner_of(which, turn):
    def step(strip, slot):
        run = run_at(slot)
        odd = run % 2
        unit = 5 * run + first_of(which, odd)
        return (strip, ((turn + odd) % 2) * 4 + (unit % 8) // 2)

    return route(step)


def flipped(pairs):
    return [(target, source) for source, target in pairs]


ROW_STEPS = ((1, 0), (-1, 0))
COLUMN_STEPS = ((0, 1), (0, -1))
EARLY = 3
OWNER_STEPS = tuple((which, turn) for which in range(3) for turn in range(2))


def nt(one, two):
    return lax.dot_general(one, two, (((1,), (1,)), ((), ())), preferred_element_type=WIDE)


def nn(one, two):
    return jnp.dot(one, two, preferred_element_type=WIDE)


def whole(count):
    return [pl.BlockSpec(memory_space=pltpu.VMEM)] * count


def owner_rows():
    rows = []
    for slot in range(SLOTS):
        row, pair = slot // 4, slot % 4
        heads = []
        for which, turn in OWNER_STEPS:
            if which == 2:
                unit = 10 * ((pair + 2) % 4) + 4
            elif (row + turn) % 2:
                unit = 10 * ((pair - 3 * which) % 4) + 8 - 2 * which
            else:
                unit = 10 * ((pair - which) % 4) + 2 * which
            heads.append(unit // 8)
        rows.append(heads + [row])
    return rows


def place_table():
    owners = owner_rows()
    rows = [
        owners[slot]
        + [strip, run_at(slot) % 2]
        + [(5 * run_at(slot) + at) % 8 for at in range(5)]
        for strip in range(STRIPS)
        for slot in range(SLOTS)
    ]
    every = jnp.asarray(np.array(rows, np.int32))
    return lax.dynamic_index_in_dim(every, lax.axis_index("tile"), 0, keepdims=False)


def spread_kernel(table, upstream, *outs):
    line = lax.broadcasted_iota(jnp.int32, (2 * TILE, 2 * TILE), 0)
    col = lax.broadcasted_iota(jnp.int32, (2 * TILE, 2 * TILE), 1)
    source = ((line & 127) >> 2) * 8 + (line >> 7) * 4 + (line & 3)
    order = (col == source).astype(LOW)
    for at, (which, turn) in enumerate(OWNER_STEPS):
        head = pl.multiple_of(table[at] * HEAD_DIM, HEAD_DIM)
        tiles = jnp.dot(order, upstream[:, pl.ds(head, HEAD_DIM)], preferred_element_type=WIDE)
        tiles = tiles.astype(LOW)
        if which == 2:
            second = ((table[6] + turn) % 2) == 1
            outs[at][...] = jnp.where(second, tiles[TILE:], tiles[:TILE])
        else:
            outs[at][...] = tiles.reshape(2, TILE, HEAD_DIM)


def spread(table, upstream):
    shapes = [
        jax.ShapeDtypeStruct((TILE, HEAD_DIM) if which == 2 else (2, TILE, HEAD_DIM), LOW)
        for which, _ in OWNER_STEPS
    ]
    return pl.pallas_call(
        spread_kernel,
        out_shape=shapes,
        in_specs=[pl.BlockSpec(memory_space=pltpu.SMEM)] + whole(1),
        out_specs=whole(6),
        compiler_params=pltpu.CompilerParams(vmem_limit_bytes=16 << 20),
        name="spread",
    )(table, upstream)


def gather_kernel(table, *refs):
    free, late, singles = refs[:2], refs[2:4], refs[4:6]
    outs = refs[6:10]
    line = lax.broadcasted_iota(jnp.int32, (2 * TILE, 2 * TILE), 0)
    col = lax.broadcasted_iota(jnp.int32, (2 * TILE, 2 * TILE), 1)
    source = ((line >> 2) & 1) * TILE + (line >> 3) * 4 + (line & 3)
    order = (col == source).astype(LOW)
    flip = table[6] == 1

    def place(at, tiles):
        head = pl.multiple_of(table[at] * HEAD_DIM, HEAD_DIM)
        ordered = nn(order, jnp.concatenate(tiles, axis=1)).astype(LOW)
        for kind, out in enumerate(outs):
            out[:, pl.ds(head, HEAD_DIM)] = ordered[:, kind * HEAD_DIM : (kind + 1) * HEAD_DIM]

    for at in range(4):
        received = (late, free)[at // 2][at % 2]
        place(at, [received[kind].reshape(2 * TILE, HEAD_DIM) for kind in range(4)])
    one, two = singles[0][...], singles[1][...]
    tops, lows = jnp.where(flip, two, one), jnp.where(flip, one, two)
    place(4, [jnp.concatenate([tops[kind], lows[kind]], axis=0) for kind in range(4)])


def gather(table, received):
    return pl.pallas_call(
        gather_kernel,
        out_shape=[jax.ShapeDtypeStruct((2 * TILE, HEADS_HERE * HEAD_DIM), LOW)] * 4,
        in_specs=[pl.BlockSpec(memory_space=pltpu.SMEM)] + whole(6),
        out_specs=whole(4),
        compiler_params=pltpu.CompilerParams(vmem_limit_bytes=16 << 20),
        name="gather",
    )(table, *received)


def deal_kernel(kinds, halo, swapped, out):
    count = 5 + 2 * halo
    for slot in range(SLOTS):
        for at in range(count):
            unit = min(max(5 * run_at(slot) + at - halo, 0), 39)
            head, column = unit // 8, unit % 8
            for place, kind in enumerate(kinds):
                lines = swapped[column, kind, head].reshape(STRIPS, 8, HEAD_DIM)
                for strip in range(STRIPS):
                    out[strip * SLOTS + slot, place * count + at] = lines[strip]


def deal(swapped, kinds, halo):
    tiles = len(kinds) * (5 + 2 * halo)
    return pl.pallas_call(
        functools.partial(deal_kernel, kinds, halo),
        out_shape=jax.ShapeDtypeStruct((STRIPS * SLOTS, tiles, 8, HEAD_DIM), LOW),
        in_specs=whole(1),
        out_specs=whole(1)[0],
        compiler_params=pltpu.CompilerParams(vmem_limit_bytes=16 << 20),
        name="deal",
    )(swapped)


def pair_shapes(kinds, count):
    return [jax.ShapeDtypeStruct((kinds, 2, TILE, HEAD_DIM), LOW)] * count


def attend_kernel(table, own, beside, above, below, *refs):
    grads, rest, terms, edges = refs[:6], refs[6], refs[7], refs[8:10]
    pair, turned, outer_turned, grad, total, held = refs[10:]
    strip, odd = table[7], table[8]
    scaling = HEAD_DIM**-0.5
    rate = scaling * math.log2(math.e)

    for kind in range(2):
        for at in range(7):
            for row in range(2):
                pair[kind, at, row] = beside[row, 7 * kind + at]
            pair[kind, at, 2] = above[7 * kind + at]
            pair[kind, at, 3] = below[7 * kind + at]
    for kind in range(2):
        for at in range(7):
            for row in range(2):
                lanes = pl.ds((2 * at + row) * TILE, TILE)
                turned[kind, :, lanes] = pair[kind, at, row].T
                outer_turned[kind, row, :, pl.ds(at * TILE, TILE)] = pair[kind, at, 2 + row].T
    for at, (which, turn) in enumerate(OWNER_STEPS):
        row = (turn + odd) % 2
        first = first_of(which, odd)
        if which == 2:
            grad[row, first] = grads[at][...]
        else:
            for part in range(2):
                grad[row, first + part] = grads[at][part]
    total[...] = jnp.zeros_like(total)

    def one_unit(unit, carry):
        column = table[9 + unit]
        queries = [own[row, unit] for row in range(2)]
        both = jnp.concatenate(queries, axis=0)
        ups = [grad[row, unit] for row in range(2)]
        up_both = jnp.concatenate(ups, axis=0)
        column_ok = (column > 0, None, column < 7)
        row_ok = (strip > 0, strip < STRIPS - 1)

        def products(kind, left, left_both):
            inner, outer = [], []
            for step in range(3):
                slot = unit + step
                near = pair[kind, slot, 0:2].reshape(2 * TILE, HEAD_DIM)
                inner.append(nt(near, left_both))
                outer.append(
                    jnp.concatenate(
                        [nt(pair[kind, slot, 2 + row], left[row]) for row in range(2)], axis=1
                    )
                )
            return inner, outer

        inner, outer = products(0, queries, both)
        lane = lax.broadcasted_iota(jnp.int32, (1, 2 * TILE), 1)
        row_bias = jnp.where(
            lane < TILE,
            jnp.where(row_ok[0], 0.0, NEVER),
            jnp.where(row_ok[1], 0.0, NEVER),
        )
        for step in range(3):
            if column_ok[step] is None:
                outer[step] = outer[step] + row_bias
            else:
                bias = jnp.where(column_ok[step], 0.0, NEVER)
                inner[step] = inner[step] + bias
                outer[step] = outer[step] + (row_bias + bias)
        highest = functools.reduce(
            jnp.maximum, [jnp.max(block, axis=0, keepdims=True) for block in inner + outer]
        )
        raised = [jnp.exp2((block - highest) * rate) for block in inner + outer]
        amount = sum(jnp.sum(block, axis=0, keepdims=True) for block in raised)
        inverse = 1.0 / amount
        weights = [block * inverse for block in raised]
        low = [block.astype(LOW) for block in weights]

        def mix(kind, parts):
            near = sum(
                nn(
                    turned[kind, :, pl.ds(pl.multiple_of((unit + step) * 256, 256), 256)],
                    parts[step],
                )
                for step in range(3)
            )
            far = [
                sum(
                    nn(
                        outer_turned[
                            kind, row, :, pl.ds(pl.multiple_of((unit + step) * TILE, TILE), TILE)
                        ],
                        parts[3 + step][:, row * TILE : (row + 1) * TILE],
                    )
                    for step in range(3)
                )
                for row in range(2)
            ]
            return near + jnp.concatenate(far, axis=1)

        def fold(kind, parts, right, right_both):
            for step in range(3):
                slot = unit + step
                near = nn(parts[step], right_both)
                for row in range(2):
                    total[kind, slot, row] += near[row * TILE : (row + 1) * TILE]
                    total[kind, slot, 2 + row] += nn(
                        parts[3 + step][:, row * TILE : (row + 1) * TILE], right[row]
                    )

        mixed = mix(1, low).T
        offsets = jnp.sum((up_both.astype(WIDE) * mixed).T, axis=0, keepdims=True)
        for row in range(2):
            held[0, row, unit] = mixed[row * TILE : (row + 1) * TILE].astype(LOW)
        fold(1, low, ups, up_both)
        inner, outer = products(1, ups, up_both)
        slopes = [
            (weight * (block - offsets)).astype(LOW)
            for weight, block in zip(weights, inner + outer)
        ]
        query_grad = mix(0, slopes).T * scaling
        for row in range(2):
            held[1, row, unit] = query_grad[row * TILE : (row + 1) * TILE].astype(LOW)
        fold(0, slopes, queries, both)
        return carry

    lax.fori_loop(0, 5, one_unit, 0, unroll=True)
    for kind in range(2):
        for turn in range(2):
            row = (turn + odd) % 2
            for part in range(2):
                rest[kind, turn, part] = held[kind, row, first_of(0, odd) + part]
                rest[kind, turn, 2 + part] = held[kind, row, first_of(1, odd) + part]
            rest[kind, turn, 4] = held[kind, row, first_of(2, odd)]
    for kind, factor in ((0, scaling), (1, 1.0)):
        for at in range(7):
            for row in range(2):
                terms[kind, row, at] = total[kind, at, row] * factor
                edges[row][kind, at] = (total[kind, at, 3 - row] * factor).astype(LOW)


def column_shapes():
    return [jax.ShapeDtypeStruct((2, 2, TILE, HEAD_DIM), LOW)] * 2


def attend(table, own, pair, halos, grads):
    return pl.pallas_call(
        attend_kernel,
        out_shape=[
            jax.ShapeDtypeStruct((2, 2, 5, TILE, HEAD_DIM), LOW),
            jax.ShapeDtypeStruct((2, 2, 7, TILE, HEAD_DIM), WIDE),
            jax.ShapeDtypeStruct((2, 7, TILE, HEAD_DIM), LOW),
            jax.ShapeDtypeStruct((2, 7, TILE, HEAD_DIM), LOW),
        ],
        in_specs=[pl.BlockSpec(memory_space=pltpu.SMEM)] + whole(10),
        out_specs=whole(4),
        scratch_shapes=[
            pltpu.VMEM((2, 7, 4, TILE, HEAD_DIM), LOW),
            pltpu.VMEM((2, HEAD_DIM, 14 * TILE), LOW),
            pltpu.VMEM((2, 2, HEAD_DIM, 7 * TILE), LOW),
            pltpu.VMEM((2, 5, TILE, HEAD_DIM), LOW),
            pltpu.VMEM((2, 7, 4, TILE, HEAD_DIM), WIDE),
            pltpu.VMEM((2, 2, 5, TILE, HEAD_DIM), LOW),
        ],
        compiler_params=pltpu.CompilerParams(vmem_limit_bytes=40 << 20),
        cost_estimate=pl.CostEstimate(
            flops=3_000_000_000, bytes_accessed=8_000_000, transcendentals=1_500_000
        ),
        name="attend",
    )(table, own, pair, *halos, *grads)


def rims_kernel(table, rest, terms, above, below, right, left, *outs):
    odd = table[8]
    edges = (above, below)
    for kind in range(2):
        for row, edge in enumerate(edges):
            for out, at in ((right, 6), (left, 0)):
                out[kind, row] = (terms[kind, row, at] + edge[kind, at].astype(WIDE)).astype(LOW)
    for turn in range(2):
        for part in range(2):
            at = first_of(1, odd) + part + 1
            for kind in range(2):
                outs[turn][kind, part] = rest[kind, turn, 2 + part]
                flip = (turn + odd) % 2 == 1
                edge = jnp.where(flip, below[kind, at], above[kind, at])
                value = terms[kind, (turn + odd) % 2, at] + edge.astype(WIDE)
                outs[turn][2 + kind, part] = value.astype(LOW)


def rims(table, rest, terms, edges):
    return pl.pallas_call(
        rims_kernel,
        out_shape=column_shapes() + pair_shapes(4, 2),
        in_specs=[pl.BlockSpec(memory_space=pltpu.SMEM)] + whole(4),
        out_specs=whole(4),
        compiler_params=pltpu.CompilerParams(vmem_limit_bytes=16 << 20),
        name="rims",
    )(table, rest, terms, *edges)


def combine_kernel(table, rest, terms, above, below, before, after, *outs):
    odd = table[8]
    flipped = odd == 1
    for turn in range(2):
        row = (turn + odd) % 2
        for kind in range(2):

            def summed(at):
                edge = jnp.where(row == 1, below[kind, at + 1], above[kind, at + 1])
                return terms[kind, row, at + 1] + edge.astype(WIDE)

            first = first_of(0, odd)
            left = before[kind, row].astype(WIDE)
            right = after[kind, row].astype(WIDE)
            one, two = summed(first), summed(first + 1)
            for part in range(2):
                outs[turn][kind, part] = rest[kind, turn, part]
            outs[turn][2 + kind, 0] = jnp.where(flipped, one, one + left).astype(LOW)
            outs[turn][2 + kind, 1] = jnp.where(flipped, two + right, two).astype(LOW)
            alone = summed(first_of(2, odd)) + jnp.where(flipped, left, right)
            outs[2 + turn][kind] = rest[kind, turn, 4]
            outs[2 + turn][2 + kind] = alone.astype(LOW)


def combine(table, rest, terms, edges, columns):
    return pl.pallas_call(
        combine_kernel,
        out_shape=pair_shapes(4, 2) + [jax.ShapeDtypeStruct((4, TILE, HEAD_DIM), LOW)] * 2,
        in_specs=[pl.BlockSpec(memory_space=pltpu.SMEM)] + whole(6),
        out_specs=whole(4),
        compiler_params=pltpu.CompilerParams(vmem_limit_bytes=16 << 20),
        name="combine",
    )(table, rest, terms, *edges, *columns)


def send_all(parts, routes):
    return [lax.ppermute(part, "tile", path) for part, path in zip(parts, routes)]


def local(query_slab, key_slab, value_slab, upstream):
    place = place_table()
    to_owner = [owner_of(which, turn) for which, turn in OWNER_STEPS]
    row_routes = [shifted(*step) for step in ROW_STEPS]
    column_routes = [shifted(*step) for step in COLUMN_STEPS]

    with jax.named_scope("upstream_to_units"):
        grads = send_all(spread(place, upstream), [flipped(path) for path in to_owner])

    with jax.named_scope("heads"):
        lines = [
            slab.reshape(8, 4, 40, 128).transpose(2, 0, 1, 3).reshape(8, 5, 32, 128)
            for slab in (query_slab, key_slab, value_slab)
        ]
        swapped = lax.all_to_all(jnp.stack(lines, axis=1), "head", 0, 0, tiled=True)

    def by_tile(dealt):
        got = lax.all_to_all(dealt, "tile", 0, 0, tiled=True)
        tiles = got.reshape(32, -1, 2, 4, 128).transpose(2, 1, 0, 3, 4)
        return tiles.reshape(2, -1, TILE, HEAD_DIM)

    with jax.named_scope("key_value_tiles"):
        dealt, early = lax.optimization_barrier((deal(swapped, (1, 2), 1), grads[:EARLY]))
        pair = by_tile(dealt)
    with jax.named_scope("query_tiles"):
        pair, late, dealt = lax.optimization_barrier(
            (pair, grads[EARLY:], deal(swapped, (0,), 0))
        )
        own = by_tile(dealt)
    with jax.named_scope("halos"):
        halos = send_all([pair[1], pair[0]], row_routes)
    with jax.named_scope("attention"):
        rest, terms, above, below = attend(place, own, pair, halos, early + late)
    with jax.named_scope("row_terms"):
        edges = send_all([above, below], row_routes)
    with jax.named_scope("column_terms"):
        right, left, *free = rims(place, rest, terms, edges)
        columns = send_all([right, left], column_routes)
        free = send_all(free, to_owner[2:4])
    with jax.named_scope("outputs_home"):
        leaving = combine(place, rest, terms, edges, columns)
        leaving, free = lax.optimization_barrier((leaving, free))
        late = send_all(leaving, to_owner[:2] + to_owner[4:])
    with jax.named_scope("settle"):
        return tuple(gather(place, free + late))


def solution(mesh):
    slab = P("tile", None, "head", None)
    block = P("tile", "head")
    return jax.shard_map(
        local,
        mesh=mesh,
        in_specs=(slab, slab, slab, block),
        out_specs=(block, block, block, block),
        check_vma=False,
    )
```

```python
import functools
import math

import jax
import jax.numpy as jnp
import numpy as np
from jax import lax
from jax.experimental import pallas as pl
from jax.experimental.pallas import tpu as pltpu
from jax.sharding import PartitionSpec as P

HEAD_DIM = 128
HEADS_HERE = 5
STRIPS = 4
SLOTS = 8
TILE = 128
LOW = jnp.bfloat16
WIDE = jnp.float32
NEVER = -1e30


def route(step):
    pairs = []
    for strip in range(STRIPS):
        for slot in range(SLOTS):
            goal = step(strip, slot)
            if goal is not None:
                pairs.append((strip * SLOTS + slot, goal[0] * SLOTS + goal[1]))
    return pairs


def run_at(slot):
    return (5 - slot) % SLOTS


def shifted(rows, columns):
    def step(strip, slot):
        there = (strip + rows, run_at(slot) + columns)
        if 0 <= there[0] < STRIPS and 0 <= there[1] < SLOTS:
            return there[0], run_at(there[1])
        return None

    return route(step)


def first_of(which, odd):
    return (3 * odd, 2 - odd, 4 - 4 * odd)[which]


def owner_of(which, turn):
    def step(strip, slot):
        run = run_at(slot)
        odd = run % 2
        unit = 5 * run + first_of(which, odd)
        return (strip, ((turn + odd) % 2) * 4 + (unit % 8) // 2)

    return route(step)


def flipped(pairs):
    return [(target, source) for source, target in pairs]


ROW_STEPS = ((1, 0), (-1, 0))
COLUMN_STEPS = ((0, 1), (0, -1))
EARLY = 3
OWNER_STEPS = tuple((which, turn) for which in range(3) for turn in range(2))


def nt(one, two):
    return lax.dot_general(one, two, (((1,), (1,)), ((), ())), preferred_element_type=WIDE)


def nn(one, two):
    return jnp.dot(one, two, preferred_element_type=WIDE)


def whole(count):
    return [pl.BlockSpec(memory_space=pltpu.VMEM)] * count


def owner_rows():
    rows = []
    for slot in range(SLOTS):
        row, pair = slot // 4, slot % 4
        heads = []
        for which, turn in OWNER_STEPS:
            if which == 2:
                unit = 10 * ((pair + 2) % 4) + 4
            elif (row + turn) % 2:
                unit = 10 * ((pair - 3 * which) % 4) + 8 - 2 * which
            else:
                unit = 10 * ((pair - which) % 4) + 2 * which
            heads.append(unit // 8)
        rows.append(heads + [row])
    return rows


def place_table():
    owners = owner_rows()
    rows = [
        owners[slot]
        + [strip, run_at(slot) % 2]
        + [(5 * run_at(slot) + at) % 8 for at in range(5)]
        for strip in range(STRIPS)
        for slot in range(SLOTS)
    ]
    every = jnp.asarray(np.array(rows, np.int32))
    return lax.dynamic_index_in_dim(every, lax.axis_index("tile"), 0, keepdims=False)


def spread_kernel(table, upstream, *outs):
    line = lax.broadcasted_iota(jnp.int32, (2 * TILE, 2 * TILE), 0)
    col = lax.broadcasted_iota(jnp.int32, (2 * TILE, 2 * TILE), 1)
    source = ((line & 127) >> 2) * 8 + (line >> 7) * 4 + (line & 3)
    order = (col == source).astype(LOW)
    for at, (which, turn) in enumerate(OWNER_STEPS):
        head = pl.multiple_of(table[at] * HEAD_DIM, HEAD_DIM)
        tiles = jnp.dot(order, upstream[:, pl.ds(head, HEAD_DIM)], preferred_element_type=WIDE)
        tiles = tiles.astype(LOW)
        if which == 2:
            second = ((table[6] + turn) % 2) == 1
            outs[at][...] = jnp.where(second, tiles[TILE:], tiles[:TILE])
        else:
            outs[at][...] = tiles.reshape(2, TILE, HEAD_DIM)


def spread(table, upstream):
    shapes = [
        jax.ShapeDtypeStruct((TILE, HEAD_DIM) if which == 2 else (2, TILE, HEAD_DIM), LOW)
        for which, _ in OWNER_STEPS
    ]
    return pl.pallas_call(
        spread_kernel,
        out_shape=shapes,
        in_specs=[pl.BlockSpec(memory_space=pltpu.SMEM)] + whole(1),
        out_specs=whole(6),
        compiler_params=pltpu.CompilerParams(vmem_limit_bytes=16 << 20),
        name="spread",
    )(table, upstream)


def gather_kernel(table, *refs):
    firsts, seconds, singles, outs = refs[:4], refs[4:8], refs[8:10], refs[10:14]
    line = lax.broadcasted_iota(jnp.int32, (2 * TILE, 2 * TILE), 0)
    col = lax.broadcasted_iota(jnp.int32, (2 * TILE, 2 * TILE), 1)
    source = ((line >> 2) & 1) * TILE + (line >> 3) * 4 + (line & 3)
    order = (col == source).astype(LOW)
    flip = table[6] == 1

    def place(at, tiles):
        head = pl.multiple_of(table[at] * HEAD_DIM, HEAD_DIM)
        ordered = nn(order, jnp.concatenate(tiles, axis=1)).astype(LOW)
        for kind, out in enumerate(outs):
            out[:, pl.ds(head, HEAD_DIM)] = ordered[:, kind * HEAD_DIM : (kind + 1) * HEAD_DIM]

    for at in range(4):
        place(
            at,
            [
                (firsts, seconds)[kind // 2][at][kind % 2].reshape(2 * TILE, HEAD_DIM)
                for kind in range(4)
            ],
        )
    one, two = singles[0][...], singles[1][...]
    tops, lows = jnp.where(flip, two, one), jnp.where(flip, one, two)
    place(4, [jnp.concatenate([tops[kind], lows[kind]], axis=0) for kind in range(4)])


def gather(table, received):
    return pl.pallas_call(
        gather_kernel,
        out_shape=[jax.ShapeDtypeStruct((2 * TILE, HEADS_HERE * HEAD_DIM), LOW)] * 4,
        in_specs=[pl.BlockSpec(memory_space=pltpu.SMEM)] + whole(10),
        out_specs=whole(4),
        compiler_params=pltpu.CompilerParams(vmem_limit_bytes=16 << 20),
        name="gather",
    )(table, *received)


def deal_kernel(swapped, out):
    for slot in range(SLOTS):
        for at in range(7):
            unit = min(max(5 * run_at(slot) + at - 1, 0), 39)
            head, column = unit // 8, unit % 8
            for kind in range(3):
                if kind == 0 and not 1 <= at <= 5:
                    continue
                place = at - 1 if kind == 0 else 7 * kind - 2 + at
                lines = swapped[column, kind, head].reshape(STRIPS, 8, HEAD_DIM)
                for strip in range(STRIPS):
                    out[strip * SLOTS + slot, place] = lines[strip]


def deal(swapped):
    return pl.pallas_call(
        deal_kernel,
        out_shape=jax.ShapeDtypeStruct((STRIPS * SLOTS, 19, 8, HEAD_DIM), LOW),
        in_specs=whole(1),
        out_specs=whole(1)[0],
        compiler_params=pltpu.CompilerParams(vmem_limit_bytes=16 << 20),
        name="deal",
    )(swapped)


def pair_shapes(kinds, count):
    return [jax.ShapeDtypeStruct((kinds, 2, TILE, HEAD_DIM), LOW)] * count


def attend_kernel(table, own, above, below, *refs):
    grads, firsts, rest, terms, edges = refs[:6], refs[6:10], refs[10], refs[11], refs[12:14]
    pair, turned, outer_turned, grad, total, held = refs[14:]
    strip, odd = table[7], table[8]
    scaling = HEAD_DIM**-0.5
    rate = scaling * math.log2(math.e)

    for kind in range(2):
        for at in range(7):
            for row in range(2):
                pair[kind, at, row] = own[row, 5 + 7 * kind + at]
            pair[kind, at, 2] = above[7 * kind + at]
            pair[kind, at, 3] = below[7 * kind + at]
    for kind in range(2):
        for at in range(7):
            for row in range(2):
                lanes = pl.ds((2 * at + row) * TILE, TILE)
                turned[kind, :, lanes] = pair[kind, at, row].T
                outer_turned[kind, row, :, pl.ds(at * TILE, TILE)] = pair[kind, at, 2 + row].T
    for at, (which, turn) in enumerate(OWNER_STEPS):
        row = (turn + odd) % 2
        first = first_of(which, odd)
        if which == 2:
            grad[row, first] = grads[at][...]
        else:
            for part in range(2):
                grad[row, first + part] = grads[at][part]
    total[...] = jnp.zeros_like(total)

    def one_unit(unit, carry):
        column = table[9 + unit]
        queries = [own[row, unit] for row in range(2)]
        both = jnp.concatenate(queries, axis=0)
        ups = [grad[row, unit] for row in range(2)]
        up_both = jnp.concatenate(ups, axis=0)
        column_ok = (column > 0, None, column < 7)
        row_ok = (strip > 0, strip < STRIPS - 1)

        def products(kind, left, left_both):
            inner, outer = [], []
            for step in range(3):
                slot = unit + step
                near = pair[kind, slot, 0:2].reshape(2 * TILE, HEAD_DIM)
                inner.append(nt(near, left_both))
                outer.append(
                    jnp.concatenate(
                        [nt(pair[kind, slot, 2 + row], left[row]) for row in range(2)], axis=1
                    )
                )
            return inner, outer

        inner, outer = products(0, queries, both)
        lane = lax.broadcasted_iota(jnp.int32, (1, 2 * TILE), 1)
        row_bias = jnp.where(
            lane < TILE,
            jnp.where(row_ok[0], 0.0, NEVER),
            jnp.where(row_ok[1], 0.0, NEVER),
        )
        for step in range(3):
            if column_ok[step] is None:
                outer[step] = outer[step] + row_bias
            else:
                bias = jnp.where(column_ok[step], 0.0, NEVER)
                inner[step] = inner[step] + bias
                outer[step] = outer[step] + (row_bias + bias)
        highest = functools.reduce(
            jnp.maximum, [jnp.max(block, axis=0, keepdims=True) for block in inner + outer]
        )
        raised = [jnp.exp2((block - highest) * rate) for block in inner + outer]
        amount = sum(jnp.sum(block, axis=0, keepdims=True) for block in raised)
        inverse = 1.0 / amount
        weights = [block * inverse for block in raised]
        low = [block.astype(LOW) for block in weights]

        def mix(kind, parts):
            near = sum(
                nn(
                    turned[kind, :, pl.ds(pl.multiple_of((unit + step) * 256, 256), 256)],
                    parts[step],
                )
                for step in range(3)
            )
            far = [
                sum(
                    nn(
                        outer_turned[
                            kind, row, :, pl.ds(pl.multiple_of((unit + step) * TILE, TILE), TILE)
                        ],
                        parts[3 + step][:, row * TILE : (row + 1) * TILE],
                    )
                    for step in range(3)
                )
                for row in range(2)
            ]
            return near + jnp.concatenate(far, axis=1)

        def fold(kind, parts, right, right_both):
            for step in range(3):
                slot = unit + step
                near = nn(parts[step], right_both)
                for row in range(2):
                    total[kind, slot, row] += near[row * TILE : (row + 1) * TILE]
                    total[kind, slot, 2 + row] += nn(
                        parts[3 + step][:, row * TILE : (row + 1) * TILE], right[row]
                    )

        mixed = mix(1, low).T
        offsets = jnp.sum((up_both.astype(WIDE) * mixed).T, axis=0, keepdims=True)
        for row in range(2):
            held[0, row, unit] = mixed[row * TILE : (row + 1) * TILE].astype(LOW)
        fold(1, low, ups, up_both)
        inner, outer = products(1, ups, up_both)
        slopes = [
            (weight * (block - offsets)).astype(LOW)
            for weight, block in zip(weights, inner + outer)
        ]
        query_grad = mix(0, slopes).T * scaling
        for row in range(2):
            held[1, row, unit] = query_grad[row * TILE : (row + 1) * TILE].astype(LOW)
        fold(0, slopes, queries, both)
        return carry

    lax.fori_loop(0, 5, one_unit, 0, unroll=True)
    for kind in range(2):
        for turn in range(2):
            row = (turn + odd) % 2
            for which in range(2):
                for part in range(2):
                    tile = held[kind, row, first_of(which, odd) + part]
                    firsts[2 * which + turn][kind, part] = tile
            rest[kind, turn] = held[kind, row, first_of(2, odd)]
    for kind, factor in ((0, scaling), (1, 1.0)):
        for at in range(7):
            for row in range(2):
                terms[kind, row, at] = total[kind, at, row] * factor
                edges[row][kind, at] = (total[kind, at, 3 - row] * factor).astype(LOW)


def column_shapes():
    return [jax.ShapeDtypeStruct((2, 2, TILE, HEAD_DIM), LOW)] * 2


def attend(table, own, halos, grads):
    return pl.pallas_call(
        attend_kernel,
        out_shape=pair_shapes(2, 4)
        + [
            jax.ShapeDtypeStruct((2, 2, TILE, HEAD_DIM), LOW),
            jax.ShapeDtypeStruct((2, 2, 7, TILE, HEAD_DIM), WIDE),
            jax.ShapeDtypeStruct((2, 7, TILE, HEAD_DIM), LOW),
            jax.ShapeDtypeStruct((2, 7, TILE, HEAD_DIM), LOW),
        ],
        in_specs=[pl.BlockSpec(memory_space=pltpu.SMEM)] + whole(9),
        out_specs=whole(8),
        scratch_shapes=[
            pltpu.VMEM((2, 7, 4, TILE, HEAD_DIM), LOW),
            pltpu.VMEM((2, HEAD_DIM, 14 * TILE), LOW),
            pltpu.VMEM((2, 2, HEAD_DIM, 7 * TILE), LOW),
            pltpu.VMEM((2, 5, TILE, HEAD_DIM), LOW),
            pltpu.VMEM((2, 7, 4, TILE, HEAD_DIM), WIDE),
            pltpu.VMEM((2, 2, 5, TILE, HEAD_DIM), LOW),
        ],
        compiler_params=pltpu.CompilerParams(vmem_limit_bytes=40 << 20),
        cost_estimate=pl.CostEstimate(
            flops=3_000_000_000, bytes_accessed=8_000_000, transcendentals=1_500_000
        ),
        name="attend",
    )(table, own, *halos, *grads)


def rims_kernel(table, terms, above, below, right, left, *outs):
    odd = table[8]
    edges = (above, below)
    for kind in range(2):
        for row, edge in enumerate(edges):
            for out, at in ((right, 6), (left, 0)):
                out[kind, row] = (terms[kind, row, at] + edge[kind, at].astype(WIDE)).astype(LOW)
    for turn in range(2):
        for part in range(2):
            at = first_of(1, odd) + part + 1
            for kind in range(2):
                flip = (turn + odd) % 2 == 1
                edge = jnp.where(flip, below[kind, at], above[kind, at])
                value = terms[kind, (turn + odd) % 2, at] + edge.astype(WIDE)
                outs[turn][kind, part] = value.astype(LOW)


def rims(table, terms, edges):
    return pl.pallas_call(
        rims_kernel,
        out_shape=column_shapes() + pair_shapes(2, 2),
        in_specs=[pl.BlockSpec(memory_space=pltpu.SMEM)] + whole(3),
        out_specs=whole(4),
        compiler_params=pltpu.CompilerParams(vmem_limit_bytes=16 << 20),
        name="rims",
    )(table, terms, *edges)


def combine_kernel(table, rest, terms, above, below, before, after, *outs):
    odd = table[8]
    flipped = odd == 1
    for turn in range(2):
        row = (turn + odd) % 2
        for kind in range(2):

            def summed(at):
                edge = jnp.where(row == 1, below[kind, at + 1], above[kind, at + 1])
                return terms[kind, row, at + 1] + edge.astype(WIDE)

            first = first_of(0, odd)
            left = before[kind, row].astype(WIDE)
            right = after[kind, row].astype(WIDE)
            one, two = summed(first), summed(first + 1)
            outs[turn][kind, 0] = jnp.where(flipped, one, one + left).astype(LOW)
            outs[turn][kind, 1] = jnp.where(flipped, two + right, two).astype(LOW)
            alone = summed(first_of(2, odd)) + jnp.where(flipped, left, right)
            outs[2 + turn][kind] = rest[kind, turn]
            outs[2 + turn][2 + kind] = alone.astype(LOW)


def combine(table, rest, terms, edges, columns):
    return pl.pallas_call(
        combine_kernel,
        out_shape=pair_shapes(2, 2) + [jax.ShapeDtypeStruct((4, TILE, HEAD_DIM), LOW)] * 2,
        in_specs=[pl.BlockSpec(memory_space=pltpu.SMEM)] + whole(6),
        out_specs=whole(4),
        compiler_params=pltpu.CompilerParams(vmem_limit_bytes=16 << 20),
        name="combine",
    )(table, rest, terms, *edges, *columns)


def send_all(parts, routes):
    return [lax.ppermute(part, "tile", path) for part, path in zip(parts, routes)]


def local(query_slab, key_slab, value_slab, upstream):
    place = place_table()
    to_owner = [owner_of(which, turn) for which, turn in OWNER_STEPS]
    row_routes = [shifted(*step) for step in ROW_STEPS]
    column_routes = [shifted(*step) for step in COLUMN_STEPS]

    with jax.named_scope("upstream_to_units"):
        grads = send_all(spread(place, upstream), [flipped(path) for path in to_owner])

    with jax.named_scope("heads"):
        lines = [
            slab.reshape(8, 4, 40, 128).transpose(2, 0, 1, 3).reshape(8, 5, 32, 128)
            for slab in (query_slab, key_slab, value_slab)
        ]
        swapped = lax.all_to_all(jnp.stack(lines, axis=1), "head", 0, 0, tiled=True)
    with jax.named_scope("tiles"):
        dealt, early = lax.optimization_barrier((deal(swapped), grads[:EARLY]))
        got = lax.all_to_all(dealt, "tile", 0, 0, tiled=True)
        own = got.reshape(32, 19, 2, 4, 128).transpose(2, 1, 0, 3, 4)
        own = own.reshape(2, 19, TILE, HEAD_DIM)
        own, late = lax.optimization_barrier((own, grads[EARLY:]))
    with jax.named_scope("halos"):
        halos = send_all([own[1, 5:], own[0, 5:]], row_routes)
    with jax.named_scope("attention"):
        *first, rest, terms, above, below = attend(place, own, halos, early + late)
    with jax.named_scope("row_terms"):
        edges = send_all([above, below], row_routes)
        first = send_all(first, to_owner[:4])
        edges, first[:2] = lax.optimization_barrier((edges, first[:2]))
    with jax.named_scope("column_terms"):
        right, left, *free = rims(place, terms, edges)
        columns = send_all([right, left], column_routes)
        free = send_all(free, to_owner[2:4])
        columns, first[2:] = lax.optimization_barrier((columns, first[2:]))
    with jax.named_scope("outputs_home"):
        leaving = combine(place, rest, terms, edges, columns)
        leaving, free = lax.optimization_barrier((leaving, free))
        late = send_all(leaving, to_owner[:2] + to_owner[4:])
    with jax.named_scope("settle"):
        return tuple(gather(place, first + late[:2] + free + late[2:]))


def solution(mesh):
    slab = P("tile", None, "head", None)
    block = P("tile", "head")
    return jax.shard_map(
        local,
        mesh=mesh,
        in_specs=(slab, slab, slab, block),
        out_specs=(block, block, block, block),
        check_vma=False,
    )
```

```python
import functools
import math

import jax
import jax.numpy as jnp
import numpy as np
from jax import lax
from jax.experimental import pallas as pl
from jax.experimental.pallas import tpu as pltpu
from jax.sharding import PartitionSpec as P

HEAD_DIM = 128
HEADS_HERE = 5
STRIPS = 4
SLOTS = 8
TILE = 128
LOW = jnp.bfloat16
WIDE = jnp.float32
NEVER = -1e30


def route(step):
    pairs = []
    for strip in range(STRIPS):
        for slot in range(SLOTS):
            goal = step(strip, slot)
            if goal is not None:
                pairs.append((strip * SLOTS + slot, goal[0] * SLOTS + goal[1]))
    return pairs


def run_at(slot):
    return (5 - slot) % SLOTS


def shifted(rows, columns):
    def step(strip, slot):
        there = (strip + rows, run_at(slot) + columns)
        if 0 <= there[0] < STRIPS and 0 <= there[1] < SLOTS:
            return there[0], run_at(there[1])
        return None

    return route(step)


def first_of(which, odd):
    return (3 * odd, 2 - odd, 4 - 4 * odd)[which]


def owner_of(which, turn):
    def step(strip, slot):
        run = run_at(slot)
        odd = run % 2
        unit = 5 * run + first_of(which, odd)
        return (strip, ((turn + odd) % 2) * 4 + (unit % 8) // 2)

    return route(step)


def on_cores(which, turn):
    pairs = []
    for group in range(8):
        for source, target in owner_of(which, (turn + group) % 2):
            pairs.append((source * 8 + group, target * 8 + group))
    return pairs


def flipped(pairs):
    return [(target, source) for source, target in pairs]


ROW_STEPS = ((1, 0), (-1, 0))
COLUMN_STEPS = ((0, 1), (0, -1))
EARLY = 3
BOTH = ("tile", "head")
OWNER_STEPS = tuple((which, turn) for which in range(3) for turn in range(2))


def nt(one, two):
    return lax.dot_general(one, two, (((1,), (1,)), ((), ())), preferred_element_type=WIDE)


def nn(one, two):
    return jnp.dot(one, two, preferred_element_type=WIDE)


def whole(count):
    return [pl.BlockSpec(memory_space=pltpu.VMEM)] * count


def owner_rows(core):
    rows = []
    for slot in range(SLOTS):
        row, pair = slot // 4, slot % 4
        heads = []
        for which, turn in OWNER_STEPS:
            if which == 2:
                unit = 10 * ((pair + 2) % 4) + 4
            elif (row + turn + core) % 2:
                unit = 10 * ((pair - 3 * which) % 4) + 8 - 2 * which
            else:
                unit = 10 * ((pair - which) % 4) + 2 * which
            heads.append(unit // 8)
        rows.append(heads + [(row + core) % 2])
    return rows


def place_table():
    rows = []
    for strip in range(STRIPS):
        for slot in range(SLOTS):
            run = run_at(slot)
            for core in range(2):
                columns = [(5 * run + at) % 8 for at in range(5)]
                swap = (run + core) % 2
                rows.append(owner_rows(core)[slot] + [strip, run % 2] + columns + [swap])
    every = jnp.asarray(np.array(rows, np.int32))
    at = lax.axis_index("tile") * 2 + lax.axis_index("head") % 2
    return lax.dynamic_index_in_dim(every, at, 0, keepdims=False)


def spread_kernel(table, upstream, *outs):
    line = lax.broadcasted_iota(jnp.int32, (2 * TILE, 2 * TILE), 0)
    col = lax.broadcasted_iota(jnp.int32, (2 * TILE, 2 * TILE), 1)
    source = ((line & 127) >> 2) * 8 + (line >> 7) * 4 + (line & 3)
    order = (col == source).astype(LOW)
    for at, (which, turn) in enumerate(OWNER_STEPS):
        head = pl.multiple_of(table[at] * HEAD_DIM, HEAD_DIM)
        tiles = jnp.dot(order, upstream[:, pl.ds(head, HEAD_DIM)], preferred_element_type=WIDE)
        tiles = tiles.astype(LOW)
        if which == 2:
            second = ((table[6] + turn) % 2) == 1
            outs[at][...] = jnp.where(second, tiles[TILE:], tiles[:TILE])
        else:
            outs[at][...] = tiles.reshape(2, TILE, HEAD_DIM)


def spread(table, upstream):
    shapes = [
        jax.ShapeDtypeStruct((TILE, HEAD_DIM) if which == 2 else (2, TILE, HEAD_DIM), LOW)
        for which, _ in OWNER_STEPS
    ]
    return pl.pallas_call(
        spread_kernel,
        out_shape=shapes,
        in_specs=[pl.BlockSpec(memory_space=pltpu.SMEM)] + whole(1),
        out_specs=whole(6),
        compiler_params=pltpu.CompilerParams(vmem_limit_bytes=16 << 20),
        name="spread",
    )(table, upstream)


def gather_kernel(table, *refs):
    free, late, singles = refs[:2], refs[2:4], refs[4:6]
    outs = refs[6:10]
    line = lax.broadcasted_iota(jnp.int32, (2 * TILE, 2 * TILE), 0)
    col = lax.broadcasted_iota(jnp.int32, (2 * TILE, 2 * TILE), 1)
    source = ((line >> 2) & 1) * TILE + (line >> 3) * 4 + (line & 3)
    order = (col == source).astype(LOW)
    flip = table[6] == 1

    def place(at, tiles):
        head = pl.multiple_of(table[at] * HEAD_DIM, HEAD_DIM)
        ordered = nn(order, jnp.concatenate(tiles, axis=1)).astype(LOW)
        for kind, out in enumerate(outs):
            out[:, pl.ds(head, HEAD_DIM)] = ordered[:, kind * HEAD_DIM : (kind + 1) * HEAD_DIM]

    for at in range(4):
        received = (late, free)[at // 2][at % 2]
        place(at, [received[kind].reshape(2 * TILE, HEAD_DIM) for kind in range(4)])
    one, two = singles[0][...], singles[1][...]
    tops, lows = jnp.where(flip, two, one), jnp.where(flip, one, two)
    place(4, [jnp.concatenate([tops[kind], lows[kind]], axis=0) for kind in range(4)])


def gather(table, received):
    return pl.pallas_call(
        gather_kernel,
        out_shape=[jax.ShapeDtypeStruct((2 * TILE, HEADS_HERE * HEAD_DIM), LOW)] * 4,
        in_specs=[pl.BlockSpec(memory_space=pltpu.SMEM)] + whole(6),
        out_specs=whole(4),
        compiler_params=pltpu.CompilerParams(vmem_limit_bytes=16 << 20),
        name="gather",
    )(table, *received)


def deal_kernel(swapped, out):
    for slot in range(SLOTS):
        for at in range(7):
            unit = min(max(5 * run_at(slot) + at - 1, 0), 39)
            head, column = unit // 8, unit % 8
            for kind in range(3):
                if kind == 0 and not 1 <= at <= 5:
                    continue
                place = at - 1 if kind == 0 else 7 * kind - 2 + at
                lines = swapped[column, kind, head].reshape(STRIPS, 8, HEAD_DIM)
                for strip in range(STRIPS):
                    out[strip * SLOTS + slot, place] = lines[strip]


def deal(swapped):
    return pl.pallas_call(
        deal_kernel,
        out_shape=jax.ShapeDtypeStruct((STRIPS * SLOTS, 19, 8, HEAD_DIM), LOW),
        in_specs=whole(1),
        out_specs=whole(1)[0],
        compiler_params=pltpu.CompilerParams(vmem_limit_bytes=16 << 20),
        name="deal",
    )(swapped)


def pair_shapes(kinds, count):
    return [jax.ShapeDtypeStruct((kinds, 2, TILE, HEAD_DIM), LOW)] * count


def attend_kernel(table, own, above, below, *refs):
    grads, rest, terms, edges = refs[:6], refs[6], refs[7], refs[8:10]
    pair, turned, outer_turned, grad, total, held = refs[10:]
    strip, odd, swap = table[7], table[8], table[14]
    scaling = HEAD_DIM**-0.5
    rate = scaling * math.log2(math.e)

    for kind in range(2):
        for at in range(7):
            for row in range(2):
                pair[kind, at, row] = own[row, 5 + 7 * kind + at]
            pair[kind, at, 2] = above[7 * kind + at]
            pair[kind, at, 3] = below[7 * kind + at]
    for kind in range(2):
        for at in range(7):
            for row in range(2):
                lanes = pl.ds((2 * at + row) * TILE, TILE)
                turned[kind, :, lanes] = pair[kind, at, row].T
                outer_turned[kind, row, :, pl.ds(at * TILE, TILE)] = pair[kind, at, 2 + row].T
    for at, (which, turn) in enumerate(OWNER_STEPS):
        row = (turn + swap) % 2
        first = first_of(which, odd)
        if which == 2:
            grad[row, first] = grads[at][...]
        else:
            for part in range(2):
                grad[row, first + part] = grads[at][part]
    total[...] = jnp.zeros_like(total)

    def one_unit(unit, carry):
        column = table[9 + unit]
        queries = [own[row, unit] for row in range(2)]
        both = jnp.concatenate(queries, axis=0)
        ups = [grad[row, unit] for row in range(2)]
        up_both = jnp.concatenate(ups, axis=0)
        column_ok = (column > 0, None, column < 7)
        row_ok = (strip > 0, strip < STRIPS - 1)

        def products(kind, left, left_both):
            inner, outer = [], []
            for step in range(3):
                slot = unit + step
                near = pair[kind, slot, 0:2].reshape(2 * TILE, HEAD_DIM)
                inner.append(nt(near, left_both))
                outer.append(
                    jnp.concatenate(
                        [nt(pair[kind, slot, 2 + row], left[row]) for row in range(2)], axis=1
                    )
                )
            return inner, outer

        inner, outer = products(0, queries, both)
        lane = lax.broadcasted_iota(jnp.int32, (1, 2 * TILE), 1)
        row_bias = jnp.where(
            lane < TILE,
            jnp.where(row_ok[0], 0.0, NEVER),
            jnp.where(row_ok[1], 0.0, NEVER),
        )
        for step in range(3):
            if column_ok[step] is None:
                outer[step] = outer[step] + row_bias
            else:
                bias = jnp.where(column_ok[step], 0.0, NEVER)
                inner[step] = inner[step] + bias
                outer[step] = outer[step] + (row_bias + bias)
        highest = functools.reduce(
            jnp.maximum, [jnp.max(block, axis=0, keepdims=True) for block in inner + outer]
        )
        raised = [jnp.exp2((block - highest) * rate) for block in inner + outer]
        amount = sum(jnp.sum(block, axis=0, keepdims=True) for block in raised)
        inverse = 1.0 / amount
        weights = [block * inverse for block in raised]
        low = [block.astype(LOW) for block in weights]

        def mix(kind, parts):
            near = sum(
                nn(
                    turned[kind, :, pl.ds(pl.multiple_of((unit + step) * 256, 256), 256)],
                    parts[step],
                )
                for step in range(3)
            )
            far = [
                sum(
                    nn(
                        outer_turned[
                            kind, row, :, pl.ds(pl.multiple_of((unit + step) * TILE, TILE), TILE)
                        ],
                        parts[3 + step][:, row * TILE : (row + 1) * TILE],
                    )
                    for step in range(3)
                )
                for row in range(2)
            ]
            return near + jnp.concatenate(far, axis=1)

        def fold(kind, parts, right, right_both):
            for step in range(3):
                slot = unit + step
                near = nn(parts[step], right_both)
                for row in range(2):
                    total[kind, slot, row] += near[row * TILE : (row + 1) * TILE]
                    total[kind, slot, 2 + row] += nn(
                        parts[3 + step][:, row * TILE : (row + 1) * TILE], right[row]
                    )

        mixed = mix(1, low).T
        offsets = jnp.sum((up_both.astype(WIDE) * mixed).T, axis=0, keepdims=True)
        for row in range(2):
            held[0, row, unit] = mixed[row * TILE : (row + 1) * TILE].astype(LOW)
        fold(1, low, ups, up_both)
        inner, outer = products(1, ups, up_both)
        slopes = [
            (weight * (block - offsets)).astype(LOW)
            for weight, block in zip(weights, inner + outer)
        ]
        query_grad = mix(0, slopes).T * scaling
        for row in range(2):
            held[1, row, unit] = query_grad[row * TILE : (row + 1) * TILE].astype(LOW)
        fold(0, slopes, queries, both)
        return carry

    lax.fori_loop(0, 5, one_unit, 0, unroll=True)
    for kind in range(2):
        for turn in range(2):
            row = (turn + swap) % 2
            for part in range(2):
                rest[kind, turn, part] = held[kind, row, first_of(0, odd) + part]
                rest[kind, turn, 2 + part] = held[kind, row, first_of(1, odd) + part]
            rest[kind, turn, 4] = held[kind, row, first_of(2, odd)]
    for kind, factor in ((0, scaling), (1, 1.0)):
        for at in range(7):
            for row in range(2):
                terms[kind, row, at] = total[kind, at, row] * factor
                edges[row][kind, at] = (total[kind, at, 3 - row] * factor).astype(LOW)


def column_shapes():
    return [jax.ShapeDtypeStruct((2, 2, TILE, HEAD_DIM), LOW)] * 2


def attend(table, own, halos, grads):
    return pl.pallas_call(
        attend_kernel,
        out_shape=[
            jax.ShapeDtypeStruct((2, 2, 5, TILE, HEAD_DIM), LOW),
            jax.ShapeDtypeStruct((2, 2, 7, TILE, HEAD_DIM), WIDE),
            jax.ShapeDtypeStruct((2, 7, TILE, HEAD_DIM), LOW),
            jax.ShapeDtypeStruct((2, 7, TILE, HEAD_DIM), LOW),
        ],
        in_specs=[pl.BlockSpec(memory_space=pltpu.SMEM)] + whole(9),
        out_specs=whole(4),
        scratch_shapes=[
            pltpu.VMEM((2, 7, 4, TILE, HEAD_DIM), LOW),
            pltpu.VMEM((2, HEAD_DIM, 14 * TILE), LOW),
            pltpu.VMEM((2, 2, HEAD_DIM, 7 * TILE), LOW),
            pltpu.VMEM((2, 5, TILE, HEAD_DIM), LOW),
            pltpu.VMEM((2, 7, 4, TILE, HEAD_DIM), WIDE),
            pltpu.VMEM((2, 2, 5, TILE, HEAD_DIM), LOW),
        ],
        compiler_params=pltpu.CompilerParams(vmem_limit_bytes=40 << 20),
        cost_estimate=pl.CostEstimate(
            flops=3_000_000_000, bytes_accessed=8_000_000, transcendentals=1_500_000
        ),
        name="attend",
    )(table, own, *halos, *grads)


def rims_kernel(table, rest, terms, above, below, right, left, *outs):
    odd, swap = table[8], table[14]
    edges = (above, below)
    for kind in range(2):
        for row, edge in enumerate(edges):
            for out, at in ((right, 6), (left, 0)):
                out[kind, row] = (terms[kind, row, at] + edge[kind, at].astype(WIDE)).astype(LOW)
    for turn in range(2):
        for part in range(2):
            at = first_of(1, odd) + part + 1
            for kind in range(2):
                outs[turn][kind, part] = rest[kind, turn, 2 + part]
                flip = (turn + swap) % 2 == 1
                edge = jnp.where(flip, below[kind, at], above[kind, at])
                value = terms[kind, (turn + swap) % 2, at] + edge.astype(WIDE)
                outs[turn][2 + kind, part] = value.astype(LOW)


def rims(table, rest, terms, edges):
    return pl.pallas_call(
        rims_kernel,
        out_shape=column_shapes() + pair_shapes(4, 2),
        in_specs=[pl.BlockSpec(memory_space=pltpu.SMEM)] + whole(4),
        out_specs=whole(4),
        compiler_params=pltpu.CompilerParams(vmem_limit_bytes=16 << 20),
        name="rims",
    )(table, rest, terms, *edges)


def combine_kernel(table, rest, terms, above, below, before, after, *outs):
    odd, swap = table[8], table[14]
    flipped = odd == 1
    for turn in range(2):
        row = (turn + swap) % 2
        for kind in range(2):

            def summed(at):
                edge = jnp.where(row == 1, below[kind, at + 1], above[kind, at + 1])
                return terms[kind, row, at + 1] + edge.astype(WIDE)

            first = first_of(0, odd)
            left = before[kind, row].astype(WIDE)
            right = after[kind, row].astype(WIDE)
            one, two = summed(first), summed(first + 1)
            for part in range(2):
                outs[turn][kind, part] = rest[kind, turn, part]
            outs[turn][2 + kind, 0] = jnp.where(flipped, one, one + left).astype(LOW)
            outs[turn][2 + kind, 1] = jnp.where(flipped, two + right, two).astype(LOW)
            alone = summed(first_of(2, odd)) + jnp.where(flipped, left, right)
            outs[2 + turn][kind] = rest[kind, turn, 4]
            outs[2 + turn][2 + kind] = alone.astype(LOW)


def combine(table, rest, terms, edges, columns):
    return pl.pallas_call(
        combine_kernel,
        out_shape=pair_shapes(4, 2) + [jax.ShapeDtypeStruct((4, TILE, HEAD_DIM), LOW)] * 2,
        in_specs=[pl.BlockSpec(memory_space=pltpu.SMEM)] + whole(6),
        out_specs=whole(4),
        compiler_params=pltpu.CompilerParams(vmem_limit_bytes=16 << 20),
        name="combine",
    )(table, rest, terms, *edges, *columns)


def send_all(parts, routes, axis="tile"):
    return [lax.ppermute(part, axis, path) for part, path in zip(parts, routes)]


def local(query_slab, key_slab, value_slab, upstream):
    place = place_table()
    to_owner = [on_cores(which, turn) for which, turn in OWNER_STEPS]
    row_routes = [shifted(*step) for step in ROW_STEPS]
    column_routes = [shifted(*step) for step in COLUMN_STEPS]

    with jax.named_scope("upstream_to_units"):
        grads = send_all(spread(place, upstream), [flipped(path) for path in to_owner], BOTH)

    with jax.named_scope("heads"):
        lines = [
            slab.reshape(8, 4, 40, 128).transpose(2, 0, 1, 3).reshape(8, 5, 32, 128)
            for slab in (query_slab, key_slab, value_slab)
        ]
        swapped = lax.all_to_all(jnp.stack(lines, axis=1), "head", 0, 0, tiled=True)
    with jax.named_scope("tiles"):
        dealt, early = lax.optimization_barrier((deal(swapped), grads[:EARLY]))
        got = lax.all_to_all(dealt, "tile", 0, 0, tiled=True)
        own = got.reshape(32, 19, 2, 4, 128).transpose(2, 1, 0, 3, 4)
        own = own.reshape(2, 19, TILE, HEAD_DIM)
        own, late = lax.optimization_barrier((own, grads[EARLY:]))
    with jax.named_scope("halos"):
        halos = send_all([own[1, 5:], own[0, 5:]], row_routes)
    with jax.named_scope("attention"):
        rest, terms, above, below = attend(place, own, halos, early + late)
    with jax.named_scope("row_terms"):
        edges = send_all([above, below], row_routes)
    with jax.named_scope("column_terms"):
        right, left, *free = rims(place, rest, terms, edges)
        columns = send_all([right, left], column_routes)
        free = send_all(free, to_owner[2:4], BOTH)
    with jax.named_scope("outputs_home"):
        leaving = combine(place, rest, terms, edges, columns)
        leaving, free = lax.optimization_barrier((leaving, free))
        late = send_all(leaving, to_owner[:2] + to_owner[4:], BOTH)
    with jax.named_scope("settle"):
        return tuple(gather(place, free + late))


def solution(mesh):
    slab = P("tile", None, "head", None)
    block = P("tile", "head")
    return jax.shard_map(
        local,
        mesh=mesh,
        in_specs=(slab, slab, slab, block),
        out_specs=(block, block, block, block),
        check_vma=False,
    )
```

```python
import functools
import math

import jax
import jax.numpy as jnp
import numpy as np
from jax import lax
from jax.experimental import pallas as pl
from jax.experimental.pallas import tpu as pltpu
from jax.sharding import PartitionSpec as P

HEAD_DIM = 128
HEADS_HERE = 5
STRIPS = 4
SLOTS = 8
TILE = 128
LOW = jnp.bfloat16
WIDE = jnp.float32
NEVER = -1e30


def route(step):
    pairs = []
    for strip in range(STRIPS):
        for slot in range(SLOTS):
            goal = step(strip, slot)
            if goal is not None:
                pairs.append((strip * SLOTS + slot, goal[0] * SLOTS + goal[1]))
    return pairs


def run_at(slot):
    return (5 - slot) % SLOTS


def shifted(rows, columns):
    def step(strip, slot):
        there = (strip + rows, run_at(slot) + columns)
        if 0 <= there[0] < STRIPS and 0 <= there[1] < SLOTS:
            return there[0], run_at(there[1])
        return None

    return route(step)


def first_of(which, odd):
    return (3 * odd, 2 - odd, 4 - 4 * odd)[which]


def owner_of(which, turn):
    def step(strip, slot):
        run = run_at(slot)
        odd = run % 2
        unit = 5 * run + first_of(which, odd)
        return (strip, ((turn + odd) % 2) * 4 + (unit % 8) // 2)

    return route(step)


def on_cores(which, turn):
    pairs = []
    for group in range(8):
        for source, target in owner_of(which, (turn + group) % 2):
            pairs.append((source * 8 + group, target * 8 + group))
    return pairs


def rows_on_cores(first):
    pairs = []
    for group in range(8):
        for source, target in shifted(first if group % 2 == 0 else -first, 0):
            pairs.append((source * 8 + group, target * 8 + group))
    return pairs


def flipped(pairs):
    return [(target, source) for source, target in pairs]


COLUMN_STEPS = ((0, 1), (0, -1))
EARLY = 3
BOTH = ("tile", "head")
OWNER_STEPS = tuple((which, turn) for which in range(3) for turn in range(2))


def nt(one, two):
    return lax.dot_general(one, two, (((1,), (1,)), ((), ())), preferred_element_type=WIDE)


def nn(one, two):
    return jnp.dot(one, two, preferred_element_type=WIDE)


def whole(count):
    return [pl.BlockSpec(memory_space=pltpu.VMEM)] * count


def owner_rows(core):
    rows = []
    for slot in range(SLOTS):
        row, pair = slot // 4, slot % 4
        heads = []
        for which, turn in OWNER_STEPS:
            if which == 2:
                unit = 10 * ((pair + 2) % 4) + 4
            elif (row + turn + core) % 2:
                unit = 10 * ((pair - 3 * which) % 4) + 8 - 2 * which
            else:
                unit = 10 * ((pair - which) % 4) + 2 * which
            heads.append(unit // 8)
        rows.append(heads + [(row + core) % 2])
    return rows


def place_table():
    rows = []
    for strip in range(STRIPS):
        for slot in range(SLOTS):
            run = run_at(slot)
            for core in range(2):
                columns = [(5 * run + at) % 8 for at in range(5)]
                swap = (run + core) % 2
                rows.append(owner_rows(core)[slot] + [strip, run % 2] + columns + [swap, core])
    every = jnp.asarray(np.array(rows, np.int32))
    at = lax.axis_index("tile") * 2 + lax.axis_index("head") % 2
    return lax.dynamic_index_in_dim(every, at, 0, keepdims=False)


def spread_kernel(table, upstream, *outs):
    line = lax.broadcasted_iota(jnp.int32, (2 * TILE, 2 * TILE), 0)
    col = lax.broadcasted_iota(jnp.int32, (2 * TILE, 2 * TILE), 1)
    source = ((line & 127) >> 2) * 8 + (line >> 7) * 4 + (line & 3)
    order = (col == source).astype(LOW)
    for at, (which, turn) in enumerate(OWNER_STEPS):
        head = pl.multiple_of(table[at] * HEAD_DIM, HEAD_DIM)
        tiles = jnp.dot(order, upstream[:, pl.ds(head, HEAD_DIM)], preferred_element_type=WIDE)
        tiles = tiles.astype(LOW)
        if which == 2:
            second = ((table[6] + turn) % 2) == 1
            outs[at][...] = jnp.where(second, tiles[TILE:], tiles[:TILE])
        else:
            outs[at][...] = tiles.reshape(2, TILE, HEAD_DIM)


def spread(table, upstream):
    shapes = [
        jax.ShapeDtypeStruct((TILE, HEAD_DIM) if which == 2 else (2, TILE, HEAD_DIM), LOW)
        for which, _ in OWNER_STEPS
    ]
    return pl.pallas_call(
        spread_kernel,
        out_shape=shapes,
        in_specs=[pl.BlockSpec(memory_space=pltpu.SMEM)] + whole(1),
        out_specs=whole(6),
        compiler_params=pltpu.CompilerParams(vmem_limit_bytes=16 << 20),
        name="spread",
    )(table, upstream)


def gather_kernel(table, *refs):
    free, late, singles = refs[:2], refs[2:4], refs[4:6]
    outs = refs[6:10]
    line = lax.broadcasted_iota(jnp.int32, (2 * TILE, 2 * TILE), 0)
    col = lax.broadcasted_iota(jnp.int32, (2 * TILE, 2 * TILE), 1)
    source = ((line >> 2) & 1) * TILE + (line >> 3) * 4 + (line & 3)
    order = (col == source).astype(LOW)
    flip = table[6] == 1

    def place(at, tiles):
        head = pl.multiple_of(table[at] * HEAD_DIM, HEAD_DIM)
        ordered = nn(order, jnp.concatenate(tiles, axis=1)).astype(LOW)
        for kind, out in enumerate(outs):
            out[:, pl.ds(head, HEAD_DIM)] = ordered[:, kind * HEAD_DIM : (kind + 1) * HEAD_DIM]

    for at in range(4):
        received = (late, free)[at // 2][at % 2]
        place(at, [received[kind].reshape(2 * TILE, HEAD_DIM) for kind in range(4)])
    one, two = singles[0][...], singles[1][...]
    tops, lows = jnp.where(flip, two, one), jnp.where(flip, one, two)
    place(4, [jnp.concatenate([tops[kind], lows[kind]], axis=0) for kind in range(4)])


def gather(table, received):
    return pl.pallas_call(
        gather_kernel,
        out_shape=[jax.ShapeDtypeStruct((2 * TILE, HEADS_HERE * HEAD_DIM), LOW)] * 4,
        in_specs=[pl.BlockSpec(memory_space=pltpu.SMEM)] + whole(6),
        out_specs=whole(4),
        compiler_params=pltpu.CompilerParams(vmem_limit_bytes=16 << 20),
        name="gather",
    )(table, *received)


def deal_kernel(swapped, out):
    for slot in range(SLOTS):
        for at in range(7):
            unit = min(max(5 * run_at(slot) + at - 1, 0), 39)
            head, column = unit // 8, unit % 8
            for kind in range(3):
                if kind == 0 and not 1 <= at <= 5:
                    continue
                place = at - 1 if kind == 0 else 7 * kind - 2 + at
                lines = swapped[column, kind, head].reshape(STRIPS, 8, HEAD_DIM)
                for strip in range(STRIPS):
                    out[strip * SLOTS + slot, place] = lines[strip]


def deal(swapped):
    return pl.pallas_call(
        deal_kernel,
        out_shape=jax.ShapeDtypeStruct((STRIPS * SLOTS, 19, 8, HEAD_DIM), LOW),
        in_specs=whole(1),
        out_specs=whole(1)[0],
        compiler_params=pltpu.CompilerParams(vmem_limit_bytes=16 << 20),
        name="deal",
    )(swapped)


def pair_shapes(kinds, count):
    return [jax.ShapeDtypeStruct((kinds, 2, TILE, HEAD_DIM), LOW)] * count


def attend_kernel(table, own, one, two, *refs):
    grads, rest, terms, edges = refs[:6], refs[6], refs[7], refs[8:10]
    pair, turned, outer_turned, grad, total, held = refs[10:]
    strip, odd, swap, core = table[7], table[8], table[14], table[15]
    scaling = HEAD_DIM**-0.5
    rate = scaling * math.log2(math.e)

    for kind in range(2):
        for at in range(7):
            for row in range(2):
                pair[kind, at, row] = own[row, 5 + 7 * kind + at]
            pair[kind, at, 2 + core] = one[7 * kind + at]
            pair[kind, at, 3 - core] = two[7 * kind + at]
    for kind in range(2):
        for at in range(7):
            for row in range(2):
                lanes = pl.ds((2 * at + row) * TILE, TILE)
                turned[kind, :, lanes] = pair[kind, at, row].T
                outer_turned[kind, row, :, pl.ds(at * TILE, TILE)] = pair[kind, at, 2 + row].T
    for at, (which, turn) in enumerate(OWNER_STEPS):
        row = (turn + swap) % 2
        first = first_of(which, odd)
        if which == 2:
            grad[row, first] = grads[at][...]
        else:
            for part in range(2):
                grad[row, first + part] = grads[at][part]
    total[...] = jnp.zeros_like(total)

    def one_unit(unit, carry):
        column = table[9 + unit]
        queries = [own[row, unit] for row in range(2)]
        both = jnp.concatenate(queries, axis=0)
        ups = [grad[row, unit] for row in range(2)]
        up_both = jnp.concatenate(ups, axis=0)
        column_ok = (column > 0, None, column < 7)
        row_ok = (strip > 0, strip < STRIPS - 1)

        def products(kind, left, left_both):
            inner, outer = [], []
            for step in range(3):
                slot = unit + step
                near = pair[kind, slot, 0:2].reshape(2 * TILE, HEAD_DIM)
                inner.append(nt(near, left_both))
                outer.append(
                    jnp.concatenate(
                        [nt(pair[kind, slot, 2 + row], left[row]) for row in range(2)], axis=1
                    )
                )
            return inner, outer

        inner, outer = products(0, queries, both)
        lane = lax.broadcasted_iota(jnp.int32, (1, 2 * TILE), 1)
        row_bias = jnp.where(
            lane < TILE,
            jnp.where(row_ok[0], 0.0, NEVER),
            jnp.where(row_ok[1], 0.0, NEVER),
        )
        for step in range(3):
            if column_ok[step] is None:
                outer[step] = outer[step] + row_bias
            else:
                bias = jnp.where(column_ok[step], 0.0, NEVER)
                inner[step] = inner[step] + bias
                outer[step] = outer[step] + (row_bias + bias)
        highest = functools.reduce(
            jnp.maximum, [jnp.max(block, axis=0, keepdims=True) for block in inner + outer]
        )
        raised = [jnp.exp2((block - highest) * rate) for block in inner + outer]
        amount = sum(jnp.sum(block, axis=0, keepdims=True) for block in raised)
        inverse = 1.0 / amount
        weights = [block * inverse for block in raised]
        low = [block.astype(LOW) for block in weights]

        def mix(kind, parts):
            near = sum(
                nn(
                    turned[kind, :, pl.ds(pl.multiple_of((unit + step) * 256, 256), 256)],
                    parts[step],
                )
                for step in range(3)
            )
            far = [
                sum(
                    nn(
                        outer_turned[
                            kind, row, :, pl.ds(pl.multiple_of((unit + step) * TILE, TILE), TILE)
                        ],
                        parts[3 + step][:, row * TILE : (row + 1) * TILE],
                    )
                    for step in range(3)
                )
                for row in range(2)
            ]
            return near + jnp.concatenate(far, axis=1)

        def fold(kind, parts, right, right_both):
            for step in range(3):
                slot = unit + step
                near = nn(parts[step], right_both)
                for row in range(2):
                    total[kind, slot, row] += near[row * TILE : (row + 1) * TILE]
                    total[kind, slot, 2 + row] += nn(
                        parts[3 + step][:, row * TILE : (row + 1) * TILE], right[row]
                    )

        mixed = mix(1, low).T
        offsets = jnp.sum((up_both.astype(WIDE) * mixed).T, axis=0, keepdims=True)
        for row in range(2):
            held[0, row, unit] = mixed[row * TILE : (row + 1) * TILE].astype(LOW)
        fold(1, low, ups, up_both)
        inner, outer = products(1, ups, up_both)
        slopes = [
            (weight * (block - offsets)).astype(LOW)
            for weight, block in zip(weights, inner + outer)
        ]
        query_grad = mix(0, slopes).T * scaling
        for row in range(2):
            held[1, row, unit] = query_grad[row * TILE : (row + 1) * TILE].astype(LOW)
        fold(0, slopes, queries, both)
        return carry

    lax.fori_loop(0, 5, one_unit, 0, unroll=True)
    for kind in range(2):
        for turn in range(2):
            row = (turn + swap) % 2
            for part in range(2):
                rest[kind, turn, part] = held[kind, row, first_of(0, odd) + part]
                rest[kind, turn, 2 + part] = held[kind, row, first_of(1, odd) + part]
            rest[kind, turn, 4] = held[kind, row, first_of(2, odd)]
    for kind, factor in ((0, scaling), (1, 1.0)):
        for at in range(7):
            for row in range(2):
                terms[kind, row, at] = total[kind, at, row] * factor
            edges[0][kind, at] = (total[kind, at, 3 - core] * factor).astype(LOW)
            edges[1][kind, at] = (total[kind, at, 2 + core] * factor).astype(LOW)


def column_shapes():
    return [jax.ShapeDtypeStruct((2, 2, TILE, HEAD_DIM), LOW)] * 2


def attend(table, own, halos, grads):
    return pl.pallas_call(
        attend_kernel,
        out_shape=[
            jax.ShapeDtypeStruct((2, 2, 5, TILE, HEAD_DIM), LOW),
            jax.ShapeDtypeStruct((2, 2, 7, TILE, HEAD_DIM), WIDE),
            jax.ShapeDtypeStruct((2, 7, TILE, HEAD_DIM), LOW),
            jax.ShapeDtypeStruct((2, 7, TILE, HEAD_DIM), LOW),
        ],
        in_specs=[pl.BlockSpec(memory_space=pltpu.SMEM)] + whole(9),
        out_specs=whole(4),
        scratch_shapes=[
            pltpu.VMEM((2, 7, 4, TILE, HEAD_DIM), LOW),
            pltpu.VMEM((2, HEAD_DIM, 14 * TILE), LOW),
            pltpu.VMEM((2, 2, HEAD_DIM, 7 * TILE), LOW),
            pltpu.VMEM((2, 5, TILE, HEAD_DIM), LOW),
            pltpu.VMEM((2, 7, 4, TILE, HEAD_DIM), WIDE),
            pltpu.VMEM((2, 2, 5, TILE, HEAD_DIM), LOW),
        ],
        compiler_params=pltpu.CompilerParams(vmem_limit_bytes=40 << 20),
        cost_estimate=pl.CostEstimate(
            flops=3_000_000_000, bytes_accessed=8_000_000, transcendentals=1_500_000
        ),
        name="attend",
    )(table, own, *halos, *grads)


def rims_kernel(table, rest, terms, first, second, right, left, *outs):
    odd, swap, core = table[8], table[14], table[15]
    for kind in range(2):
        for row in range(2):
            for out, at in ((right, 6), (left, 0)):
                edge = jnp.where(core == row, first[kind, at], second[kind, at])
                out[kind, row] = (terms[kind, row, at] + edge.astype(WIDE)).astype(LOW)
    for turn in range(2):
        for part in range(2):
            at = first_of(1, odd) + part + 1
            for kind in range(2):
                outs[turn][kind, part] = rest[kind, turn, 2 + part]
                same = (turn + swap) % 2 == core
                edge = jnp.where(same, first[kind, at], second[kind, at])
                value = terms[kind, (turn + swap) % 2, at] + edge.astype(WIDE)
                outs[turn][2 + kind, part] = value.astype(LOW)


def rims(table, rest, terms, edges):
    return pl.pallas_call(
        rims_kernel,
        out_shape=column_shapes() + pair_shapes(4, 2),
        in_specs=[pl.BlockSpec(memory_space=pltpu.SMEM)] + whole(4),
        out_specs=whole(4),
        compiler_params=pltpu.CompilerParams(vmem_limit_bytes=16 << 20),
        name="rims",
    )(table, rest, terms, *edges)


def combine_kernel(table, rest, terms, upper, lower, before, after, *outs):
    odd, swap, core = table[8], table[14], table[15]
    flipped = odd == 1
    for turn in range(2):
        row = (turn + swap) % 2
        for kind in range(2):

            def summed(at):
                edge = jnp.where(row == core, upper[kind, at + 1], lower[kind, at + 1])
                return terms[kind, row, at + 1] + edge.astype(WIDE)

            first = first_of(0, odd)
            left = before[kind, row].astype(WIDE)
            right = after[kind, row].astype(WIDE)
            one, two = summed(first), summed(first + 1)
            for part in range(2):
                outs[turn][kind, part] = rest[kind, turn, part]
            outs[turn][2 + kind, 0] = jnp.where(flipped, one, one + left).astype(LOW)
            outs[turn][2 + kind, 1] = jnp.where(flipped, two + right, two).astype(LOW)
            alone = summed(first_of(2, odd)) + jnp.where(flipped, left, right)
            outs[2 + turn][kind] = rest[kind, turn, 4]
            outs[2 + turn][2 + kind] = alone.astype(LOW)


def combine(table, rest, terms, edges, columns):
    return pl.pallas_call(
        combine_kernel,
        out_shape=pair_shapes(4, 2) + [jax.ShapeDtypeStruct((4, TILE, HEAD_DIM), LOW)] * 2,
        in_specs=[pl.BlockSpec(memory_space=pltpu.SMEM)] + whole(6),
        out_specs=whole(4),
        compiler_params=pltpu.CompilerParams(vmem_limit_bytes=16 << 20),
        name="combine",
    )(table, rest, terms, *edges, *columns)


def send_all(parts, routes, axis="tile"):
    return [lax.ppermute(part, axis, path) for part, path in zip(parts, routes)]


def local(query_slab, key_slab, value_slab, upstream):
    place = place_table()
    to_owner = [on_cores(which, turn) for which, turn in OWNER_STEPS]
    row_routes = [rows_on_cores(first) for first in (1, -1)]
    core = lax.axis_index("head") % 2
    column_routes = [shifted(*step) for step in COLUMN_STEPS]

    with jax.named_scope("upstream_to_units"):
        grads = send_all(spread(place, upstream), [flipped(path) for path in to_owner], BOTH)

    with jax.named_scope("heads"):
        lines = [
            slab.reshape(8, 4, 40, 128).transpose(2, 0, 1, 3).reshape(8, 5, 32, 128)
            for slab in (query_slab, key_slab, value_slab)
        ]
        swapped = lax.all_to_all(jnp.stack(lines, axis=1), "head", 0, 0, tiled=True)
    with jax.named_scope("tiles"):
        dealt, early = lax.optimization_barrier((deal(swapped), grads[:EARLY]))
        got = lax.all_to_all(dealt, "tile", 0, 0, tiled=True)
        own = got.reshape(32, 19, 2, 4, 128).transpose(2, 1, 0, 3, 4)
        own = own.reshape(2, 19, TILE, HEAD_DIM)
        own, late = lax.optimization_barrier((own, grads[EARLY:]))
    with jax.named_scope("halos"):
        pair = own[:, 5:]
        leaving = [lax.dynamic_index_in_dim(pair, at, 0, keepdims=False) for at in (1 - core, core)]
        halos = send_all(leaving, row_routes, BOTH)
    with jax.named_scope("attention"):
        rest, terms, *edges = attend(place, own, halos, early + late)
    with jax.named_scope("row_terms"):
        edges = send_all(edges, row_routes, BOTH)
    with jax.named_scope("column_terms"):
        right, left, *free = rims(place, rest, terms, edges)
        columns = send_all([right, left], column_routes)
        free = send_all(free, to_owner[2:4], BOTH)
    with jax.named_scope("outputs_home"):
        leaving = combine(place, rest, terms, edges, columns)
        leaving, free = lax.optimization_barrier((leaving, free))
        late = send_all(leaving, to_owner[:2] + to_owner[4:], BOTH)
    with jax.named_scope("settle"):
        return tuple(gather(place, free + late))


def solution(mesh):
    slab = P("tile", None, "head", None)
    block = P("tile", "head")
    return jax.shard_map(
        local,
        mesh=mesh,
        in_specs=(slab, slab, slab, block),
        out_specs=(block, block, block, block),
        check_vma=False,
    )
```

```python
import functools
import math

import jax
import jax.numpy as jnp
import numpy as np
from jax import lax
from jax.experimental import pallas as pl
from jax.experimental.pallas import tpu as pltpu
from jax.sharding import PartitionSpec as P

HEAD_DIM = 128
HEADS_HERE = 5
STRIPS = 4
SLOTS = 8
TILE = 128
LOW = jnp.bfloat16
WIDE = jnp.float32
NEVER = -1e30


def route(step):
    pairs = []
    for strip in range(STRIPS):
        for slot in range(SLOTS):
            goal = step(strip, slot)
            if goal is not None:
                pairs.append((strip * SLOTS + slot, goal[0] * SLOTS + goal[1]))
    return pairs


def run_at(slot):
    return slot


def shifted(rows, columns):
    def step(strip, slot):
        there = (strip + rows, run_at(slot) + columns)
        if 0 <= there[0] < STRIPS and 0 <= there[1] < SLOTS:
            return there[0], run_at(there[1])
        return None

    return route(step)


def first_of(which, odd):
    return (3 * odd, 2 - odd, 4 - 4 * odd)[which]


def owner_of(which, turn):
    def step(strip, slot):
        run = run_at(slot)
        odd = run % 2
        unit = 5 * run + first_of(which, odd)
        return (strip, ((turn + odd) % 2) * 4 + (unit % 8) // 2)

    return route(step)


def on_cores(which, turn):
    pairs = []
    for group in range(8):
        for source, target in owner_of(which, (turn + group) % 2):
            pairs.append((source * 8 + group, target * 8 + group))
    return pairs


def flipped(pairs):
    return [(target, source) for source, target in pairs]


ROW_STEPS = ((1, 0), (-1, 0))
COLUMN_STEPS = ((0, 1), (0, -1))
EARLY = 3
BOTH = ("tile", "head")
OWNER_STEPS = tuple((which, turn) for which in range(3) for turn in range(2))


def nt(one, two):
    return lax.dot_general(one, two, (((1,), (1,)), ((), ())), preferred_element_type=WIDE)


def nn(one, two):
    return jnp.dot(one, two, preferred_element_type=WIDE)


def whole(count):
    return [pl.BlockSpec(memory_space=pltpu.VMEM)] * count


def owner_rows(core):
    rows = []
    for slot in range(SLOTS):
        row, pair = slot // 4, slot % 4
        heads = []
        for which, turn in OWNER_STEPS:
            if which == 2:
                unit = 10 * ((pair + 2) % 4) + 4
            elif (row + turn + core) % 2:
                unit = 10 * ((pair - 3 * which) % 4) + 8 - 2 * which
            else:
                unit = 10 * ((pair - which) % 4) + 2 * which
            heads.append(unit // 8)
        rows.append(heads + [(row + core) % 2])
    return rows


def place_table():
    rows = []
    for strip in range(STRIPS):
        for slot in range(SLOTS):
            run = run_at(slot)
            for core in range(2):
                columns = [(5 * run + at) % 8 for at in range(5)]
                swap = (run + core) % 2
                rows.append(owner_rows(core)[slot] + [strip, run % 2] + columns + [swap])
    every = jnp.asarray(np.array(rows, np.int32))
    at = lax.axis_index("tile") * 2 + lax.axis_index("head") % 2
    return lax.dynamic_index_in_dim(every, at, 0, keepdims=False)


def spread_kernel(table, upstream, *outs):
    line = lax.broadcasted_iota(jnp.int32, (2 * TILE, 2 * TILE), 0)
    col = lax.broadcasted_iota(jnp.int32, (2 * TILE, 2 * TILE), 1)
    source = ((line & 127) >> 2) * 8 + (line >> 7) * 4 + (line & 3)
    order = (col == source).astype(LOW)
    for at, (which, turn) in enumerate(OWNER_STEPS):
        head = pl.multiple_of(table[at] * HEAD_DIM, HEAD_DIM)
        tiles = jnp.dot(order, upstream[:, pl.ds(head, HEAD_DIM)], preferred_element_type=WIDE)
        tiles = tiles.astype(LOW)
        if which == 2:
            second = ((table[6] + turn) % 2) == 1
            outs[at][...] = jnp.where(second, tiles[TILE:], tiles[:TILE])
        else:
            outs[at][...] = tiles.reshape(2, TILE, HEAD_DIM)


def spread(table, upstream):
    shapes = [
        jax.ShapeDtypeStruct((TILE, HEAD_DIM) if which == 2 else (2, TILE, HEAD_DIM), LOW)
        for which, _ in OWNER_STEPS
    ]
    return pl.pallas_call(
        spread_kernel,
        out_shape=shapes,
        in_specs=[pl.BlockSpec(memory_space=pltpu.SMEM)] + whole(1),
        out_specs=whole(6),
        compiler_params=pltpu.CompilerParams(vmem_limit_bytes=16 << 20),
        name="spread",
    )(table, upstream)


def gather_kernel(table, *refs):
    free, late, singles = refs[:2], refs[2:4], refs[4:6]
    outs = refs[6:10]
    line = lax.broadcasted_iota(jnp.int32, (2 * TILE, 2 * TILE), 0)
    col = lax.broadcasted_iota(jnp.int32, (2 * TILE, 2 * TILE), 1)
    source = ((line >> 2) & 1) * TILE + (line >> 3) * 4 + (line & 3)
    order = (col == source).astype(LOW)
    flip = table[6] == 1

    def place(at, tiles):
        head = pl.multiple_of(table[at] * HEAD_DIM, HEAD_DIM)
        ordered = nn(order, jnp.concatenate(tiles, axis=1)).astype(LOW)
        for kind, out in enumerate(outs):
            out[:, pl.ds(head, HEAD_DIM)] = ordered[:, kind * HEAD_DIM : (kind + 1) * HEAD_DIM]

    for at in range(4):
        received = (late, free)[at // 2][at % 2]
        place(at, [received[kind].reshape(2 * TILE, HEAD_DIM) for kind in range(4)])
    one, two = singles[0][...], singles[1][...]
    tops, lows = jnp.where(flip, two, one), jnp.where(flip, one, two)
    place(4, [jnp.concatenate([tops[kind], lows[kind]], axis=0) for kind in range(4)])


def gather(table, received):
    return pl.pallas_call(
        gather_kernel,
        out_shape=[jax.ShapeDtypeStruct((2 * TILE, HEADS_HERE * HEAD_DIM), LOW)] * 4,
        in_specs=[pl.BlockSpec(memory_space=pltpu.SMEM)] + whole(6),
        out_specs=whole(4),
        compiler_params=pltpu.CompilerParams(vmem_limit_bytes=16 << 20),
        name="gather",
    )(table, *received)


def deal_kernel(swapped, out):
    for slot in range(SLOTS):
        for at in range(7):
            unit = min(max(5 * run_at(slot) + at - 1, 0), 39)
            head, column = unit // 8, unit % 8
            for kind in range(3):
                if kind == 0 and not 1 <= at <= 5:
                    continue
                place = at - 1 if kind == 0 else 7 * kind - 2 + at
                lines = swapped[column, kind, head].reshape(STRIPS, 8, HEAD_DIM)
                for strip in range(STRIPS):
                    out[strip * SLOTS + slot, place] = lines[strip]


def deal(swapped):
    return pl.pallas_call(
        deal_kernel,
        out_shape=jax.ShapeDtypeStruct((STRIPS * SLOTS, 19, 8, HEAD_DIM), LOW),
        in_specs=whole(1),
        out_specs=whole(1)[0],
        compiler_params=pltpu.CompilerParams(vmem_limit_bytes=16 << 20),
        name="deal",
    )(swapped)


def pair_shapes(kinds, count):
    return [jax.ShapeDtypeStruct((kinds, 2, TILE, HEAD_DIM), LOW)] * count


def attend_kernel(table, own, above, below, *refs):
    grads, rest, terms, edges = refs[:6], refs[6], refs[7], refs[8:10]
    pair, turned, outer_turned, grad, total, held = refs[10:]
    strip, odd, swap = table[7], table[8], table[14]
    scaling = HEAD_DIM**-0.5
    rate = scaling * math.log2(math.e)

    for kind in range(2):
        for at in range(7):
            for row in range(2):
                pair[kind, at, row] = own[row, 5 + 7 * kind + at]
            pair[kind, at, 2] = above[7 * kind + at]
            pair[kind, at, 3] = below[7 * kind + at]
    for kind in range(2):
        for at in range(7):
            for row in range(2):
                lanes = pl.ds((2 * at + row) * TILE, TILE)
                turned[kind, :, lanes] = pair[kind, at, row].T
                outer_turned[kind, row, :, pl.ds(at * TILE, TILE)] = pair[kind, at, 2 + row].T
    for at, (which, turn) in enumerate(OWNER_STEPS):
        row = (turn + swap) % 2
        first = first_of(which, odd)
        if which == 2:
            grad[row, first] = grads[at][...]
        else:
            for part in range(2):
                grad[row, first + part] = grads[at][part]
    total[...] = jnp.zeros_like(total)

    def one_unit(unit, carry):
        column = table[9 + unit]
        queries = [own[row, unit] for row in range(2)]
        both = jnp.concatenate(queries, axis=0)
        ups = [grad[row, unit] for row in range(2)]
        up_both = jnp.concatenate(ups, axis=0)
        column_ok = (column > 0, None, column < 7)
        row_ok = (strip > 0, strip < STRIPS - 1)

        def products(kind, left, left_both):
            inner, outer = [], []
            for step in range(3):
                slot = unit + step
                near = pair[kind, slot, 0:2].reshape(2 * TILE, HEAD_DIM)
                inner.append(nt(near, left_both))
                outer.append(
                    jnp.concatenate(
                        [nt(pair[kind, slot, 2 + row], left[row]) for row in range(2)], axis=1
                    )
                )
            return inner, outer

        inner, outer = products(0, queries, both)
        lane = lax.broadcasted_iota(jnp.int32, (1, 2 * TILE), 1)
        row_bias = jnp.where(
            lane < TILE,
            jnp.where(row_ok[0], 0.0, NEVER),
            jnp.where(row_ok[1], 0.0, NEVER),
        )
        for step in range(3):
            if column_ok[step] is None:
                outer[step] = outer[step] + row_bias
            else:
                bias = jnp.where(column_ok[step], 0.0, NEVER)
                inner[step] = inner[step] + bias
                outer[step] = outer[step] + (row_bias + bias)
        highest = functools.reduce(
            jnp.maximum, [jnp.max(block, axis=0, keepdims=True) for block in inner + outer]
        )
        raised = [jnp.exp2((block - highest) * rate) for block in inner + outer]
        amount = sum(jnp.sum(block, axis=0, keepdims=True) for block in raised)
        inverse = 1.0 / amount
        weights = [block * inverse for block in raised]
        low = [block.astype(LOW) for block in weights]

        def mix(kind, parts):
            near = sum(
                nn(
                    turned[kind, :, pl.ds(pl.multiple_of((unit + step) * 256, 256), 256)],
                    parts[step],
                )
                for step in range(3)
            )
            far = [
                sum(
                    nn(
                        outer_turned[
                            kind, row, :, pl.ds(pl.multiple_of((unit + step) * TILE, TILE), TILE)
                        ],
                        parts[3 + step][:, row * TILE : (row + 1) * TILE],
                    )
                    for step in range(3)
                )
                for row in range(2)
            ]
            return near + jnp.concatenate(far, axis=1)

        def fold(kind, parts, right, right_both):
            for step in range(3):
                slot = unit + step
                near = nn(parts[step], right_both)
                for row in range(2):
                    total[kind, slot, row] += near[row * TILE : (row + 1) * TILE]
                    total[kind, slot, 2 + row] += nn(
                        parts[3 + step][:, row * TILE : (row + 1) * TILE], right[row]
                    )

        mixed = mix(1, low).T
        offsets = jnp.sum((up_both.astype(WIDE) * mixed).T, axis=0, keepdims=True)
        for row in range(2):
            held[0, row, unit] = mixed[row * TILE : (row + 1) * TILE].astype(LOW)
        fold(1, low, ups, up_both)
        inner, outer = products(1, ups, up_both)
        slopes = [
            (weight * (block - offsets)).astype(LOW)
            for weight, block in zip(weights, inner + outer)
        ]
        query_grad = mix(0, slopes).T * scaling
        for row in range(2):
            held[1, row, unit] = query_grad[row * TILE : (row + 1) * TILE].astype(LOW)
        fold(0, slopes, queries, both)
        return carry

    lax.fori_loop(0, 5, one_unit, 0, unroll=True)
    for kind in range(2):
        for turn in range(2):
            row = (turn + swap) % 2
            for part in range(2):
                rest[kind, turn, part] = held[kind, row, first_of(0, odd) + part]
                rest[kind, turn, 2 + part] = held[kind, row, first_of(1, odd) + part]
            rest[kind, turn, 4] = held[kind, row, first_of(2, odd)]
    for kind, factor in ((0, scaling), (1, 1.0)):
        for at in range(7):
            for row in range(2):
                terms[kind, row, at] = total[kind, at, row] * factor
                edges[row][kind, at] = (total[kind, at, 3 - row] * factor).astype(LOW)


def column_shapes():
    return [jax.ShapeDtypeStruct((2, 2, TILE, HEAD_DIM), LOW)] * 2


def attend(table, own, halos, grads):
    return pl.pallas_call(
        attend_kernel,
        out_shape=[
            jax.ShapeDtypeStruct((2, 2, 5, TILE, HEAD_DIM), LOW),
            jax.ShapeDtypeStruct((2, 2, 7, TILE, HEAD_DIM), WIDE),
            jax.ShapeDtypeStruct((2, 7, TILE, HEAD_DIM), LOW),
            jax.ShapeDtypeStruct((2, 7, TILE, HEAD_DIM), LOW),
        ],
        in_specs=[pl.BlockSpec(memory_space=pltpu.SMEM)] + whole(9),
        out_specs=whole(4),
        scratch_shapes=[
            pltpu.VMEM((2, 7, 4, TILE, HEAD_DIM), LOW),
            pltpu.VMEM((2, HEAD_DIM, 14 * TILE), LOW),
            pltpu.VMEM((2, 2, HEAD_DIM, 7 * TILE), LOW),
            pltpu.VMEM((2, 5, TILE, HEAD_DIM), LOW),
            pltpu.VMEM((2, 7, 4, TILE, HEAD_DIM), WIDE),
            pltpu.VMEM((2, 2, 5, TILE, HEAD_DIM), LOW),
        ],
        compiler_params=pltpu.CompilerParams(vmem_limit_bytes=40 << 20),
        cost_estimate=pl.CostEstimate(
            flops=3_000_000_000, bytes_accessed=8_000_000, transcendentals=1_500_000
        ),
        name="attend",
    )(table, own, *halos, *grads)


def rims_kernel(table, rest, terms, above, below, right, left, *outs):
    odd, swap = table[8], table[14]
    edges = (above, below)
    for kind in range(2):
        for row, edge in enumerate(edges):
            for out, at in ((right, 6), (left, 0)):
                out[kind, row] = (terms[kind, row, at] + edge[kind, at].astype(WIDE)).astype(LOW)
    for turn in range(2):
        for part in range(2):
            at = first_of(1, odd) + part + 1
            for kind in range(2):
                outs[turn][kind, part] = rest[kind, turn, 2 + part]
                flip = (turn + swap) % 2 == 1
                edge = jnp.where(flip, below[kind, at], above[kind, at])
                value = terms[kind, (turn + swap) % 2, at] + edge.astype(WIDE)
                outs[turn][2 + kind, part] = value.astype(LOW)


def rims(table, rest, terms, edges):
    return pl.pallas_call(
        rims_kernel,
        out_shape=column_shapes() + pair_shapes(4, 2),
        in_specs=[pl.BlockSpec(memory_space=pltpu.SMEM)] + whole(4),
        out_specs=whole(4),
        compiler_params=pltpu.CompilerParams(vmem_limit_bytes=16 << 20),
        name="rims",
    )(table, rest, terms, *edges)


def combine_kernel(table, rest, terms, above, below, before, after, *outs):
    odd, swap = table[8], table[14]
    flipped = odd == 1
    for turn in range(2):
        row = (turn + swap) % 2
        for kind in range(2):

            def summed(at):
                edge = jnp.where(row == 1, below[kind, at + 1], above[kind, at + 1])
                return terms[kind, row, at + 1] + edge.astype(WIDE)

            first = first_of(0, odd)
            left = before[kind, row].astype(WIDE)
            right = after[kind, row].astype(WIDE)
            one, two = summed(first), summed(first + 1)
            for part in range(2):
                outs[turn][kind, part] = rest[kind, turn, part]
            outs[turn][2 + kind, 0] = jnp.where(flipped, one, one + left).astype(LOW)
            outs[turn][2 + kind, 1] = jnp.where(flipped, two + right, two).astype(LOW)
            alone = summed(first_of(2, odd)) + jnp.where(flipped, left, right)
            outs[2 + turn][kind] = rest[kind, turn, 4]
            outs[2 + turn][2 + kind] = alone.astype(LOW)


def combine(table, rest, terms, edges, columns):
    return pl.pallas_call(
        combine_kernel,
        out_shape=pair_shapes(4, 2) + [jax.ShapeDtypeStruct((4, TILE, HEAD_DIM), LOW)] * 2,
        in_specs=[pl.BlockSpec(memory_space=pltpu.SMEM)] + whole(6),
        out_specs=whole(4),
        compiler_params=pltpu.CompilerParams(vmem_limit_bytes=16 << 20),
        name="combine",
    )(table, rest, terms, *edges, *columns)


def send_all(parts, routes, axis="tile"):
    return [lax.ppermute(part, axis, path) for part, path in zip(parts, routes)]


def local(query_slab, key_slab, value_slab, upstream):
    place = place_table()
    to_owner = [on_cores(which, turn) for which, turn in OWNER_STEPS]
    row_routes = [shifted(*step) for step in ROW_STEPS]
    column_routes = [shifted(*step) for step in COLUMN_STEPS]

    with jax.named_scope("upstream_to_units"):
        grads = send_all(spread(place, upstream), [flipped(path) for path in to_owner], BOTH)

    with jax.named_scope("heads"):
        lines = [
            slab.reshape(8, 4, 40, 128).transpose(2, 0, 1, 3).reshape(8, 5, 32, 128)
            for slab in (query_slab, key_slab, value_slab)
        ]
        swapped = lax.all_to_all(jnp.stack(lines, axis=1), "head", 0, 0, tiled=True)
    with jax.named_scope("tiles"):
        dealt, early = lax.optimization_barrier((deal(swapped), grads[:EARLY]))
        got = lax.all_to_all(dealt, "tile", 0, 0, tiled=True)
        own = got.reshape(32, 19, 2, 4, 128).transpose(2, 1, 0, 3, 4)
        own = own.reshape(2, 19, TILE, HEAD_DIM)
        own, late = lax.optimization_barrier((own, grads[EARLY:]))
    with jax.named_scope("halos"):
        halos = send_all([own[1, 5:], own[0, 5:]], row_routes)
    with jax.named_scope("attention"):
        rest, terms, above, below = attend(place, own, halos, early + late)
    with jax.named_scope("row_terms"):
        edges = send_all([above, below], row_routes)
    with jax.named_scope("column_terms"):
        right, left, *free = rims(place, rest, terms, edges)
        columns = send_all([right, left], column_routes)
        free = send_all(free, to_owner[2:4], BOTH)
    with jax.named_scope("outputs_home"):
        leaving = combine(place, rest, terms, edges, columns)
        leaving, free = lax.optimization_barrier((leaving, free))
        late = send_all(leaving, to_owner[:2] + to_owner[4:], BOTH)
    with jax.named_scope("settle"):
        return tuple(gather(place, free + late))


def solution(mesh):
    slab = P("tile", None, "head", None)
    block = P("tile", "head")
    return jax.shard_map(
        local,
        mesh=mesh,
        in_specs=(slab, slab, slab, block),
        out_specs=(block, block, block, block),
        check_vma=False,
    )
```

```python
import functools
import math

import jax
import jax.numpy as jnp
import numpy as np
from jax import lax
from jax.experimental import pallas as pl
from jax.experimental.pallas import tpu as pltpu
from jax.sharding import PartitionSpec as P

HEAD_DIM = 128
HEADS_HERE = 5
STRIPS = 4
SLOTS = 8
TILE = 128
LOW = jnp.bfloat16
WIDE = jnp.float32
NEVER = -1e30


def route(step):
    pairs = []
    for strip in range(STRIPS):
        for slot in range(SLOTS):
            goal = step(strip, slot)
            if goal is not None:
                pairs.append((strip * SLOTS + slot, goal[0] * SLOTS + goal[1]))
    return pairs


def run_at(slot):
    return (5 - slot) % SLOTS


def shifted(rows, columns):
    def step(strip, slot):
        there = (strip + rows, run_at(slot) + columns)
        if 0 <= there[0] < STRIPS and 0 <= there[1] < SLOTS:
            return there[0], run_at(there[1])
        return None

    return route(step)


def first_of(which, odd):
    return (3 * odd, 2 - odd, 4 - 4 * odd)[which]


def owner_of(which, turn):
    def step(strip, slot):
        run = run_at(slot)
        odd = run % 2
        unit = 5 * run + first_of(which, odd)
        return (strip, ((turn + odd) % 2) * 4 + (unit % 8) // 2)

    return route(step)


def flipped(pairs):
    return [(target, source) for source, target in pairs]


ROW_STEPS = ((1, 0), (-1, 0))
COLUMN_STEPS = ((0, 1), (0, -1))
EARLY = 3
OWNER_STEPS = tuple((which, turn) for which in range(3) for turn in range(2))


def nt(one, two):
    return lax.dot_general(one, two, (((1,), (1,)), ((), ())), preferred_element_type=WIDE)


def nn(one, two):
    return jnp.dot(one, two, preferred_element_type=WIDE)


def whole(count):
    return [pl.BlockSpec(memory_space=pltpu.VMEM)] * count


def owner_rows():
    rows = []
    for slot in range(SLOTS):
        row, pair = slot // 4, slot % 4
        heads = []
        for which, turn in OWNER_STEPS:
            if which == 2:
                unit = 10 * ((pair + 2) % 4) + 4
            elif (row + turn) % 2:
                unit = 10 * ((pair - 3 * which) % 4) + 8 - 2 * which
            else:
                unit = 10 * ((pair - which) % 4) + 2 * which
            heads.append(unit // 8)
        rows.append(heads + [row])
    return rows


def place_table():
    owners = owner_rows()
    rows = [
        owners[slot]
        + [strip, run_at(slot) % 2]
        + [(5 * run_at(slot) + at) % 8 for at in range(5)]
        for strip in range(STRIPS)
        for slot in range(SLOTS)
    ]
    every = jnp.asarray(np.array(rows, np.int32))
    return lax.dynamic_index_in_dim(every, lax.axis_index("tile"), 0, keepdims=False)


def spread_kernel(table, upstream, *outs):
    line = lax.broadcasted_iota(jnp.int32, (2 * TILE, 2 * TILE), 0)
    col = lax.broadcasted_iota(jnp.int32, (2 * TILE, 2 * TILE), 1)
    source = ((line & 127) >> 2) * 8 + (line >> 7) * 4 + (line & 3)
    order = (col == source).astype(LOW)
    for at, (which, turn) in enumerate(OWNER_STEPS):
        head = pl.multiple_of(table[at] * HEAD_DIM, HEAD_DIM)
        tiles = jnp.dot(order, upstream[:, pl.ds(head, HEAD_DIM)], preferred_element_type=WIDE)
        tiles = tiles.astype(LOW)
        if which == 2:
            second = ((table[6] + turn) % 2) == 1
            outs[at][...] = jnp.where(second, tiles[TILE:], tiles[:TILE])
        else:
            outs[at][...] = tiles.reshape(2, TILE, HEAD_DIM)


def spread(table, upstream):
    shapes = [
        jax.ShapeDtypeStruct((TILE, HEAD_DIM) if which == 2 else (2, TILE, HEAD_DIM), LOW)
        for which, _ in OWNER_STEPS
    ]
    return pl.pallas_call(
        spread_kernel,
        out_shape=shapes,
        in_specs=[pl.BlockSpec(memory_space=pltpu.SMEM)] + whole(1),
        out_specs=whole(6),
        compiler_params=pltpu.CompilerParams(vmem_limit_bytes=16 << 20),
        name="spread",
    )(table, upstream)


def gather_kernel(table, *refs):
    free, late, singles = refs[:2], refs[2:4], refs[4:6]
    outs = refs[6:10]
    line = lax.broadcasted_iota(jnp.int32, (2 * TILE, 2 * TILE), 0)
    col = lax.broadcasted_iota(jnp.int32, (2 * TILE, 2 * TILE), 1)
    source = ((line >> 2) & 1) * TILE + (line >> 3) * 4 + (line & 3)
    order = (col == source).astype(LOW)
    flip = table[6] == 1

    def place(at, tiles):
        head = pl.multiple_of(table[at] * HEAD_DIM, HEAD_DIM)
        ordered = nn(order, jnp.concatenate(tiles, axis=1)).astype(LOW)
        for kind, out in enumerate(outs):
            out[:, pl.ds(head, HEAD_DIM)] = ordered[:, kind * HEAD_DIM : (kind + 1) * HEAD_DIM]

    for at in range(4):
        received = (late, free)[at // 2][at % 2]
        place(at, [received[kind].reshape(2 * TILE, HEAD_DIM) for kind in range(4)])
    one, two = singles[0][...], singles[1][...]
    tops, lows = jnp.where(flip, two, one), jnp.where(flip, one, two)
    place(4, [jnp.concatenate([tops[kind], lows[kind]], axis=0) for kind in range(4)])


def gather(table, received):
    return pl.pallas_call(
        gather_kernel,
        out_shape=[jax.ShapeDtypeStruct((2 * TILE, HEADS_HERE * HEAD_DIM), LOW)] * 4,
        in_specs=[pl.BlockSpec(memory_space=pltpu.SMEM)] + whole(6),
        out_specs=whole(4),
        compiler_params=pltpu.CompilerParams(vmem_limit_bytes=16 << 20),
        name="gather",
    )(table, *received)


def deal_kernel(swapped, out):
    for slot in range(SLOTS):
        for at in range(7):
            unit = min(max(5 * run_at(slot) + at - 1, 0), 39)
            head, column = unit // 8, unit % 8
            for kind in range(3):
                if kind == 0 and not 1 <= at <= 5:
                    continue
                place = at - 1 if kind == 0 else 7 * kind - 2 + at
                lines = swapped[column, kind, head].reshape(STRIPS, 8, HEAD_DIM)
                for strip in range(STRIPS):
                    out[strip * SLOTS + slot, place] = lines[strip]


def deal(swapped):
    return pl.pallas_call(
        deal_kernel,
        out_shape=jax.ShapeDtypeStruct((STRIPS * SLOTS, 19, 8, HEAD_DIM), LOW),
        in_specs=whole(1),
        out_specs=whole(1)[0],
        compiler_params=pltpu.CompilerParams(vmem_limit_bytes=16 << 20),
        name="deal",
    )(swapped)


def pair_shapes(kinds, count):
    return [jax.ShapeDtypeStruct((kinds, 2, TILE, HEAD_DIM), LOW)] * count


def attend_kernel(table, own, above, below, *refs):
    grads, rest, terms, edges = refs[:6], refs[6], refs[7], refs[8:10]
    pair, turned, outer_turned, grad, total, held = refs[10:]
    strip, odd = table[7], table[8]
    scaling = HEAD_DIM**-0.5
    rate = scaling * math.log2(math.e)

    for kind in range(2):
        for at in range(7):
            for row in range(2):
                pair[kind, at, row] = own[row, 5 + 7 * kind + at]
            pair[kind, at, 2] = above[7 * kind + at]
            pair[kind, at, 3] = below[7 * kind + at]
    for kind in range(2):
        for at in range(7):
            for row in range(2):
                lanes = pl.ds((2 * at + row) * TILE, TILE)
                turned[kind, :, lanes] = pair[kind, at, row].T
                outer_turned[kind, row, :, pl.ds(at * TILE, TILE)] = pair[kind, at, 2 + row].T
    for at, (which, turn) in enumerate(OWNER_STEPS):
        row = (turn + odd) % 2
        first = first_of(which, odd)
        if which == 2:
            grad[row, first] = grads[at][...]
        else:
            for part in range(2):
                grad[row, first + part] = grads[at][part]
    total[...] = jnp.zeros_like(total)

    def one_unit(unit, carry):
        column = table[9 + unit]
        queries = [own[row, unit] for row in range(2)]
        both = jnp.concatenate(queries, axis=0)
        ups = [grad[row, unit] for row in range(2)]
        up_both = jnp.concatenate(ups, axis=0)
        column_ok = (column > 0, None, column < 7)
        row_ok = (strip > 0, strip < STRIPS - 1)

        def products(kind, left, left_both):
            inner, outer = [], []
            for step in range(3):
                slot = unit + step
                near = pair[kind, slot, 0:2].reshape(2 * TILE, HEAD_DIM)
                inner.append(nt(near, left_both))
                outer.append(
                    jnp.concatenate(
                        [nt(pair[kind, slot, 2 + row], left[row]) for row in range(2)], axis=1
                    )
                )
            return inner, outer

        inner, outer = products(0, queries, both)
        lane = lax.broadcasted_iota(jnp.int32, (1, 2 * TILE), 1)
        row_bias = jnp.where(
            lane < TILE,
            jnp.where(row_ok[0], 0.0, NEVER),
            jnp.where(row_ok[1], 0.0, NEVER),
        )
        for step in range(3):
            if column_ok[step] is None:
                outer[step] = outer[step] + row_bias
            else:
                bias = jnp.where(column_ok[step], 0.0, NEVER)
                inner[step] = inner[step] + bias
                outer[step] = outer[step] + (row_bias + bias)
        highest = functools.reduce(
            jnp.maximum, [jnp.max(block, axis=0, keepdims=True) for block in inner + outer]
        )
        raised = [jnp.exp2((block - highest) * rate) for block in inner + outer]
        amount = sum(jnp.sum(block, axis=0, keepdims=True) for block in raised)
        inverse = 1.0 / amount
        weights = [block * inverse for block in raised]
        low = [block.astype(LOW) for block in weights]

        def mix(kind, parts):
            near = sum(
                nn(
                    turned[kind, :, pl.ds(pl.multiple_of((unit + step) * 256, 256), 256)],
                    parts[step],
                )
                for step in range(3)
            )
            far = [
                sum(
                    nn(
                        outer_turned[
                            kind, row, :, pl.ds(pl.multiple_of((unit + step) * TILE, TILE), TILE)
                        ],
                        parts[3 + step][:, row * TILE : (row + 1) * TILE],
                    )
                    for step in range(3)
                )
                for row in range(2)
            ]
            return near + jnp.concatenate(far, axis=1)

        def fold(kind, parts, right, right_both):
            for step in range(3):
                slot = unit + step
                near = nn(parts[step], right_both)
                for row in range(2):
                    total[kind, slot, row] += near[row * TILE : (row + 1) * TILE]
                    total[kind, slot, 2 + row] += nn(
                        parts[3 + step][:, row * TILE : (row + 1) * TILE], right[row]
                    )

        mixed = mix(1, low).T
        offsets = jnp.sum((up_both.astype(WIDE) * mixed).T, axis=0, keepdims=True)
        for row in range(2):
            held[0, row, unit] = mixed[row * TILE : (row + 1) * TILE].astype(LOW)
        fold(1, low, ups, up_both)
        inner, outer = products(1, ups, up_both)
        slopes = [
            (weight * (block - offsets)).astype(LOW)
            for weight, block in zip(weights, inner + outer)
        ]
        query_grad = mix(0, slopes).T * scaling
        for row in range(2):
            held[1, row, unit] = query_grad[row * TILE : (row + 1) * TILE].astype(LOW)
        fold(0, slopes, queries, both)
        return carry

    lax.fori_loop(0, 5, one_unit, 0, unroll=True)
    for kind in range(2):
        for turn in range(2):
            row = (turn + odd) % 2
            for part in range(2):
                rest[kind, turn, part] = held[kind, row, first_of(0, odd) + part]
                rest[kind, turn, 2 + part] = held[kind, row, first_of(1, odd) + part]
            rest[kind, turn, 4] = held[kind, row, first_of(2, odd)]
    for kind, factor in ((0, scaling), (1, 1.0)):
        for at in range(7):
            for row in range(2):
                terms[kind, row, at] = total[kind, at, row] * factor
                edges[row][kind, at] = (total[kind, at, 3 - row] * factor).astype(LOW)


def column_shapes():
    return [jax.ShapeDtypeStruct((2, 2, TILE, HEAD_DIM), LOW)] * 2


def attend(table, own, halos, grads):
    return pl.pallas_call(
        attend_kernel,
        out_shape=[
            jax.ShapeDtypeStruct((2, 2, 5, TILE, HEAD_DIM), LOW),
            jax.ShapeDtypeStruct((2, 2, 7, TILE, HEAD_DIM), WIDE),
            jax.ShapeDtypeStruct((2, 7, TILE, HEAD_DIM), LOW),
            jax.ShapeDtypeStruct((2, 7, TILE, HEAD_DIM), LOW),
        ],
        in_specs=[pl.BlockSpec(memory_space=pltpu.SMEM)] + whole(9),
        out_specs=whole(4),
        scratch_shapes=[
            pltpu.VMEM((2, 7, 4, TILE, HEAD_DIM), LOW),
            pltpu.VMEM((2, HEAD_DIM, 14 * TILE), LOW),
            pltpu.VMEM((2, 2, HEAD_DIM, 7 * TILE), LOW),
            pltpu.VMEM((2, 5, TILE, HEAD_DIM), LOW),
            pltpu.VMEM((2, 7, 4, TILE, HEAD_DIM), WIDE),
            pltpu.VMEM((2, 2, 5, TILE, HEAD_DIM), LOW),
        ],
        compiler_params=pltpu.CompilerParams(vmem_limit_bytes=40 << 20),
        cost_estimate=pl.CostEstimate(
            flops=3_000_000_000, bytes_accessed=8_000_000, transcendentals=1_500_000
        ),
        name="attend",
    )(table, own, *halos, *grads)


def rims_kernel(table, rest, terms, above, below, right, left, *outs):
    odd = table[8]
    edges = (above, below)
    for kind in range(2):
        for row, edge in enumerate(edges):
            for out, at in ((right, 6), (left, 0)):
                out[kind, row] = (terms[kind, row, at] + edge[kind, at].astype(WIDE)).astype(LOW)
    for turn in range(2):
        for part in range(2):
            at = first_of(1, odd) + part + 1
            for kind in range(2):
                outs[turn][kind, part] = rest[kind, turn, 2 + part]
                flip = (turn + odd) % 2 == 1
                edge = jnp.where(flip, below[kind, at], above[kind, at])
                value = terms[kind, (turn + odd) % 2, at] + edge.astype(WIDE)
                outs[turn][2 + kind, part] = value.astype(LOW)


def rims(table, rest, terms, edges):
    return pl.pallas_call(
        rims_kernel,
        out_shape=column_shapes() + pair_shapes(4, 2),
        in_specs=[pl.BlockSpec(memory_space=pltpu.SMEM)] + whole(4),
        out_specs=whole(4),
        compiler_params=pltpu.CompilerParams(vmem_limit_bytes=16 << 20),
        name="rims",
    )(table, rest, terms, *edges)


def combine_kernel(table, rest, terms, above, below, before, after, *outs):
    odd = table[8]
    flipped = odd == 1
    for turn in range(2):
        row = (turn + odd) % 2
        for kind in range(2):

            def summed(at):
                edge = jnp.where(row == 1, below[kind, at + 1], above[kind, at + 1])
                return terms[kind, row, at + 1] + edge.astype(WIDE)

            first = first_of(0, odd)
            left = before[kind, row].astype(WIDE)
            right = after[kind, row].astype(WIDE)
            one, two = summed(first), summed(first + 1)
            for part in range(2):
                outs[turn][kind, part] = rest[kind, turn, part]
            outs[turn][2 + kind, 0] = jnp.where(flipped, one, one + left).astype(LOW)
            outs[turn][2 + kind, 1] = jnp.where(flipped, two + right, two).astype(LOW)
            alone = summed(first_of(2, odd)) + jnp.where(flipped, left, right)
            outs[2 + turn][kind] = rest[kind, turn, 4]
            outs[2 + turn][2 + kind] = alone.astype(LOW)


def combine(table, rest, terms, edges, columns):
    return pl.pallas_call(
        combine_kernel,
        out_shape=pair_shapes(4, 2) + [jax.ShapeDtypeStruct((4, TILE, HEAD_DIM), LOW)] * 2,
        in_specs=[pl.BlockSpec(memory_space=pltpu.SMEM)] + whole(6),
        out_specs=whole(4),
        compiler_params=pltpu.CompilerParams(vmem_limit_bytes=16 << 20),
        name="combine",
    )(table, rest, terms, *edges, *columns)


def send_all(parts, routes):
    return [lax.ppermute(part, "tile", path) for part, path in zip(parts, routes)]


def local(query_slab, key_slab, value_slab, upstream):
    place = place_table()
    to_owner = [owner_of(which, turn) for which, turn in OWNER_STEPS]
    row_routes = [shifted(*step) for step in ROW_STEPS]
    column_routes = [shifted(*step) for step in COLUMN_STEPS]

    with jax.named_scope("upstream_to_units"):
        grads = send_all(spread(place, upstream), [flipped(path) for path in to_owner])

    with jax.named_scope("heads"):
        lines = [
            slab.reshape(8, 4, 40, 128).transpose(2, 0, 1, 3).reshape(8, 5, 32, 128)
            for slab in (query_slab, key_slab, value_slab)
        ]
        swapped = lax.all_to_all(jnp.stack(lines, axis=1), "head", 0, 0, tiled=True)
    with jax.named_scope("tiles"):
        dealt, early = lax.optimization_barrier((deal(swapped), grads[:EARLY]))
        got = lax.all_to_all(dealt, "tile", 0, 0, tiled=True)
        own = got.reshape(32, 19, 2, 4, 128).transpose(2, 1, 0, 3, 4)
        own = own.reshape(2, 19, TILE, HEAD_DIM)
        own, late = lax.optimization_barrier((own, grads[EARLY:]))
    with jax.named_scope("halos"):
        halos = send_all([own[1, 5:], own[0, 5:]], row_routes)
    with jax.named_scope("attention"):
        rest, terms, above, below = attend(place, own, halos, early + late)
    with jax.named_scope("row_terms"):
        edges = send_all([above, below], row_routes)
    with jax.named_scope("column_terms"):
        right, left, *free = rims(place, rest, terms, edges)
        columns = send_all([right, left], column_routes)
        free = send_all(free, to_owner[2:4])
    with jax.named_scope("outputs_home"):
        leaving = combine(place, rest, terms, edges, columns)
        leaving, free = lax.optimization_barrier((leaving, free))
        late = send_all(leaving, to_owner[:2] + to_owner[4:])
    with jax.named_scope("settle"):
        return tuple(gather(place, free + late))


def solution(mesh):
    slab = P("tile", None, "head", None)
    block = P("tile", "head")
    return jax.shard_map(
        local,
        mesh=mesh,
        in_specs=(slab, slab, slab, block),
        out_specs=(block, block, block, block),
        check_vma=False,
    )
```

```python
import functools
import math

import jax
import jax.numpy as jnp
import numpy as np
from jax import lax
from jax.experimental import pallas as pl
from jax.experimental.pallas import tpu as pltpu
from jax.sharding import PartitionSpec as P

HEAD_DIM = 128
HEADS_HERE = 5
STRIPS = 4
SLOTS = 8
TILE = 128
LOW = jnp.bfloat16
WIDE = jnp.float32
NEVER = -1e30


def route(step):
    pairs = []
    for strip in range(STRIPS):
        for slot in range(SLOTS):
            goal = step(strip, slot)
            if goal is not None:
                pairs.append((strip * SLOTS + slot, goal[0] * SLOTS + goal[1]))
    return pairs


def run_at(slot):
    return (5 - slot) % SLOTS


def shifted(rows, columns):
    def step(strip, slot):
        there = (strip + rows, run_at(slot) + columns)
        if 0 <= there[0] < STRIPS and 0 <= there[1] < SLOTS:
            return there[0], run_at(there[1])
        return None

    return route(step)


def first_of(which, odd):
    return (3 * odd, 2 - odd, 4 - 4 * odd)[which]


def owner_of(which, turn):
    def step(strip, slot):
        run = run_at(slot)
        odd = run % 2
        unit = 5 * run + first_of(which, odd)
        return (strip, ((turn + odd) % 2) * 4 + (unit % 8) // 2)

    return route(step)


def flipped(pairs):
    return [(target, source) for source, target in pairs]


ROW_STEPS = ((1, 0), (-1, 0))
COLUMN_STEPS = ((0, 1), (0, -1))
EARLY = 2
OWNER_STEPS = tuple((which, turn) for which in range(3) for turn in range(2))


def nt(one, two):
    return lax.dot_general(one, two, (((1,), (1,)), ((), ())), preferred_element_type=WIDE)


def nn(one, two):
    return jnp.dot(one, two, preferred_element_type=WIDE)


def whole(count):
    return [pl.BlockSpec(memory_space=pltpu.VMEM)] * count


def owner_rows():
    rows = []
    for slot in range(SLOTS):
        row, pair = slot // 4, slot % 4
        heads = []
        for which, turn in OWNER_STEPS:
            if which == 2:
                unit = 10 * ((pair + 2) % 4) + 4
            elif (row + turn) % 2:
                unit = 10 * ((pair - 3 * which) % 4) + 8 - 2 * which
            else:
                unit = 10 * ((pair - which) % 4) + 2 * which
            heads.append(unit // 8)
        rows.append(heads + [row])
    return rows


def place_table():
    owners = owner_rows()
    rows = [
        owners[slot]
        + [strip, run_at(slot) % 2]
        + [(5 * run_at(slot) + at) % 8 for at in range(5)]
        for strip in range(STRIPS)
        for slot in range(SLOTS)
    ]
    every = jnp.asarray(np.array(rows, np.int32))
    return lax.dynamic_index_in_dim(every, lax.axis_index("tile"), 0, keepdims=False)


def spread_kernel(table, upstream, *outs):
    line = lax.broadcasted_iota(jnp.int32, (2 * TILE, 2 * TILE), 0)
    col = lax.broadcasted_iota(jnp.int32, (2 * TILE, 2 * TILE), 1)
    source = ((line & 127) >> 2) * 8 + (line >> 7) * 4 + (line & 3)
    order = (col == source).astype(LOW)
    for at, (which, turn) in enumerate(OWNER_STEPS):
        head = pl.multiple_of(table[at] * HEAD_DIM, HEAD_DIM)
        tiles = jnp.dot(order, upstream[:, pl.ds(head, HEAD_DIM)], preferred_element_type=WIDE)
        tiles = tiles.astype(LOW)
        if which == 2:
            second = ((table[6] + turn) % 2) == 1
            outs[at][...] = jnp.where(second, tiles[TILE:], tiles[:TILE])
        else:
            outs[at][...] = tiles.reshape(2, TILE, HEAD_DIM)


def spread(table, upstream):
    shapes = [
        jax.ShapeDtypeStruct((TILE, HEAD_DIM) if which == 2 else (2, TILE, HEAD_DIM), LOW)
        for which, _ in OWNER_STEPS
    ]
    return pl.pallas_call(
        spread_kernel,
        out_shape=shapes,
        in_specs=[pl.BlockSpec(memory_space=pltpu.SMEM)] + whole(1),
        out_specs=whole(6),
        compiler_params=pltpu.CompilerParams(vmem_limit_bytes=16 << 20),
        name="spread",
    )(table, upstream)


def gather_kernel(table, *refs):
    free, late, singles = refs[:2], refs[2:4], refs[4:6]
    outs = refs[6:10]
    line = lax.broadcasted_iota(jnp.int32, (2 * TILE, 2 * TILE), 0)
    col = lax.broadcasted_iota(jnp.int32, (2 * TILE, 2 * TILE), 1)
    source = ((line >> 2) & 1) * TILE + (line >> 3) * 4 + (line & 3)
    order = (col == source).astype(LOW)
    flip = table[6] == 1

    def place(at, tiles):
        head = pl.multiple_of(table[at] * HEAD_DIM, HEAD_DIM)
        ordered = nn(order, jnp.concatenate(tiles, axis=1)).astype(LOW)
        for kind, out in enumerate(outs):
            out[:, pl.ds(head, HEAD_DIM)] = ordered[:, kind * HEAD_DIM : (kind + 1) * HEAD_DIM]

    for at in range(4):
        received = (late, free)[at // 2][at % 2]
        place(at, [received[kind].reshape(2 * TILE, HEAD_DIM) for kind in range(4)])
    one, two = singles[0][...], singles[1][...]
    tops, lows = jnp.where(flip, two, one), jnp.where(flip, one, two)
    place(4, [jnp.concatenate([tops[kind], lows[kind]], axis=0) for kind in range(4)])


def gather(table, received):
    return pl.pallas_call(
        gather_kernel,
        out_shape=[jax.ShapeDtypeStruct((2 * TILE, HEADS_HERE * HEAD_DIM), LOW)] * 4,
        in_specs=[pl.BlockSpec(memory_space=pltpu.SMEM)] + whole(6),
        out_specs=whole(4),
        compiler_params=pltpu.CompilerParams(vmem_limit_bytes=16 << 20),
        name="gather",
    )(table, *received)


def deal_kernel(swapped, out):
    for slot in range(SLOTS):
        for at in range(7):
            unit = min(max(5 * run_at(slot) + at - 1, 0), 39)
            head, column = unit // 8, unit % 8
            for kind in range(3):
                if kind == 0 and not 1 <= at <= 5:
                    continue
                place = at - 1 if kind == 0 else 7 * kind - 2 + at
                lines = swapped[column, kind, head].reshape(STRIPS, 8, HEAD_DIM)
                for strip in range(STRIPS):
                    out[strip * SLOTS + slot, place] = lines[strip]


def deal(swapped):
    return pl.pallas_call(
        deal_kernel,
        out_shape=jax.ShapeDtypeStruct((STRIPS * SLOTS, 19, 8, HEAD_DIM), LOW),
        in_specs=whole(1),
        out_specs=whole(1)[0],
        compiler_params=pltpu.CompilerParams(vmem_limit_bytes=16 << 20),
        name="deal",
    )(swapped)


def pair_shapes(kinds, count):
    return [jax.ShapeDtypeStruct((kinds, 2, TILE, HEAD_DIM), LOW)] * count


def attend_kernel(table, own, above, below, *refs):
    grads, rest, terms, edges = refs[:6], refs[6], refs[7], refs[8:10]
    pair, turned, outer_turned, grad, total, held = refs[10:]
    strip, odd = table[7], table[8]
    scaling = HEAD_DIM**-0.5
    rate = scaling * math.log2(math.e)

    for kind in range(2):
        for at in range(7):
            for row in range(2):
                pair[kind, at, row] = own[row, 5 + 7 * kind + at]
            pair[kind, at, 2] = above[7 * kind + at]
            pair[kind, at, 3] = below[7 * kind + at]
    for kind in range(2):
        for at in range(7):
            for row in range(2):
                lanes = pl.ds((2 * at + row) * TILE, TILE)
                turned[kind, :, lanes] = pair[kind, at, row].T
                outer_turned[kind, row, :, pl.ds(at * TILE, TILE)] = pair[kind, at, 2 + row].T
    for at, (which, turn) in enumerate(OWNER_STEPS):
        row = (turn + odd) % 2
        first = first_of(which, odd)
        if which == 2:
            grad[row, first] = grads[at][...]
        else:
            for part in range(2):
                grad[row, first + part] = grads[at][part]
    total[...] = jnp.zeros_like(total)

    def one_unit(unit, carry):
        column = table[9 + unit]
        queries = [own[row, unit] for row in range(2)]
        both = jnp.concatenate(queries, axis=0)
        ups = [grad[row, unit] for row in range(2)]
        up_both = jnp.concatenate(ups, axis=0)
        column_ok = (column > 0, None, column < 7)
        row_ok = (strip > 0, strip < STRIPS - 1)

        def products(kind, left, left_both):
            inner, outer = [], []
            for step in range(3):
                slot = unit + step
                near = pair[kind, slot, 0:2].reshape(2 * TILE, HEAD_DIM)
                inner.append(nt(near, left_both))
                outer.append(
                    jnp.concatenate(
                        [nt(pair[kind, slot, 2 + row], left[row]) for row in range(2)], axis=1
                    )
                )
            return inner, outer

        inner, outer = products(0, queries, both)
        lane = lax.broadcasted_iota(jnp.int32, (1, 2 * TILE), 1)
        row_bias = jnp.where(
            lane < TILE,
            jnp.where(row_ok[0], 0.0, NEVER),
            jnp.where(row_ok[1], 0.0, NEVER),
        )
        for step in range(3):
            if column_ok[step] is None:
                outer[step] = outer[step] + row_bias
            else:
                bias = jnp.where(column_ok[step], 0.0, NEVER)
                inner[step] = inner[step] + bias
                outer[step] = outer[step] + (row_bias + bias)
        highest = functools.reduce(
            jnp.maximum, [jnp.max(block, axis=0, keepdims=True) for block in inner + outer]
        )
        raised = [jnp.exp2((block - highest) * rate) for block in inner + outer]
        amount = sum(jnp.sum(block, axis=0, keepdims=True) for block in raised)
        inverse = 1.0 / amount
        weights = [block * inverse for block in raised]
        low = [block.astype(LOW) for block in weights]

        def mix(kind, parts):
            near = sum(
                nn(
                    turned[kind, :, pl.ds(pl.multiple_of((unit + step) * 256, 256), 256)],
                    parts[step],
                )
                for step in range(3)
            )
            far = [
                sum(
                    nn(
                        outer_turned[
                            kind, row, :, pl.ds(pl.multiple_of((unit + step) * TILE, TILE), TILE)
                        ],
                        parts[3 + step][:, row * TILE : (row + 1) * TILE],
                    )
                    for step in range(3)
                )
                for row in range(2)
            ]
            return near + jnp.concatenate(far, axis=1)

        def fold(kind, parts, right, right_both):
            for step in range(3):
                slot = unit + step
                near = nn(parts[step], right_both)
                for row in range(2):
                    total[kind, slot, row] += near[row * TILE : (row + 1) * TILE]
                    total[kind, slot, 2 + row] += nn(
                        parts[3 + step][:, row * TILE : (row + 1) * TILE], right[row]
                    )

        mixed = mix(1, low).T
        offsets = jnp.sum((up_both.astype(WIDE) * mixed).T, axis=0, keepdims=True)
        for row in range(2):
            held[0, row, unit] = mixed[row * TILE : (row + 1) * TILE].astype(LOW)
        fold(1, low, ups, up_both)
        inner, outer = products(1, ups, up_both)
        slopes = [
            (weight * (block - offsets)).astype(LOW)
            for weight, block in zip(weights, inner + outer)
        ]
        query_grad = mix(0, slopes).T * scaling
        for row in range(2):
            held[1, row, unit] = query_grad[row * TILE : (row + 1) * TILE].astype(LOW)
        fold(0, slopes, queries, both)
        return carry

    lax.fori_loop(0, 5, one_unit, 0, unroll=True)
    for kind in range(2):
        for turn in range(2):
            row = (turn + odd) % 2
            for part in range(2):
                rest[kind, turn, part] = held[kind, row, first_of(0, odd) + part]
                rest[kind, turn, 2 + part] = held[kind, row, first_of(1, odd) + part]
            rest[kind, turn, 4] = held[kind, row, first_of(2, odd)]
    for kind, factor in ((0, scaling), (1, 1.0)):
        for at in range(7):
            for row in range(2):
                terms[kind, row, at] = total[kind, at, row] * factor
                edges[row][kind, at] = (total[kind, at, 3 - row] * factor).astype(LOW)


def column_shapes():
    return [jax.ShapeDtypeStruct((2, 2, TILE, HEAD_DIM), LOW)] * 2


def attend(table, own, halos, grads):
    return pl.pallas_call(
        attend_kernel,
        out_shape=[
            jax.ShapeDtypeStruct((2, 2, 5, TILE, HEAD_DIM), LOW),
            jax.ShapeDtypeStruct((2, 2, 7, TILE, HEAD_DIM), WIDE),
            jax.ShapeDtypeStruct((2, 7, TILE, HEAD_DIM), LOW),
            jax.ShapeDtypeStruct((2, 7, TILE, HEAD_DIM), LOW),
        ],
        in_specs=[pl.BlockSpec(memory_space=pltpu.SMEM)] + whole(9),
        out_specs=whole(4),
        scratch_shapes=[
            pltpu.VMEM((2, 7, 4, TILE, HEAD_DIM), LOW),
            pltpu.VMEM((2, HEAD_DIM, 14 * TILE), LOW),
            pltpu.VMEM((2, 2, HEAD_DIM, 7 * TILE), LOW),
            pltpu.VMEM((2, 5, TILE, HEAD_DIM), LOW),
            pltpu.VMEM((2, 7, 4, TILE, HEAD_DIM), WIDE),
            pltpu.VMEM((2, 2, 5, TILE, HEAD_DIM), LOW),
        ],
        compiler_params=pltpu.CompilerParams(vmem_limit_bytes=40 << 20),
        cost_estimate=pl.CostEstimate(
            flops=3_000_000_000, bytes_accessed=8_000_000, transcendentals=1_500_000
        ),
        name="attend",
    )(table, own, *halos, *grads)


def rims_kernel(table, rest, terms, above, below, right, left, *outs):
    odd = table[8]
    edges = (above, below)
    for kind in range(2):
        for row, edge in enumerate(edges):
            for out, at in ((right, 6), (left, 0)):
                out[kind, row] = (terms[kind, row, at] + edge[kind, at].astype(WIDE)).astype(LOW)
    for turn in range(2):
        for part in range(2):
            at = first_of(1, odd) + part + 1
            for kind in range(2):
                outs[turn][kind, part] = rest[kind, turn, 2 + part]
                flip = (turn + odd) % 2 == 1
                edge = jnp.where(flip, below[kind, at], above[kind, at])
                value = terms[kind, (turn + odd) % 2, at] + edge.astype(WIDE)
                outs[turn][2 + kind, part] = value.astype(LOW)


def rims(table, rest, terms, edges):
    return pl.pallas_call(
        rims_kernel,
        out_shape=column_shapes() + pair_shapes(4, 2),
        in_specs=[pl.BlockSpec(memory_space=pltpu.SMEM)] + whole(4),
        out_specs=whole(4),
        compiler_params=pltpu.CompilerParams(vmem_limit_bytes=16 << 20),
        name="rims",
    )(table, rest, terms, *edges)


def combine_kernel(table, rest, terms, above, below, before, after, *outs):
    odd = table[8]
    flipped = odd == 1
    for turn in range(2):
        row = (turn + odd) % 2
        for kind in range(2):

            def summed(at):
                edge = jnp.where(row == 1, below[kind, at + 1], above[kind, at + 1])
                return terms[kind, row, at + 1] + edge.astype(WIDE)

            first = first_of(0, odd)
            left = before[kind, row].astype(WIDE)
            right = after[kind, row].astype(WIDE)
            one, two = summed(first), summed(first + 1)
            for part in range(2):
                outs[turn][kind, part] = rest[kind, turn, part]
            outs[turn][2 + kind, 0] = jnp.where(flipped, one, one + left).astype(LOW)
            outs[turn][2 + kind, 1] = jnp.where(flipped, two + right, two).astype(LOW)
            alone = summed(first_of(2, odd)) + jnp.where(flipped, left, right)
            outs[2 + turn][kind] = rest[kind, turn, 4]
            outs[2 + turn][2 + kind] = alone.astype(LOW)


def combine(table, rest, terms, edges, columns):
    return pl.pallas_call(
        combine_kernel,
        out_shape=pair_shapes(4, 2) + [jax.ShapeDtypeStruct((4, TILE, HEAD_DIM), LOW)] * 2,
        in_specs=[pl.BlockSpec(memory_space=pltpu.SMEM)] + whole(6),
        out_specs=whole(4),
        compiler_params=pltpu.CompilerParams(vmem_limit_bytes=16 << 20),
        name="combine",
    )(table, rest, terms, *edges, *columns)


def send_all(parts, routes):
    return [lax.ppermute(part, "tile", path) for part, path in zip(parts, routes)]


def local(query_slab, key_slab, value_slab, upstream):
    place = place_table()
    to_owner = [owner_of(which, turn) for which, turn in OWNER_STEPS]
    row_routes = [shifted(*step) for step in ROW_STEPS]
    column_routes = [shifted(*step) for step in COLUMN_STEPS]

    with jax.named_scope("upstream_to_units"):
        grads = send_all(spread(place, upstream), [flipped(path) for path in to_owner])

    with jax.named_scope("heads"):
        lines = [
            slab.reshape(8, 4, 40, 128).transpose(2, 0, 1, 3).reshape(8, 5, 32, 128)
            for slab in (query_slab, key_slab, value_slab)
        ]
        swapped = lax.all_to_all(jnp.stack(lines, axis=1), "head", 0, 0, tiled=True)
    with jax.named_scope("tiles"):
        dealt, early = lax.optimization_barrier((deal(swapped), grads[:EARLY]))
        got = lax.all_to_all(dealt, "tile", 0, 0, tiled=True)
        own = got.reshape(32, 19, 2, 4, 128).transpose(2, 1, 0, 3, 4)
        own = own.reshape(2, 19, TILE, HEAD_DIM)
        own, late = lax.optimization_barrier((own, grads[EARLY:]))
    with jax.named_scope("halos"):
        halos = send_all([own[1, 5:], own[0, 5:]], row_routes)
    with jax.named_scope("attention"):
        rest, terms, above, below = attend(place, own, halos, early + late)
    with jax.named_scope("row_terms"):
        edges = send_all([above, below], row_routes)
    with jax.named_scope("column_terms"):
        right, left, *free = rims(place, rest, terms, edges)
        columns = send_all([right, left], column_routes)
        free = send_all(free, to_owner[2:4])
    with jax.named_scope("outputs_home"):
        leaving = combine(place, rest, terms, edges, columns)
        leaving, free = lax.optimization_barrier((leaving, free))
        late = send_all(leaving, to_owner[:2] + to_owner[4:])
    with jax.named_scope("settle"):
        return tuple(gather(place, free + late))


def solution(mesh):
    slab = P("tile", None, "head", None)
    block = P("tile", "head")
    return jax.shard_map(
        local,
        mesh=mesh,
        in_specs=(slab, slab, slab, block),
        out_specs=(block, block, block, block),
        check_vma=False,
    )
```
